32 devices in a mesh: seq: 8 (over z, x), tp: 4 (over y, core).
Axes of the slice: x: 2, y: 2, z: 4, core: 2. Of those that a mesh axis runs over, the one named last changes fastest.
Arguments:
- values: bfloat16 [2048, 4096], P('seq', 'tp'), may hold values from -6 to 6
- gate: bfloat16 [2048, 4096], P('seq', 'tp'), may hold values from -6 to 6
- residues: float32 [16, 4096], P(None, 'tp'), may hold values from -1.5 to 1.5
- rates: float32 [16, 4096], P(None, 'tp'), may hold values from 0 to 1, as said below
- skip: float32 [4096], P('tp'), may hold values from -4 to 4
- out_weight: bfloat16 [4096, 4096], P('tp'), may hold values from -0.09375 to 0.09375
Outputs:
- output: bfloat16 [2048, 4096], P('seq', 'tp')
The draws below stay inside these ranges and needn't reach their ends.
Inputs may be any that keep to these rules, and one draw needn't show every extreme that they name: rates are positive and at most 1; the smallest are near 0.25 / 2048.
All inputs are finite; a program needn't handle non-finite values.
Results may differ from the reference program's by a relative error of at most 0.013.
Values may be sent and summed in bfloat16 or wider, within the bound.
No kernel may reach another device: no remote copies, remote signals or barrier semaphores. Data moves between devices by JAX's collectives and lax.ppermute only.
A program may use at most 128 MiB of HBM per device.

```python
import math
import jax
import jax.numpy as jnp
from jax import lax

D = 4096
MODES = 16
TOKENS = 2048
N_TP = 4


def draw_rates(key, part):
    key = jax.random.fold_in(key, 7)
    first = jax.random.fold_in(key, 0)
    lowest = math.log(0.25 / TOKENS)
    highest = 0.0
    spread = jax.random.uniform(first, (MODES, D), jnp.float32)
    return jnp.exp(lowest + spread * (highest - lowest))


def levels(rng, dims, cuts, smallest, top_value):
    gain, own = 1.0, jax.random.fold_in(rng, 6)
    for axis_at, parts in cuts:
        steps = jnp.exp(jax.random.uniform(jax.random.fold_in(own, axis_at), (parts,), jnp.float32, smallest / len(cuts), top_value / len(cuts)))
        gain = gain * jnp.repeat(steps, dims[axis_at] // parts).reshape([-1 if axis == axis_at else 1 for axis in range(len(dims))])
    return gain


def noise(own_key, shape, deviation, bound, pieces=(), kind=jnp.bfloat16):
    entries = jax.random.normal(own_key, shape, jnp.float32) * deviation
    if len(pieces) > 0:
        entries = levels(own_key, shape, pieces, -0.22, 0.18) * entries
    return jnp.clip(entries, min=-bound, max=bound).astype(kind)


def setup_inputs(seed: int = 0) -> dict:
    seeds = jax.random.split(jax.random.key(seed), 7)
    return {
        "values": noise(seeds[0], (TOKENS, D), 1.0, 6.0, ((0, 8), (1, 4))),
        "gate": noise(seeds[1], (TOKENS, D), 1.0, 6.0, ((0, 8), (1, 4))),
        "residues": noise(seeds[2], (MODES, D), 0.25, 1.5, ((1, 4),), jnp.float32),
        "rates": draw_rates(jax.random.fold_in(seeds[6], 71), 0),
        "skip": noise(seeds[4], (D,), 1.0, 4.0, ((0, 4),), jnp.float32),
        "out_weight": noise(seeds[5], (D, D), D ** -0.5, 0.09375, ((0, 4),)),
    }


def modal_filter(residues, rates, positions):
    result = jnp.zeros((positions.shape[0], residues.shape[1]), jnp.float32)
    for mode in range(residues.shape[0]):
        result = result + residues[mode] * jnp.sqrt(2.0 * rates[mode]) * jnp.exp(-rates[mode] * positions)
    return result

def reference(values, gate, residues, rates, skip, out_weight):
    width = D // N_TP
    positions = jnp.arange(TOKENS).astype(jnp.float32)[:, None]

    def group_step(carry, group):
        start = (group * width).astype(jnp.int32)
        value_block = lax.dynamic_slice_in_dim(values, start, width, 1).astype(jnp.float32)
        gate_block = lax.dynamic_slice_in_dim(gate, start, width, 1).astype(jnp.float32)
        filt = modal_filter(lax.dynamic_slice_in_dim(residues, start, width, 1), lax.dynamic_slice_in_dim(rates, start, width, 1), positions)
        spectrum = jnp.fft.rfft(value_block, n=2 * TOKENS, axis=0) * jnp.fft.rfft(filt, n=2 * TOKENS, axis=0)
        conv = jnp.fft.irfft(spectrum, n=2 * TOKENS, axis=0)[:TOKENS]
        mixed = conv + lax.dynamic_slice_in_dim(skip, start, width, 0) * value_block
        gated = (gate_block * mixed).astype(jnp.bfloat16)
        weight_rows = lax.dynamic_slice_in_dim(out_weight, start, width, 0)
        partial_sum = jnp.dot(gated, weight_rows, preferred_element_type=jnp.float32).astype(jnp.bfloat16)
        return (carry + partial_sum.astype(jnp.float32), None)
    total, _ = lax.scan(group_step, jnp.zeros((TOKENS, D), jnp.float32), jnp.arange(N_TP, dtype=jnp.int32))
    return total.astype(jnp.bfloat16)
```

```python
from functools import partial

import jax
import jax.numpy as jnp
from jax import lax
from jax.experimental import pallas as pl
from jax.experimental.pallas import tpu as pltpu
from jax.sharding import PartitionSpec as P

SUB, LANE = 8, 128
F32, BF16 = jnp.float32, jnp.bfloat16

VMEM = pl.BlockSpec(memory_space=pltpu.VMEM)
ANY = pl.BlockSpec(memory_space=pl.ANY)
HBM = "hbm"
PARAMS = pltpu.CompilerParams(vmem_limit_bytes=24 * 2**20)


def in_hbm(array):
    return pltpu.with_memory_space_constraint(array, pltpu.HBM)


def in_vmem(array):
    return pltpu.with_memory_space_constraint(array, pltpu.VMEM)


def row_of(block, mode):
    return jnp.broadcast_to(block[mode : mode + 1, :], (SUB, LANE))


def sublane():
    return lax.broadcasted_iota(jnp.int32, (SUB, LANE), 0)


def lanes_at(step):
    return pl.ds(pl.multiple_of(step * LANE, LANE), LANE)


def gains_of(residues, rates):
    return residues * jnp.sqrt(2.0 * rates)


def spread_table(tok, back):
    run = tok // SUB
    row = lax.broadcasted_iota(jnp.int32, (tok, tok), 1 if back else 0)
    col = lax.broadcasted_iota(jnp.int32, (tok, tok), 0 if back else 1)
    return (col == row % SUB * run + row // SUB).astype(F32).astype(BF16)


ROW_CUTS = 4


def column_copies(other, begin, slots, weight_hbm, out_ref, sems):
    rank = lax.axis_index("tp")
    chips = lax.axis_size("tp") // 2
    block = weight_hbm.shape[1] // (2 * chips)
    wide = out_ref.shape[1] // len(slots)
    tall = out_ref.shape[0] // ROW_CUTS
    core = 1 - rank % 2 if other else rank % 2
    copies = []
    for at, slot in enumerate(slots):
        owner = (rank // 2 + slot) % chips * 2 + core
        columns = pl.ds(pl.multiple_of(owner * block + begin, LANE), wide)
        for cut in range(ROW_CUTS):
            rows = pl.ds(cut * tall, tall)
            copies.append(
                pltpu.make_async_copy(
                    weight_hbm.at[rows, columns],
                    out_ref.at[rows, pl.ds(at * wide, wide)],
                    sems.at[at * ROW_CUTS + cut],
                )
            )
            copies[-1].start()
    return copies


def wait_all(copies):
    for copy in copies:
        copy.wait()


def state_kernel(
    values_hbm, rates_hbm, wire_hbm, values_ref, rates_ref, state_ref, sems, out_sems
):
    tok, chan = values_ref.shape
    modes = rates_ref.shape[0]
    shards = wire_hbm.shape[0]
    parts = sems.shape[0] - 1
    width = chan // parts
    first = pltpu.make_async_copy(rates_hbm, rates_ref, sems.at[parts])
    first.start()
    pieces, outs = [], []
    for part in range(parts):
        lanes = pl.ds(part * width, width)
        pieces.append(
            pltpu.make_async_copy(
                values_hbm.at[:, lanes], values_ref.at[:, lanes], sems.at[part]
            )
        )
        pieces[-1].start()
    left = (SUB - 1 - sublane()).astype(F32)
    first.wait()
    for index in range(chan // LANE):
        if index * LANE % width == 0:
            pieces[index * LANE // width].wait()
        lanes = slice(index * LANE, (index + 1) * LANE)
        rates = rates_ref[:, lanes]
        decay = jnp.exp(-float(SUB) * rates)
        decays = [row_of(decay, mode) for mode in range(modes)]
        held = [jnp.zeros((SUB, LANE), F32)] * modes
        for at in range(0, tok, 2 * SUB):
            pair = values_ref[at : at + 2 * SUB, lanes].astype(F32)
            for half in (pair[:SUB], pair[SUB:]):
                held = [decays[mode] * held[mode] + half for mode in range(modes)]
        rows = [
            jnp.sum(held[mode] * jnp.exp(-row_of(rates, mode) * left), axis=0, keepdims=True)
            for mode in range(modes)
        ]
        state_ref[:, lanes] = jnp.concatenate(rows, axis=0).astype(BF16)
        if (index + 1) * LANE % width == 0:
            part = index * LANE // width
            lanes = pl.ds(part * width, width)
            for shard in range(shards):
                outs.append(
                    pltpu.make_async_copy(
                        state_ref.at[:, lanes], wire_hbm.at[shard, :, lanes],
                        out_sems.at[part, shard],
                    )
                )
                outs[-1].start()
    wait_all(outs)


def local_kernel(
    values_hbm, rates_hbm, residues_hbm, skip_hbm, gate_hbm, weight_hbm,
    near_ref, starts_ref, ahead_ref, rates_ref, spread_ref, first_weight,
    values_ref, residues_ref, skip_ref, gate_ref, wide_ref, taps_ref, sems, weight_sems,
):
    tok, chan = values_ref.shape
    modes = rates_ref.shape[0]
    run = tok // SUB
    copies = [
        pltpu.make_async_copy(source, target, sems.at[at])
        for at, (source, target) in enumerate(
            (
                (values_hbm, values_ref),
                (gate_hbm, gate_ref),
                (rates_hbm, rates_ref),
                (residues_hbm, residues_ref),
                (skip_hbm, skip_ref),
            )
        )
    ]
    for copy in copies:
        copy.start()
    slots = range(lax.axis_size("tp") // 2)
    rest = column_copies(1, 0, slots, weight_hbm, first_weight, weight_sems)
    table = spread_table(tok, False)
    wait_all(copies)
    wide_ref[...] = jnp.dot(table, values_ref[...], preferred_element_type=F32)
    spread_ref[...] = jnp.dot(table, gate_ref[...], preferred_element_type=F32).astype(BF16)

    def step(index, carry):
        lanes = lanes_at(index)
        place = sublane()
        rates = rates_ref[:, lanes]
        gains = gains_of(residues_ref[:, lanes], rates)

        ahead = place.astype(F32)
        decay = jnp.exp(-float(SUB) * rates)
        terms = [
            row_of(gains, mode) * jnp.exp(-row_of(rates, mode) * ahead) for mode in range(modes)
        ]
        for at in range(0, run, SUB):
            total = terms[0]
            for mode in range(1, modes):
                total = total + terms[mode]
            if at == 0:
                total = jnp.where(place == 0, total + skip_ref[:, lanes], total)
            terms = [terms[mode] * row_of(decay, mode) for mode in range(modes)]
            taps_ref[at : at + SUB, :] = total

        for at in range(0, run, SUB):
            sums = [jnp.zeros((SUB, LANE), F32)] * SUB
            for early in range(0, at + SUB, SUB):
                for lag in range(at - early - SUB + 1, at - early + SUB):
                    if lag < 0:
                        continue
                    tap = jnp.broadcast_to(taps_ref[lag : lag + 1, :], (SUB, LANE))
                    for source in range(SUB):
                        target = early + source + lag - at
                        if 0 <= target < SUB:
                            rows = pl.ds((early + source) * SUB, SUB)
                            sums[target] = sums[target] + tap * wide_ref[rows, lanes]
            for target in range(SUB):
                near_ref[pl.ds((at + target) * SUB, SUB), lanes] = sums[target]

        decay = jnp.exp(-rates)
        decay_run = jnp.exp(-float(run) * rates)
        decays = [row_of(decay, mode) for mode in range(modes)]
        held = [jnp.zeros((SUB, LANE), F32)] * modes
        for at in range(run):
            value = wide_ref[at * SUB : (at + 1) * SUB, lanes]
            held = [decays[mode] * held[mode] + value for mode in range(modes)]
        for mode in range(modes):
            whole, power = held[mode], row_of(decay_run, mode)
            for shift in (1, 2, 4):
                moved = jnp.where(place >= shift, pltpu.roll(whole, shift, 0), 0.0)
                whole = whole + power * moved
                power = power * power
            before = jnp.where(place >= 1, pltpu.roll(whole, 1, 0), 0.0)
            first = row_of(gains, mode) * decays[mode]
            rows = slice(mode * SUB, (mode + 1) * SUB)
            starts_ref[rows, lanes] = first * before
        ahead_ref[:, lanes] = gains * decay
        return carry

    lax.fori_loop(0, chan // LANE, step, 0)
    wait_all(rest)


def gate_kernel(
    states_ref, near_ref, starts_ref, ahead_ref, rates_ref, spread_ref, weight_ref, weight_hbm,
    gated_ref, sent_ref, kept_weight, later_weight, held_ref, state_ref, decay_ref, sems,
):
    slots = range(lax.axis_size("tp") // 2)
    begin = weight_ref.shape[1] // len(slots)
    rest = column_copies(0, 0, slots, weight_hbm, kept_weight, sems.at[0])
    rest += column_copies(1, begin, slots, weight_hbm, later_weight, sems.at[1])
    tok, chan = spread_ref.shape
    shards, modes = states_ref.shape[:2]
    run = tok // SUB
    place = lax.axis_index("seq")
    rates = rates_ref[...]
    decay_ref[...] = jnp.exp(-rates)
    far = jnp.exp(-float(tok) * rates)
    before = jnp.zeros((modes, chan), F32)
    for shard in range(shards - 1):
        passed = far * before + states_ref[shard].astype(F32)
        before = jnp.where(shard < place, passed, before)
    state_ref[...] = before * ahead_ref[...]
    passed = (sublane() * run).astype(F32)

    def step(index, carry):
        lanes = lanes_at(index)
        decays, terms = [], []
        for mode in range(modes):
            rows, row = slice(mode * SUB, (mode + 1) * SUB), slice(mode, mode + 1)
            decays.append(jnp.broadcast_to(decay_ref[row, lanes], (SUB, LANE)))
            state = jnp.broadcast_to(state_ref[row, lanes], (SUB, LANE))
            rate = jnp.broadcast_to(rates_ref[row, lanes], (SUB, LANE))
            terms.append(starts_ref[rows, lanes] + state * jnp.exp(-rate * passed))
        for at in range(0, run, 2):
            totals = []
            for spot in (at, at + 1):
                total = near_ref[spot * SUB : (spot + 1) * SUB, lanes]
                for mode in range(modes):
                    total = total + terms[mode]
                terms = [terms[mode] * decays[mode] for mode in range(modes)]
                totals.append(total)
            rows = slice(at * SUB, (at + 2) * SUB)
            gate = spread_ref[rows, lanes].astype(F32)
            held_ref[rows, lanes] = (gate * jnp.concatenate(totals, axis=0)).astype(BF16)
        return carry

    lax.fori_loop(0, chan // LANE, step, 0)
    project(spread_table(tok, True), held_ref, gated_ref)
    project(gated_ref, weight_ref, sent_ref)
    wait_all(rest)


def project(left_ref, right_ref, out_ref):
    total = out_ref.shape[1]
    tile = 2 * LANE if total % (2 * LANE) == 0 else LANE
    for first in range(0, total, tile):
        lanes = slice(first, first + tile)
        out_ref[:, lanes] = jnp.dot(
            left_ref[...], right_ref[:, lanes], preferred_element_type=F32
        ).astype(out_ref.dtype)


def product(gated_ref, weight):
    return jnp.dot(gated_ref[...], weight, preferred_element_type=F32)


def middle_kernel(
    gated_ref, kept_weight, sent_weight, weight_hbm, kept_ref, sent_ref, later_ref, sems
):
    chips = lax.axis_size("tp") // 2
    begin = kept_ref.shape[1] // chips
    copies = column_copies(0, begin, range(1, chips), weight_hbm, later_ref, sems)
    project(gated_ref, kept_weight, kept_ref)
    project(gated_ref, sent_weight, sent_ref)
    wait_all(copies)


def join_kernel(kept_ref, moved_ref, *going_refs):
    wide = going_refs[0].shape[1]
    for hop, going_ref in enumerate(going_refs, 1):
        lanes = slice(hop * wide, (hop + 1) * wide)
        going_ref[...] = (kept_ref[:, lanes] + moved_ref[:, lanes].astype(F32)).astype(BF16)


def going_kernel(gated_ref, weight_ref, moved_ref, *going_refs):
    wide = going_refs[0].shape[1]
    for hop, going_ref in enumerate(going_refs, 1):
        lanes = slice((hop - 1) * wide, hop * wide)
        total = product(gated_ref, weight_ref[:, lanes])
        total = total + moved_ref[:, hop * wide : (hop + 1) * wide].astype(F32)
        going_ref[...] = total.astype(BF16)


def own_kernel(gated_ref, weight_hbm, moved_ref, kept_ref, moved_first_ref, *refs):
    others, (first_ref, own_ref, weight_ref, sems) = refs[:-4], refs[-4:]
    narrow, wide = first_ref.shape[1], own_ref.shape[1]
    copies = column_copies(0, narrow, range(1), weight_hbm, weight_ref, sems)
    total = kept_ref[:, :narrow] + moved_first_ref[:, :narrow].astype(F32)
    for other in others:
        total = total + other[...].astype(F32)
    first_ref[...] = total.astype(BF16)
    wait_all(copies)
    own_ref[...] = moved_ref[:, :wide].astype(F32) + product(gated_ref, weight_ref[...])


def final_kernel(first_ref, own_ref, *refs):
    others, (out_hbm, wide_ref, sems) = refs[:-3], refs[-3:]
    tok, narrow = first_ref.shape
    count = sems.shape[0] - 1
    copies = [
        pltpu.make_async_copy(first_ref, out_hbm.at[:, pl.ds(0, narrow)], sems.at[count])
    ]
    copies[0].start()
    for part in range(count):
        rows = pl.ds(part * tok // count, tok // count)
        total = own_ref[rows, :]
        for other in others:
            total = total + other[rows, :].astype(F32)
        wide_ref[rows, :] = total.astype(BF16)
        columns = pl.ds(narrow, wide_ref.shape[1])
        copies.append(
            pltpu.make_async_copy(wide_ref.at[rows], out_hbm.at[rows, columns], sems.at[part])
        )
        copies[-1].start()
    wait_all(copies)


def call(kernel, outs, *operands, scratch=(), macs=0, out_spec=VMEM):
    specs, arrays = [], []
    for operand in operands:
        spec, array = operand if isinstance(operand, tuple) else (VMEM, operand)
        specs.append(ANY if spec is HBM else spec)
        arrays.append(in_hbm(array) if spec is HBM else array)
    return pl.pallas_call(
        kernel,
        out_shape=outs,
        in_specs=specs,
        out_specs=[out_spec] * len(outs),
        scratch_shapes=scratch,
        compiler_params=PARAMS,
        cost_estimate=pl.CostEstimate(flops=2 * macs, bytes_accessed=0, transcendentals=0),
    )(*arrays)


def body(values, gate, residues, rates, skip, out_weight):
    shards, tp = lax.axis_size("seq"), lax.axis_size("tp")
    tok, chan = values.shape
    modes = rates.shape[0]
    chips = tp // 2
    block = out_weight.shape[1] // tp
    here = pltpu.VMEM
    parts = 4 if chan % (4 * LANE) == 0 else 1
    cores = [(rank, rank ^ 1) for rank in range(tp)]
    sources = [(HBM, each) for each in (values, rates, residues, skip.reshape(1, chan), gate)]
    (wire,) = call(
        state_kernel,
        [jax.ShapeDtypeStruct((shards, modes, chan), BF16)],
        *sources[:2],
        scratch=[
            here((tok, chan), BF16),
            here((modes, chan), F32),
            here((modes, chan), BF16),
            pltpu.SemaphoreType.DMA((parts + 1,)),
            pltpu.SemaphoreType.DMA((parts, shards)),
        ],
        out_spec=ANY,
    )
    states = lax.all_to_all(wire, "seq", split_axis=0, concat_axis=0, tiled=True)
    narrow = max(LANE, block // 4)
    wide = block - narrow
    weight = (HBM, out_weight)
    tables = call(
        local_kernel,
        [
            here((tok, chan), F32),
            here((modes * SUB, chan), F32),
            here((modes, chan), F32),
            here((modes, chan), F32),
            here((tok, chan), BF16),
            here((chan, chips * narrow), BF16),
        ],
        *sources, weight,
        scratch=[
            here((tok, chan), BF16),
            here((modes, chan), F32),
            here((1, chan), F32),
            here((tok, chan), BF16),
            here((tok, chan), F32),
            here((tok // SUB, LANE), F32),
            pltpu.SemaphoreType.DMA((len(sources),)),
            pltpu.SemaphoreType.DMA((chips * ROW_CUTS,)),
        ],
    )

    gated, sent, kept_weight, sent_weight = call(
        gate_kernel,
        [
            here((tok, chan), BF16),
            here((tok, chips * narrow), BF16),
            here((chan, chips * narrow), BF16),
            here((chan, chips * wide), BF16),
        ],
        states, *tables, weight,
        scratch=[
            here((tok, chan), BF16),
            here((modes, chan), F32),
            here((modes, chan), F32),
            pltpu.SemaphoreType.DMA((2, chips * ROW_CUTS)),
        ],
    )
    moved_first = lax.ppermute(sent, "tp", cores)
    kept, sent, later = call(
        middle_kernel,
        [
            here((tok, chips * narrow), F32),
            here((tok, chips * wide), BF16),
            here((chan, (chips - 1) * wide), BF16),
        ],
        gated, kept_weight, sent_weight, weight,
        scratch=[pltpu.SemaphoreType.DMA(((chips - 1) * ROW_CUTS,))],
    )
    moved = lax.ppermute(sent, "tp", cores)

    def to_chips(going):
        return [
            lax.ppermute(each, "tp", [(rank, (rank + 2 * hop) % tp) for rank in range(tp)])
            for hop, each in enumerate(going, 1)
        ]

    first = to_chips(
        call(
            join_kernel, [here((tok, narrow), BF16)] * (chips - 1), kept, moved_first,
            macs=16 * tok * chan * block,
        )
    )
    second = to_chips(
        call(going_kernel, [here((tok, wide), BF16)] * (chips - 1), gated, later, moved)
    )
    done, own = call(
        own_kernel, [here((tok, narrow), BF16), here((tok, wide), F32)],
        gated, weight, moved, kept, moved_first, *first,
        macs=16 * tok * chan * block,
        scratch=[here((chan, wide), BF16), pltpu.SemaphoreType.DMA((ROW_CUTS,))],
    )
    (out,) = call(
        final_kernel, [jax.ShapeDtypeStruct((tok, block), BF16)], done, own, *second,
        scratch=[here((tok, wide), BF16), pltpu.SemaphoreType.DMA((5,))],
        out_spec=ANY,
    )
    return out


def solution(mesh):
    placed = (P("seq", "tp"), P("seq", "tp"), P(None, "tp"), P(None, "tp"), P("tp"), P("tp", None))
    return jax.shard_map(
        body, mesh=mesh, in_specs=placed, out_specs=P("seq", "tp"), check_vma=False
    )
```

```python
from functools import partial

import jax
import jax.numpy as jnp
from jax import lax
from jax.experimental import pallas as pl
from jax.experimental.pallas import tpu as pltpu
from jax.sharding import PartitionSpec as P

SUB, LANE = 8, 128
F32, BF16 = jnp.float32, jnp.bfloat16

VMEM = pl.BlockSpec(memory_space=pltpu.VMEM)
ANY = pl.BlockSpec(memory_space=pl.ANY)
HBM = "hbm"
PARAMS = pltpu.CompilerParams(vmem_limit_bytes=24 * 2**20)


def in_hbm(array):
    return pltpu.with_memory_space_constraint(array, pltpu.HBM)


def in_vmem(array):
    return pltpu.with_memory_space_constraint(array, pltpu.VMEM)


def row_of(block, mode):
    return jnp.broadcast_to(block[mode : mode + 1, :], (SUB, LANE))


def sublane():
    return lax.broadcasted_iota(jnp.int32, (SUB, LANE), 0)


def lanes_at(step):
    return pl.ds(pl.multiple_of(step * LANE, LANE), LANE)


def gains_of(residues, rates):
    return residues * jnp.sqrt(2.0 * rates)


def spread_table(tok, back):
    run = tok // SUB
    row = lax.broadcasted_iota(jnp.int32, (tok, tok), 1 if back else 0)
    col = lax.broadcasted_iota(jnp.int32, (tok, tok), 0 if back else 1)
    return (col == row % SUB * run + row // SUB).astype(F32).astype(BF16)


ROW_CUTS = 4


def column_copies(other, begin, slots, weight_hbm, out_ref, sems):
    rank = lax.axis_index("tp")
    chips = lax.axis_size("tp") // 2
    block = weight_hbm.shape[1] // (2 * chips)
    wide = out_ref.shape[1] // len(slots)
    tall = out_ref.shape[0] // ROW_CUTS
    core = 1 - rank % 2 if other else rank % 2
    copies = []
    for at, slot in enumerate(slots):
        owner = (rank // 2 + slot) % chips * 2 + core
        columns = pl.ds(pl.multiple_of(owner * block + begin, LANE), wide)
        for cut in range(ROW_CUTS):
            rows = pl.ds(cut * tall, tall)
            copies.append(
                pltpu.make_async_copy(
                    weight_hbm.at[rows, columns],
                    out_ref.at[rows, pl.ds(at * wide, wide)],
                    sems.at[at * ROW_CUTS + cut],
                )
            )
            copies[-1].start()
    return copies


def group_order(count):
    return sorted(range(count), key=lambda rank: (abs(2 * rank + 1 - count), -rank))


def wait_all(copies):
    for copy in copies:
        copy.wait()


def state_kernel(values_hbm, rates_hbm, wire_ref, values_ref, rates_ref, sems):
    tok, chan = values_ref.shape
    modes = rates_ref.shape[0]
    parts = sems.shape[0] - 1
    width = chan // parts
    first = pltpu.make_async_copy(rates_hbm, rates_ref, sems.at[parts])
    first.start()
    pieces = []
    for part in range(parts):
        lanes = pl.ds(part * width, width)
        pieces.append(
            pltpu.make_async_copy(
                values_hbm.at[:, lanes], values_ref.at[:, lanes], sems.at[part]
            )
        )
        pieces[-1].start()
    left = (SUB - 1 - sublane()).astype(F32)
    first.wait()
    for index in range(chan // LANE):
        if index * LANE % width == 0:
            pieces[index * LANE // width].wait()
        lanes = slice(index * LANE, (index + 1) * LANE)
        rates = rates_ref[:, lanes]
        decay = jnp.exp(-float(SUB) * rates)
        decays = [row_of(decay, mode) for mode in range(modes)]
        held = [jnp.zeros((SUB, LANE), F32)] * modes
        for at in range(0, tok, 2 * SUB):
            pair = values_ref[at : at + 2 * SUB, lanes].astype(F32)
            for half in (pair[:SUB], pair[SUB:]):
                held = [decays[mode] * held[mode] + half for mode in range(modes)]
        rows = [
            jnp.sum(held[mode] * jnp.exp(-row_of(rates, mode) * left), axis=0, keepdims=True)
            for mode in range(modes)
        ]
        state = jnp.concatenate(rows, axis=0).astype(BF16)
        for shard in range(wire_ref.shape[0]):
            wire_ref[shard, :, lanes] = state


def local_kernel(
    values_hbm, rates_hbm, residues_hbm, skip_hbm, gate_hbm, weight_hbm,
    near_ref, starts_ref, ahead_ref, rates_ref, spread_ref, first_weight, kept_weight,
    values_ref, residues_ref, skip_ref, gate_ref, wide_ref, taps_ref, sems, weight_sems,
):
    tok, chan = values_ref.shape
    modes = rates_ref.shape[0]
    run = tok // SUB
    copies = [
        pltpu.make_async_copy(source, target, sems.at[at])
        for at, (source, target) in enumerate(
            (
                (values_hbm, values_ref),
                (gate_hbm, gate_ref),
                (rates_hbm, rates_ref),
                (residues_hbm, residues_ref),
                (skip_hbm, skip_ref),
            )
        )
    ]
    for copy in copies:
        copy.start()
    slots = range(1, lax.axis_size("tp") // 2)
    rest = column_copies(1, 0, slots, weight_hbm, first_weight, weight_sems.at[0])
    rest += column_copies(0, 0, slots, weight_hbm, kept_weight, weight_sems.at[1])
    table = spread_table(tok, False)
    wait_all(copies)
    wide_ref[...] = jnp.dot(table, values_ref[...], preferred_element_type=F32)
    spread_ref[...] = jnp.dot(table, gate_ref[...], preferred_element_type=F32).astype(BF16)

    def step(index, carry):
        lanes = lanes_at(index)
        place = sublane()
        rates = rates_ref[:, lanes]
        gains = gains_of(residues_ref[:, lanes], rates)

        ahead = place.astype(F32)
        decay = jnp.exp(-float(SUB) * rates)
        terms = [
            row_of(gains, mode) * jnp.exp(-row_of(rates, mode) * ahead) for mode in range(modes)
        ]
        for at in range(0, run, SUB):
            total = terms[0]
            for mode in range(1, modes):
                total = total + terms[mode]
            if at == 0:
                total = jnp.where(place == 0, total + skip_ref[:, lanes], total)
            terms = [terms[mode] * row_of(decay, mode) for mode in range(modes)]
            taps_ref[at : at + SUB, :] = total

        for at in range(0, run, SUB):
            sums = [jnp.zeros((SUB, LANE), F32)] * SUB
            for early in range(0, at + SUB, SUB):
                for lag in range(at - early - SUB + 1, at - early + SUB):
                    if lag < 0:
                        continue
                    tap = jnp.broadcast_to(taps_ref[lag : lag + 1, :], (SUB, LANE))
                    for source in range(SUB):
                        target = early + source + lag - at
                        if 0 <= target < SUB:
                            rows = pl.ds((early + source) * SUB, SUB)
                            sums[target] = sums[target] + tap * wide_ref[rows, lanes]
            for target in range(SUB):
                near_ref[pl.ds((at + target) * SUB, SUB), lanes] = sums[target]

        decay = jnp.exp(-rates)
        decay_run = jnp.exp(-float(run) * rates)
        decays = [row_of(decay, mode) for mode in range(modes)]
        held = [jnp.zeros((SUB, LANE), F32)] * modes
        for at in range(run):
            value = wide_ref[at * SUB : (at + 1) * SUB, lanes]
            held = [decays[mode] * held[mode] + value for mode in range(modes)]
        for mode in range(modes):
            whole, power = held[mode], row_of(decay_run, mode)
            for shift in (1, 2, 4):
                moved = jnp.where(place >= shift, pltpu.roll(whole, shift, 0), 0.0)
                whole = whole + power * moved
                power = power * power
            before = jnp.where(place >= 1, pltpu.roll(whole, 1, 0), 0.0)
            first = row_of(gains, mode) * decays[mode]
            rows = slice(mode * SUB, (mode + 1) * SUB)
            starts_ref[rows, lanes] = first * before
        ahead_ref[:, lanes] = gains * decay
        return carry

    lax.fori_loop(0, chan // LANE, step, 0)
    wait_all(rest)


def gate_kernel(
    states_ref, near_ref, starts_ref, ahead_ref, rates_ref, spread_ref, weight_ref, weight_hbm,
    gated_ref, sent_ref, later_weight, last_weight, held_ref, state_ref, decay_ref, sems,
):
    slots = range(1, lax.axis_size("tp") // 2)
    begin = weight_ref.shape[1] // len(slots)
    rest = column_copies(1, begin, slots, weight_hbm, later_weight, sems.at[0])
    rest += column_copies(0, begin, slots, weight_hbm, last_weight, sems.at[1])
    tok, chan = spread_ref.shape
    shards, modes = states_ref.shape[:2]
    run = tok // SUB
    place = lax.axis_index("seq")
    rates = rates_ref[...]
    decay_ref[...] = jnp.exp(-rates)
    far = jnp.exp(-float(tok) * rates)
    before = jnp.zeros((modes, chan), F32)
    order = group_order(shards)
    for shard in range(shards - 1):
        passed = far * before + states_ref[order.index(shard)].astype(F32)
        before = jnp.where(shard < place, passed, before)
    state_ref[...] = before * ahead_ref[...]
    passed = (sublane() * run).astype(F32)

    def step(index, carry):
        lanes = lanes_at(index)
        decays, terms = [], []
        for mode in range(modes):
            rows, row = slice(mode * SUB, (mode + 1) * SUB), slice(mode, mode + 1)
            decays.append(jnp.broadcast_to(decay_ref[row, lanes], (SUB, LANE)))
            state = jnp.broadcast_to(state_ref[row, lanes], (SUB, LANE))
            rate = jnp.broadcast_to(rates_ref[row, lanes], (SUB, LANE))
            terms.append(starts_ref[rows, lanes] + state * jnp.exp(-rate * passed))
        for at in range(0, run, 2):
            totals = []
            for spot in (at, at + 1):
                total = near_ref[spot * SUB : (spot + 1) * SUB, lanes]
                for mode in range(modes):
                    total = total + terms[mode]
                terms = [terms[mode] * decays[mode] for mode in range(modes)]
                totals.append(total)
            rows = slice(at * SUB, (at + 2) * SUB)
            gate = spread_ref[rows, lanes].astype(F32)
            held_ref[rows, lanes] = (gate * jnp.concatenate(totals, axis=0)).astype(BF16)
        return carry

    lax.fori_loop(0, chan // LANE, step, 0)
    project(spread_table(tok, True), held_ref, gated_ref)
    project(gated_ref, weight_ref, sent_ref)
    wait_all(rest)


def project(left_ref, right_ref, out_ref):
    total = out_ref.shape[1]
    tile = 2 * LANE if total % (2 * LANE) == 0 else LANE
    for first in range(0, total, tile):
        lanes = slice(first, first + tile)
        out_ref[:, lanes] = jnp.dot(
            left_ref[...], right_ref[:, lanes], preferred_element_type=F32
        ).astype(out_ref.dtype)


def product(gated_ref, weight):
    return jnp.dot(gated_ref[...], weight, preferred_element_type=F32)


def middle_kernel(gated_ref, kept_weight, sent_weight, kept_ref, sent_ref):
    project(gated_ref, kept_weight, kept_ref)
    project(gated_ref, sent_weight, sent_ref)


def join_kernel(kept_ref, moved_ref, *going_refs):
    wide = going_refs[0].shape[1]
    for at, going_ref in enumerate(going_refs):
        lanes = slice(at * wide, (at + 1) * wide)
        going_ref[...] = (kept_ref[:, lanes] + moved_ref[:, lanes].astype(F32)).astype(BF16)


def going_kernel(gated_ref, weight_ref, moved_ref, after_ref, *going_refs):
    wide = going_refs[0].shape[1]
    for at, going_ref in enumerate(going_refs):
        lanes = slice(at * wide, (at + 1) * wide)
        total = product(gated_ref, weight_ref[:, lanes])
        going_ref[...] = (total + moved_ref[:, lanes].astype(F32)).astype(BF16)


def late_kernel(gated_ref, weight_hbm, *refs):
    (low_ref, high_ref, weight_ref, sems) = refs[-4:]
    half = low_ref.shape[1]
    wait_all(column_copies(1, 0, range(1), weight_hbm, weight_ref, sems))
    low_ref[...] = product(gated_ref, weight_ref[:, :half]).astype(BF16)
    high_ref[...] = product(gated_ref, weight_ref[:, half:]).astype(BF16)


def own_kernel(gated_ref, weight_hbm, low_ref, high_ref, *refs):
    others, (first_ref, own_ref, weight_ref, sems) = refs[:-4], refs[-4:]
    narrow, half = first_ref.shape[1], low_ref.shape[1]
    wait_all(column_copies(0, 0, range(1), weight_hbm, weight_ref, sems))
    total = low_ref[:, :narrow].astype(F32) + product(gated_ref, weight_ref[:, :narrow])
    for other in others:
        total = total + other[...].astype(F32)
    first_ref[...] = total.astype(BF16)
    own_ref[:, : half - narrow] = low_ref[:, narrow:].astype(F32) + product(
        gated_ref, weight_ref[:, narrow:half]
    )
    own_ref[:, half - narrow :] = high_ref[...].astype(F32) + product(
        gated_ref, weight_ref[:, half:]
    )


def final_kernel(first_ref, own_ref, *refs):
    others, (out_hbm, wide_ref, sems) = refs[:-3], refs[-3:]
    tok, narrow = first_ref.shape
    count = sems.shape[0] - 1
    copies = [
        pltpu.make_async_copy(first_ref, out_hbm.at[:, pl.ds(0, narrow)], sems.at[count])
    ]
    copies[0].start()
    for part in range(count):
        rows = pl.ds(part * tok // count, tok // count)
        total = own_ref[rows, :]
        for other in others:
            total = total + other[rows, :].astype(F32)
        wide_ref[rows, :] = total.astype(BF16)
        columns = pl.ds(narrow, wide_ref.shape[1])
        copies.append(
            pltpu.make_async_copy(wide_ref.at[rows], out_hbm.at[rows, columns], sems.at[part])
        )
        copies[-1].start()
    wait_all(copies)


def call(kernel, outs, *operands, scratch=(), macs=0, out_spec=VMEM):
    specs, arrays = [], []
    for operand in operands:
        spec, array = operand if isinstance(operand, tuple) else (VMEM, operand)
        specs.append(ANY if spec is HBM else spec)
        arrays.append(in_hbm(array) if spec is HBM else array)
    return pl.pallas_call(
        kernel,
        out_shape=outs,
        in_specs=specs,
        out_specs=[out_spec] * len(outs),
        scratch_shapes=scratch,
        compiler_params=PARAMS,
        cost_estimate=pl.CostEstimate(flops=2 * macs, bytes_accessed=0, transcendentals=0),
    )(*arrays)


def body(values, gate, residues, rates, skip, out_weight):
    shards, tp = lax.axis_size("seq"), lax.axis_size("tp")
    tok, chan = values.shape
    modes = rates.shape[0]
    chips = tp // 2
    away = chips - 1
    block = out_weight.shape[1] // tp
    here = pltpu.VMEM
    parts = 4 if chan % (4 * LANE) == 0 else 1
    cores = [(rank, rank ^ 1) for rank in range(tp)]
    sources = [(HBM, each) for each in (values, rates, residues, skip.reshape(1, chan), gate)]
    (wire,) = call(
        state_kernel,
        [jax.ShapeDtypeStruct((shards, modes, chan), BF16)],
        *sources[:2],
        scratch=[
            here((tok, chan), BF16),
            here((modes, chan), F32),
            pltpu.SemaphoreType.DMA((parts + 1,)),
        ],
    )
    states = lax.all_to_all(
        wire, "seq", split_axis=0, concat_axis=0, tiled=True,
        axis_index_groups=[group_order(shards)],
    )
    narrow = max(LANE, block // 4)
    wide = block - narrow
    weight = (HBM, out_weight)
    *tables, first_weight, kept_weight = call(
        local_kernel,
        [
            here((tok, chan), F32),
            here((modes * SUB, chan), F32),
            here((modes, chan), F32),
            here((modes, chan), F32),
            here((tok, chan), BF16),
            here((chan, away * narrow), BF16),
            here((chan, away * narrow), BF16),
        ],
        *sources, weight,
        scratch=[
            here((tok, chan), BF16),
            here((modes, chan), F32),
            here((1, chan), F32),
            here((tok, chan), BF16),
            here((tok, chan), F32),
            here((tok // SUB, LANE), F32),
            pltpu.SemaphoreType.DMA((len(sources),)),
            pltpu.SemaphoreType.DMA((2, away * ROW_CUTS)),
        ],
    )

    gated, sent, sent_weight, last_weight = call(
        gate_kernel,
        [
            here((tok, chan), BF16),
            here((tok, away * narrow), BF16),
            here((chan, away * wide), BF16),
            here((chan, away * wide), BF16),
        ],
        states, *tables, first_weight, weight,
        scratch=[
            here((tok, chan), BF16),
            here((modes, chan), F32),
            here((modes, chan), F32),
            pltpu.SemaphoreType.DMA((2, away * ROW_CUTS)),
        ],
    )
    moved_first = lax.ppermute(sent, "tp", cores)
    kept, sent = call(
        middle_kernel,
        [here((tok, away * narrow), F32), here((tok, away * wide), BF16)],
        gated, kept_weight, sent_weight,
    )
    moved = lax.ppermute(sent, "tp", cores)

    def to_chips(going):
        return [
            lax.ppermute(each, "tp", [(rank, (rank + 2 * hop) % tp) for rank in range(tp)])
            for hop, each in enumerate(going, 1)
        ]

    hint = 16 * tok * chan * block
    going = call(join_kernel, [here((tok, narrow), BF16)] * away, kept, moved_first, macs=hint)
    first = to_chips(going)
    going = call(
        going_kernel, [here((tok, wide), BF16)] * away,
        gated, last_weight, moved, (ANY, going[-1]),
    )
    second = to_chips(going)
    late = [here((chan, block), BF16), pltpu.SemaphoreType.DMA((ROW_CUTS,))]
    halves = call(
        late_kernel, [here((tok, block // 2), BF16)] * 2,
        gated, weight, (ANY, going[-1]), (ANY, first[-1]), scratch=late, macs=hint,
    )
    halves = [lax.ppermute(each, "tp", cores) for each in halves]
    done, own = call(
        own_kernel, [here((tok, narrow), BF16), here((tok, wide), F32)],
        gated, weight, *halves, *first, scratch=late,
    )
    (out,) = call(
        final_kernel, [jax.ShapeDtypeStruct((tok, block), BF16)], done, own, *second,
        scratch=[here((tok, wide), BF16), pltpu.SemaphoreType.DMA((3,))],
        out_spec=ANY,
    )
    return out


def solution(mesh):
    placed = (P("seq", "tp"), P("seq", "tp"), P(None, "tp"), P(None, "tp"), P("tp"), P("tp", None))
    return jax.shard_map(
        body, mesh=mesh, in_specs=placed, out_specs=P("seq", "tp"), check_vma=False
    )
```

```python
from functools import partial

import jax
import jax.numpy as jnp
from jax import lax
from jax.experimental import pallas as pl
from jax.experimental.pallas import tpu as pltpu
from jax.sharding import PartitionSpec as P

SUB, LANE = 8, 128
F32, BF16 = jnp.float32, jnp.bfloat16

VMEM = pl.BlockSpec(memory_space=pltpu.VMEM)
ANY = pl.BlockSpec(memory_space=pl.ANY)
HBM = "hbm"
PARAMS = pltpu.CompilerParams(vmem_limit_bytes=24 * 2**20)


def in_hbm(array):
    return pltpu.with_memory_space_constraint(array, pltpu.HBM)


def in_vmem(array):
    return pltpu.with_memory_space_constraint(array, pltpu.VMEM)


def row_of(block, mode):
    return jnp.broadcast_to(block[mode : mode + 1, :], (SUB, LANE))


def sublane():
    return lax.broadcasted_iota(jnp.int32, (SUB, LANE), 0)


def lanes_at(step):
    return pl.ds(pl.multiple_of(step * LANE, LANE), LANE)


def gains_of(residues, rates):
    return residues * jnp.sqrt(2.0 * rates)


def spread_table(tok):
    run = tok // SUB
    row = lax.broadcasted_iota(jnp.int32, (tok, tok), 0)
    col = lax.broadcasted_iota(jnp.int32, (tok, tok), 1)
    return (col == row % SUB * run + row // SUB).astype(F32).astype(BF16)


ROW_CUTS = 4


def column_copies(other, begin, slots, weight_hbm, out_ref, sems):
    rank = lax.axis_index("tp")
    chips = lax.axis_size("tp") // 2
    block = weight_hbm.shape[1] // (2 * chips)
    wide = out_ref.shape[1] // len(slots)
    tall = out_ref.shape[0] // ROW_CUTS
    core = 1 - rank % 2 if other else rank % 2
    copies = []
    for at, slot in enumerate(slots):
        owner = (rank // 2 + slot) % chips * 2 + core
        columns = pl.ds(pl.multiple_of(owner * block + begin, LANE), wide)
        for cut in range(ROW_CUTS):
            rows = pl.ds(cut * tall, tall)
            copies.append(
                pltpu.make_async_copy(
                    weight_hbm.at[rows, columns],
                    out_ref.at[rows, pl.ds(at * wide, wide)],
                    sems.at[at * ROW_CUTS + cut],
                )
            )
            copies[-1].start()
    return copies


def group_order(count):
    others = [rank for rank in range(count) if rank != count // 2]
    return [count // 2] + sorted(others, key=lambda rank: (-abs(2 * rank + 1 - count), rank))


def wait_all(copies):
    for copy in copies:
        copy.wait()


def state_kernel(values_hbm, rates_hbm, wire_ref, values_ref, rates_ref, sems):
    tok, chan = values_ref.shape
    modes = rates_ref.shape[0]
    parts = sems.shape[0] - 1
    width = chan // parts
    first = pltpu.make_async_copy(rates_hbm, rates_ref, sems.at[parts])
    first.start()
    pieces = []
    for part in range(parts):
        lanes = pl.ds(part * width, width)
        pieces.append(
            pltpu.make_async_copy(
                values_hbm.at[:, lanes], values_ref.at[:, lanes], sems.at[part]
            )
        )
        pieces[-1].start()
    left = (SUB - 1 - sublane()).astype(F32)
    first.wait()
    for index in range(chan // LANE):
        if index * LANE % width == 0:
            pieces[index * LANE // width].wait()
        lanes = slice(index * LANE, (index + 1) * LANE)
        rates = rates_ref[:, lanes]
        decay = jnp.exp(-float(SUB) * rates)
        decays = [row_of(decay, mode) for mode in range(modes)]
        held = [jnp.zeros((SUB, LANE), F32)] * modes
        for at in range(0, tok, 2 * SUB):
            pair = values_ref[at : at + 2 * SUB, lanes].astype(F32)
            for half in (pair[:SUB], pair[SUB:]):
                held = [decays[mode] * held[mode] + half for mode in range(modes)]
        rows = [
            jnp.sum(held[mode] * jnp.exp(-row_of(rates, mode) * left), axis=0, keepdims=True)
            for mode in range(modes)
        ]
        state = jnp.concatenate(rows, axis=0).astype(BF16)
        for shard in range(wire_ref.shape[0]):
            wire_ref[shard, :, lanes] = state


def local_kernel(
    values_hbm, rates_hbm, residues_hbm, skip_hbm, gate_hbm, weight_hbm,
    near_ref, reach_ref, decay_ref, far_ref, gate_ref, first_weight, kept_weight,
    values_ref, rates_ref, residues_ref, skip_ref, wide_ref, taps_ref, sum_ref, order_ref, sems, weight_sems,
):
    tok, chan = values_ref.shape
    modes = rates_ref.shape[0]
    run = tok // SUB
    copies = [
        pltpu.make_async_copy(source, target, sems.at[at])
        for at, (source, target) in enumerate(
            (
                (values_hbm, values_ref),
                (gate_hbm, gate_ref),
                (rates_hbm, rates_ref),
                (residues_hbm, residues_ref),
                (skip_hbm, skip_ref),
            )
        )
    ]
    for copy in copies:
        copy.start()
    slots = range(1, lax.axis_size("tp") // 2)
    rest = column_copies(1, 0, slots, weight_hbm, first_weight, weight_sems.at[0])
    rest += column_copies(0, 0, slots, weight_hbm, kept_weight, weight_sems.at[1])
    table = spread_table(tok)
    wait_all(copies)
    wide_ref[...] = jnp.dot(table, values_ref[...], preferred_element_type=F32)

    def step(index, carry):
        lanes = lanes_at(index)
        place = sublane()
        rates = rates_ref[:, lanes]
        gains = gains_of(residues_ref[:, lanes], rates)

        ahead = place.astype(F32)
        decay = jnp.exp(-float(SUB) * rates)
        terms = [
            row_of(gains, mode) * jnp.exp(-row_of(rates, mode) * ahead) for mode in range(modes)
        ]
        for at in range(0, run, SUB):
            total = terms[0]
            for mode in range(1, modes):
                total = total + terms[mode]
            if at == 0:
                total = jnp.where(place == 0, total + skip_ref[:, lanes], total)
            terms = [terms[mode] * row_of(decay, mode) for mode in range(modes)]
            taps_ref[at : at + SUB, :] = total

        for at in range(0, run, SUB):
            sums = [jnp.zeros((SUB, LANE), F32)] * SUB
            for early in range(0, at + SUB, SUB):
                for lag in range(at - early - SUB + 1, at - early + SUB):
                    if lag < 0:
                        continue
                    tap = jnp.broadcast_to(taps_ref[lag : lag + 1, :], (SUB, LANE))
                    for source in range(SUB):
                        target = early + source + lag - at
                        if 0 <= target < SUB:
                            rows = pl.ds((early + source) * SUB, SUB)
                            sums[target] = sums[target] + tap * wide_ref[rows, lanes]
            for target in range(SUB):
                sum_ref[pl.ds((at + target) * SUB, SUB), :] = sums[target]

        decay = jnp.exp(-rates)
        decay_run = jnp.exp(-float(run) * rates)
        decays = [row_of(decay, mode) for mode in range(modes)]
        held = [jnp.zeros((SUB, LANE), F32)] * modes
        for at in range(run):
            value = wide_ref[at * SUB : (at + 1) * SUB, lanes]
            held = [decays[mode] * held[mode] + value for mode in range(modes)]
        terms = []
        for mode in range(modes):
            whole, power = held[mode], row_of(decay_run, mode)
            for shift in (1, 2, 4):
                moved = jnp.where(place >= shift, pltpu.roll(whole, shift, 0), 0.0)
                whole = whole + power * moved
                power = power * power
            before = jnp.where(place >= 1, pltpu.roll(whole, 1, 0), 0.0)
            first = row_of(gains, mode) * decays[mode]
            terms.append(first * before)
            rows = slice(mode * SUB, (mode + 1) * SUB)
            reach_ref[rows, lanes] = first * jnp.exp(-row_of(rates, mode) * ahead)
        for at in range(run):
            total = sum_ref[at * SUB : (at + 1) * SUB, :]
            for mode in range(modes):
                total = total + terms[mode]
            terms = [terms[mode] * decays[mode] for mode in range(modes)]
            order_ref[pl.ds(at, SUB, stride=run), :] = total
        near_ref[:, lanes] = order_ref[...]
        decay_ref[:, lanes] = jnp.exp(-float(SUB) * rates)
        far_ref[:, lanes] = jnp.exp(-float(tok) * rates)
        return carry

    lax.fori_loop(0, chan // LANE, step, 0)
    wait_all(rest)


def gate_kernel(
    states_ref, near_ref, reach_ref, decay_ref, far_ref, gate_ref, weight_ref, weight_hbm,
    gated_ref, sent_ref, later_weight, last_weight, state_ref, sems,
):
    slots = range(1, lax.axis_size("tp") // 2)
    begin = weight_ref.shape[1] // len(slots)
    rest = column_copies(1, begin, slots, weight_hbm, later_weight, sems.at[0])
    rest += column_copies(0, begin, slots, weight_hbm, last_weight, sems.at[1])
    tok, chan = gate_ref.shape
    shards, modes = states_ref.shape[:2]
    place = lax.axis_index("seq")
    far = far_ref[...]
    before = jnp.zeros((modes, chan), F32)
    order = group_order(shards)
    for shard in range(shards - 1):
        passed = far * before + states_ref[order.index(shard)].astype(F32)
        before = jnp.where(shard < place, passed, before)
    state_ref[...] = before

    def step(index, carry):
        lanes = lanes_at(index)
        decays, terms = [], []
        for mode in range(modes):
            rows, row = slice(mode * SUB, (mode + 1) * SUB), slice(mode, mode + 1)
            decays.append(jnp.broadcast_to(decay_ref[row, lanes], (SUB, LANE)))
            state = jnp.broadcast_to(state_ref[row, lanes], (SUB, LANE))
            terms.append(state * reach_ref[rows, lanes])
        for at in range(0, tok, 2 * SUB):
            totals = []
            for first in (at, at + SUB):
                total = near_ref[first : first + SUB, lanes]
                for mode in range(modes):
                    total = total + terms[mode]
                terms = [terms[mode] * decays[mode] for mode in range(modes)]
                totals.append(total)
            rows = slice(at, at + 2 * SUB)
            gate = gate_ref[rows, lanes].astype(F32)
            gated_ref[rows, lanes] = (gate * jnp.concatenate(totals, axis=0)).astype(BF16)
        return carry

    lax.fori_loop(0, chan // LANE, step, 0)
    project(gated_ref, weight_ref, sent_ref)
    wait_all(rest)


def project(left_ref, right_ref, out_ref):
    total = out_ref.shape[1]
    tile = 2 * LANE if total % (2 * LANE) == 0 else LANE
    for first in range(0, total, tile):
        lanes = slice(first, first + tile)
        out_ref[:, lanes] = jnp.dot(
            left_ref[...], right_ref[:, lanes], preferred_element_type=F32
        ).astype(out_ref.dtype)


def product(gated_ref, weight):
    return jnp.dot(gated_ref[...], weight, preferred_element_type=F32)


def middle_kernel(gated_ref, kept_weight, sent_weight, kept_ref, sent_ref):
    project(gated_ref, kept_weight, kept_ref)
    project(gated_ref, sent_weight, sent_ref)


def join_kernel(kept_ref, moved_ref, *going_refs):
    wide = going_refs[0].shape[1]
    for at, going_ref in enumerate(going_refs):
        lanes = slice(at * wide, (at + 1) * wide)
        going_ref[...] = (kept_ref[:, lanes] + moved_ref[:, lanes].astype(F32)).astype(BF16)


def going_kernel(gated_ref, weight_ref, moved_ref, after_ref, *going_refs):
    wide = going_refs[0].shape[1]
    for at, going_ref in enumerate(going_refs):
        lanes = slice(at * wide, (at + 1) * wide)
        total = product(gated_ref, weight_ref[:, lanes])
        going_ref[...] = (total + moved_ref[:, lanes].astype(F32)).astype(BF16)


def late_kernel(gated_ref, weight_hbm, *refs):
    (low_ref, high_ref, weight_ref, sems) = refs[-4:]
    half = low_ref.shape[1]
    wait_all(column_copies(1, 0, range(1), weight_hbm, weight_ref, sems))
    low_ref[...] = product(gated_ref, weight_ref[:, :half]).astype(BF16)
    high_ref[...] = product(gated_ref, weight_ref[:, half:]).astype(BF16)


def own_kernel(gated_ref, weight_hbm, low_ref, high_ref, *refs):
    others, (first_ref, own_ref, weight_ref, sems) = refs[:-4], refs[-4:]
    narrow, half = first_ref.shape[1], low_ref.shape[1]
    wait_all(column_copies(0, 0, range(1), weight_hbm, weight_ref, sems))
    total = low_ref[:, :narrow].astype(F32) + product(gated_ref, weight_ref[:, :narrow])
    for other in others:
        total = total + other[...].astype(F32)
    first_ref[...] = total.astype(BF16)
    own_ref[:, : half - narrow] = low_ref[:, narrow:].astype(F32) + product(
        gated_ref, weight_ref[:, narrow:half]
    )
    own_ref[:, half - narrow :] = high_ref[...].astype(F32) + product(
        gated_ref, weight_ref[:, half:]
    )


def final_kernel(first_ref, own_ref, *refs):
    others, (out_hbm, wide_ref, sems) = refs[:-3], refs[-3:]
    tok, narrow = first_ref.shape
    count = sems.shape[0] - 1
    copies = [
        pltpu.make_async_copy(first_ref, out_hbm.at[:, pl.ds(0, narrow)], sems.at[count])
    ]
    copies[0].start()
    for part in range(count):
        rows = pl.ds(part * tok // count, tok // count)
        total = own_ref[rows, :]
        for other in others:
            total = total + other[rows, :].astype(F32)
        wide_ref[rows, :] = total.astype(BF16)
        columns = pl.ds(narrow, wide_ref.shape[1])
        copies.append(
            pltpu.make_async_copy(wide_ref.at[rows], out_hbm.at[rows, columns], sems.at[part])
        )
        copies[-1].start()
    wait_all(copies)


def call(kernel, outs, *operands, scratch=(), macs=0, out_spec=VMEM):
    specs, arrays = [], []
    for operand in operands:
        spec, array = operand if isinstance(operand, tuple) else (VMEM, operand)
        specs.append(ANY if spec is HBM else spec)
        arrays.append(in_hbm(array) if spec is HBM else array)
    return pl.pallas_call(
        kernel,
        out_shape=outs,
        in_specs=specs,
        out_specs=[out_spec] * len(outs),
        scratch_shapes=scratch,
        compiler_params=PARAMS,
        cost_estimate=pl.CostEstimate(flops=2 * macs, bytes_accessed=0, transcendentals=0),
    )(*arrays)


def body(values, gate, residues, rates, skip, out_weight):
    shards, tp = lax.axis_size("seq"), lax.axis_size("tp")
    tok, chan = values.shape
    modes = rates.shape[0]
    chips = tp // 2
    away = chips - 1
    block = out_weight.shape[1] // tp
    here = pltpu.VMEM
    parts = 4 if chan % (4 * LANE) == 0 else 1
    cores = [(rank, rank ^ 1) for rank in range(tp)]
    sources = [(HBM, each) for each in (values, rates, residues, skip.reshape(1, chan), gate)]
    (wire,) = call(
        state_kernel,
        [jax.ShapeDtypeStruct((shards, modes, chan), BF16)],
        *sources[:2],
        scratch=[
            here((tok, chan), BF16),
            here((modes, chan), F32),
            pltpu.SemaphoreType.DMA((parts + 1,)),
        ],
    )
    states = lax.all_to_all(
        wire, "seq", split_axis=0, concat_axis=0, tiled=True,
        axis_index_groups=[group_order(shards)],
    )
    narrow = max(LANE, block // 4)
    wide = block - narrow
    weight = (HBM, out_weight)
    *tables, first_weight, kept_weight = call(
        local_kernel,
        [
            here((tok, chan), F32),
            here((modes * SUB, chan), F32),
            here((modes, chan), F32),
            here((modes, chan), F32),
            here((tok, chan), BF16),
            here((chan, away * narrow), BF16),
            here((chan, away * narrow), BF16),
        ],
        *sources, weight,
        scratch=[
            here((tok, chan), BF16),
            here((modes, chan), F32),
            here((modes, chan), F32),
            here((1, chan), F32),
            here((tok, chan), F32),
            here((tok // SUB, LANE), F32),
            here((tok, LANE), F32),
            here((tok, LANE), F32),
            pltpu.SemaphoreType.DMA((len(sources),)),
            pltpu.SemaphoreType.DMA((2, away * ROW_CUTS)),
        ],
    )

    gated, sent, sent_weight, last_weight = call(
        gate_kernel,
        [
            here((tok, chan), BF16),
            here((tok, away * narrow), BF16),
            here((chan, away * wide), BF16),
            here((chan, away * wide), BF16),
        ],
        states, *tables, first_weight, weight,
        scratch=[
            here((modes, chan), F32),
            pltpu.SemaphoreType.DMA((2, away * ROW_CUTS)),
        ],
    )
    moved_first = lax.ppermute(sent, "tp", cores)
    kept, sent = call(
        middle_kernel,
        [here((tok, away * narrow), F32), here((tok, away * wide), BF16)],
        gated, kept_weight, sent_weight,
    )
    moved = lax.ppermute(sent, "tp", cores)

    def to_chips(going):
        return [
            lax.ppermute(each, "tp", [(rank, (rank + 2 * hop) % tp) for rank in reversed(range(tp))])
            for hop, each in enumerate(going, 1)
        ]

    hint = 16 * tok * chan * block
    going = call(join_kernel, [here((tok, narrow), BF16)] * away, kept, moved_first, macs=hint)
    first = to_chips(going)
    going = call(
        going_kernel, [here((tok, wide), BF16)] * away,
        gated, last_weight, moved, (ANY, going[-1]),
    )
    second = to_chips(going)
    late = [here((chan, block), BF16), pltpu.SemaphoreType.DMA((ROW_CUTS,))]
    halves = call(
        late_kernel, [here((tok, block // 2), BF16)] * 2,
        gated, weight, (ANY, going[-1]), (ANY, first[-1]), scratch=late, macs=hint,
    )
    halves = [lax.ppermute(each, "tp", cores) for each in halves]
    done, own = call(
        own_kernel, [here((tok, narrow), BF16), here((tok, wide), F32)],
        gated, weight, *halves, *first, scratch=late,
    )
    (out,) = call(
        final_kernel, [jax.ShapeDtypeStruct((tok, block), BF16)], done, own, *second,
        scratch=[here((tok, wide), BF16), pltpu.SemaphoreType.DMA((3,))],
        out_spec=ANY,
    )
    return out


def solution(mesh):
    placed = (P("seq", "tp"), P("seq", "tp"), P(None, "tp"), P(None, "tp"), P("tp"), P("tp", None))
    return jax.shard_map(
        body, mesh=mesh, in_specs=placed, out_specs=P("seq", "tp"), check_vma=False
    )
```

```python
from functools import partial

import jax
import jax.numpy as jnp
from jax import lax
from jax.experimental import pallas as pl
from jax.experimental.pallas import tpu as pltpu
from jax.sharding import PartitionSpec as P

SUB, LANE = 8, 128
F32, BF16 = jnp.float32, jnp.bfloat16

VMEM = pl.BlockSpec(memory_space=pltpu.VMEM)
ANY = pl.BlockSpec(memory_space=pl.ANY)
HBM = "hbm"
PARAMS = pltpu.CompilerParams(vmem_limit_bytes=24 * 2**20)


def in_hbm(array):
    return pltpu.with_memory_space_constraint(array, pltpu.HBM)


def in_vmem(array):
    return pltpu.with_memory_space_constraint(array, pltpu.VMEM)


def row_of(block, mode):
    return jnp.broadcast_to(block[mode : mode + 1, :], (SUB, LANE))


def sublane():
    return lax.broadcasted_iota(jnp.int32, (SUB, LANE), 0)


def lanes_at(step):
    return pl.ds(pl.multiple_of(step * LANE, LANE), LANE)


def gains_of(residues, rates):
    return residues * jnp.sqrt(2.0 * rates)


def spread_table(tok):
    run = tok // SUB
    row = lax.broadcasted_iota(jnp.int32, (tok, tok), 0)
    col = lax.broadcasted_iota(jnp.int32, (tok, tok), 1)
    return (col == row % SUB * run + row // SUB).astype(F32).astype(BF16)


ROW_CUTS = 4


def column_copies(other, begin, slots, weight_hbm, out_ref, sems):
    rank = lax.axis_index("tp")
    chips = lax.axis_size("tp") // 2
    block = weight_hbm.shape[1] // (2 * chips)
    wide = out_ref.shape[1] // len(slots)
    tall = out_ref.shape[0] // ROW_CUTS
    core = 1 - rank % 2 if other else rank % 2
    copies = []
    for at, slot in enumerate(slots):
        owner = (rank // 2 + slot) % chips * 2 + core
        columns = pl.ds(pl.multiple_of(owner * block + begin, LANE), wide)
        for cut in range(ROW_CUTS):
            rows = pl.ds(cut * tall, tall)
            copies.append(
                pltpu.make_async_copy(
                    weight_hbm.at[rows, columns],
                    out_ref.at[rows, pl.ds(at * wide, wide)],
                    sems.at[at * ROW_CUTS + cut],
                )
            )
            copies[-1].start()
    return copies


def group_order(count):
    others = [rank for rank in range(count) if rank != count // 2]
    return [count // 2] + sorted(others, key=lambda rank: (-abs(2 * rank + 1 - count), rank))


def wait_all(copies):
    for copy in copies:
        copy.wait()


def state_kernel(values_hbm, rates_hbm, wire_ref, values_ref, rates_ref, sems):
    tok, chan = values_ref.shape
    modes = rates_ref.shape[0]
    parts = sems.shape[0] - 1
    width = chan // parts
    first = pltpu.make_async_copy(rates_hbm, rates_ref, sems.at[parts])
    first.start()
    pieces = []
    for part in range(parts):
        lanes = pl.ds(part * width, width)
        pieces.append(
            pltpu.make_async_copy(
                values_hbm.at[:, lanes], values_ref.at[:, lanes], sems.at[part]
            )
        )
        pieces[-1].start()
    left = (SUB - 1 - sublane()).astype(F32)
    first.wait()
    for index in range(chan // LANE):
        if index * LANE % width == 0:
            pieces[index * LANE // width].wait()
        lanes = slice(index * LANE, (index + 1) * LANE)
        rates = rates_ref[:, lanes]
        decay = jnp.exp(-float(SUB) * rates)
        decays = [row_of(decay, mode) for mode in range(modes)]
        held = [jnp.zeros((SUB, LANE), F32)] * modes
        for at in range(0, tok, 2 * SUB):
            pair = values_ref[at : at + 2 * SUB, lanes].astype(F32)
            for half in (pair[:SUB], pair[SUB:]):
                held = [decays[mode] * held[mode] + half for mode in range(modes)]
        rows = [
            jnp.sum(held[mode] * jnp.exp(-row_of(rates, mode) * left), axis=0, keepdims=True)
            for mode in range(modes)
        ]
        state = jnp.concatenate(rows, axis=0).astype(BF16)
        for shard in range(wire_ref.shape[0]):
            wire_ref[shard, :, lanes] = state


def local_kernel(
    values_hbm, rates_hbm, residues_hbm, skip_hbm, gate_hbm, weight_hbm,
    near_ref, reach_ref, decay_ref, far_ref, gate_ref, first_weight, kept_weight,
    values_ref, rates_ref, residues_ref, skip_ref, wide_ref, taps_ref, first_ref, snap_ref,
    order_ref, sems, weight_sems,
):
    tok, chan = values_ref.shape
    modes = rates_ref.shape[0]
    run = tok // SUB
    copies = [
        pltpu.make_async_copy(source, target, sems.at[at])
        for at, (source, target) in enumerate(
            (
                (values_hbm, values_ref),
                (rates_hbm, rates_ref),
                (residues_hbm, residues_ref),
                (skip_hbm, skip_ref),
                (gate_hbm, gate_ref),
            )
        )
    ]
    for copy in copies:
        copy.start()
    slots = range(1, lax.axis_size("tp") // 2)
    rest = column_copies(1, 0, slots, weight_hbm, first_weight, weight_sems.at[0])
    rest += column_copies(0, 0, slots, weight_hbm, kept_weight, weight_sems.at[1])
    rest.append(copies.pop())
    table = spread_table(tok)
    wait_all(copies)
    wide_ref[...] = jnp.dot(table, values_ref[...], preferred_element_type=F32)

    def step(index, carry):
        lanes = lanes_at(index)
        place = sublane()
        rates = rates_ref[:, lanes]
        gains = gains_of(residues_ref[:, lanes], rates)

        ahead = place.astype(F32)
        decay, decay_block = jnp.exp(-rates), jnp.exp(-float(SUB) * rates)
        decay_run = jnp.exp(-float(run) * rates)
        decays = [row_of(decay, mode) for mode in range(modes)]
        taps = jnp.where(place == 0, skip_ref[:, lanes], 0.0)
        for mode in range(modes):
            gain = row_of(gains, mode)
            term = gain * jnp.exp(-row_of(rates, mode) * ahead)
            taps = taps + term
            first_ref[mode * SUB : (mode + 1) * SUB, :] = gain * decays[mode]
            reach_ref[mode * SUB : (mode + 1) * SUB, lanes] = term * decays[mode]
        taps_ref[...] = taps

        held = [jnp.zeros((SUB, LANE), F32)] * modes
        for at in range(run):
            if at % SUB == 0:
                for mode in range(modes):
                    snap_ref[at // SUB, mode * SUB : (mode + 1) * SUB, :] = held[mode]
            value = wide_ref[at * SUB : (at + 1) * SUB, lanes]
            held = [decays[mode] * held[mode] + value for mode in range(modes)]
        for mode in range(modes):
            whole, power = held[mode], row_of(decay_run, mode)
            for shift in (1, 2, 4):
                moved = jnp.where(place >= shift, pltpu.roll(whole, shift, 0), 0.0)
                whole = whole + power * moved
                power = power * power
            before = jnp.where(place >= 1, pltpu.roll(whole, 1, 0), 0.0)
            rows = slice(mode * SUB, (mode + 1) * SUB)
            fade = row_of(decay_block, mode)
            for block in range(run // SUB):
                snap_ref[block, rows, :] = first_ref[rows, :] * (snap_ref[block, rows, :] + before)
                before = fade * before

        for block in range(run // SUB):
            values = [
                wide_ref[(block * SUB + at) * SUB : (block * SUB + at + 1) * SUB, lanes]
                for at in range(SUB)
            ]
            sums = [jnp.zeros((SUB, LANE), F32)] * SUB
            for lag in range(SUB):
                tap = jnp.broadcast_to(taps_ref[lag : lag + 1, :], (SUB, LANE))
                for at in range(lag, SUB):
                    sums[at] = sums[at] + tap * values[at - lag]
            terms = [
                snap_ref[block, mode * SUB : (mode + 1) * SUB, :] for mode in range(modes)
            ]
            for at in range(SUB):
                total = sums[at]
                for mode in range(modes):
                    total = total + terms[mode]
                terms = [terms[mode] * decays[mode] for mode in range(modes)]
                order_ref[pl.ds(block * SUB + at, SUB, stride=run), :] = total
        near_ref[:, lanes] = order_ref[...]
        decay_ref[:, lanes] = jnp.exp(-float(SUB) * rates)
        far_ref[:, lanes] = jnp.exp(-float(tok) * rates)
        return carry

    lax.fori_loop(0, chan // LANE, step, 0)
    wait_all(rest)


def gate_kernel(
    states_ref, near_ref, reach_ref, decay_ref, far_ref, gate_ref, weight_ref, weight_hbm,
    gated_ref, sent_ref, later_weight, last_weight, state_ref, sems,
):
    slots = range(1, lax.axis_size("tp") // 2)
    begin = weight_ref.shape[1] // len(slots)
    rest = column_copies(1, begin, slots, weight_hbm, later_weight, sems.at[0])
    rest += column_copies(0, begin, slots, weight_hbm, last_weight, sems.at[1])
    tok, chan = gate_ref.shape
    shards, modes = states_ref.shape[:2]
    place = lax.axis_index("seq")
    far = far_ref[...]
    before = jnp.zeros((modes, chan), F32)
    order = group_order(shards)
    for shard in range(shards - 1):
        passed = far * before + states_ref[order.index(shard)].astype(F32)
        before = jnp.where(shard < place, passed, before)
    state_ref[...] = before

    def step(index, carry):
        lanes = lanes_at(index)
        decays, terms = [], []
        for mode in range(modes):
            rows, row = slice(mode * SUB, (mode + 1) * SUB), slice(mode, mode + 1)
            decays.append(jnp.broadcast_to(decay_ref[row, lanes], (SUB, LANE)))
            state = jnp.broadcast_to(state_ref[row, lanes], (SUB, LANE))
            terms.append(state * reach_ref[rows, lanes])
        for at in range(0, tok, 2 * SUB):
            totals = []
            for first in (at, at + SUB):
                total = near_ref[first : first + SUB, lanes]
                for mode in range(modes):
                    total = total + terms[mode]
                terms = [terms[mode] * decays[mode] for mode in range(modes)]
                totals.append(total)
            rows = slice(at, at + 2 * SUB)
            gate = gate_ref[rows, lanes].astype(F32)
            gated_ref[rows, lanes] = (gate * jnp.concatenate(totals, axis=0)).astype(BF16)
        return carry

    lax.fori_loop(0, chan // LANE, step, 0)
    project(gated_ref, weight_ref, sent_ref)
    wait_all(rest)


def project(left_ref, right_ref, out_ref):
    total = out_ref.shape[1]
    tile = 2 * LANE if total % (2 * LANE) == 0 else LANE
    for first in range(0, total, tile):
        lanes = slice(first, first + tile)
        out_ref[:, lanes] = jnp.dot(
            left_ref[...], right_ref[:, lanes], preferred_element_type=F32
        ).astype(out_ref.dtype)


def product(gated_ref, weight):
    return jnp.dot(gated_ref[...], weight, preferred_element_type=F32)


def middle_kernel(gated_ref, kept_weight, sent_weight, kept_ref, sent_ref):
    project(gated_ref, kept_weight, kept_ref)
    project(gated_ref, sent_weight, sent_ref)


def join_kernel(kept_ref, moved_ref, *going_refs):
    wide = going_refs[0].shape[1]
    for at, going_ref in enumerate(going_refs):
        lanes = slice(at * wide, (at + 1) * wide)
        going_ref[...] = (kept_ref[:, lanes] + moved_ref[:, lanes].astype(F32)).astype(BF16)


def going_kernel(gated_ref, weight_ref, moved_ref, after_ref, *going_refs):
    wide = going_refs[0].shape[1]
    for at, going_ref in enumerate(going_refs):
        lanes = slice(at * wide, (at + 1) * wide)
        total = product(gated_ref, weight_ref[:, lanes])
        going_ref[...] = (total + moved_ref[:, lanes].astype(F32)).astype(BF16)


def late_kernel(gated_ref, weight_hbm, *refs):
    (low_ref, high_ref, weight_ref, sems) = refs[-4:]
    half = low_ref.shape[1]
    wait_all(column_copies(1, 0, range(1), weight_hbm, weight_ref, sems))
    low_ref[...] = product(gated_ref, weight_ref[:, :half]).astype(BF16)
    high_ref[...] = product(gated_ref, weight_ref[:, half:]).astype(BF16)


def own_kernel(gated_ref, weight_hbm, low_ref, high_ref, *refs):
    others, (first_ref, own_ref, weight_ref, sems) = refs[:-4], refs[-4:]
    narrow, half = first_ref.shape[1], low_ref.shape[1]
    wait_all(column_copies(0, 0, range(1), weight_hbm, weight_ref, sems))
    total = low_ref[:, :narrow].astype(F32) + product(gated_ref, weight_ref[:, :narrow])
    for other in others:
        total = total + other[...].astype(F32)
    first_ref[...] = total.astype(BF16)
    own_ref[:, : half - narrow] = low_ref[:, narrow:].astype(F32) + product(
        gated_ref, weight_ref[:, narrow:half]
    )
    own_ref[:, half - narrow :] = high_ref[...].astype(F32) + product(
        gated_ref, weight_ref[:, half:]
    )


def final_kernel(first_ref, own_ref, *refs):
    others, (out_hbm, wide_ref, sems) = refs[:-3], refs[-3:]
    tok, narrow = first_ref.shape
    count = sems.shape[0] - 1
    copies = [
        pltpu.make_async_copy(first_ref, out_hbm.at[:, pl.ds(0, narrow)], sems.at[count])
    ]
    copies[0].start()
    for part in range(count):
        rows = pl.ds(part * tok // count, tok // count)
        total = own_ref[rows, :]
        for other in others:
            total = total + other[rows, :].astype(F32)
        wide_ref[rows, :] = total.astype(BF16)
        columns = pl.ds(narrow, wide_ref.shape[1])
        copies.append(
            pltpu.make_async_copy(wide_ref.at[rows], out_hbm.at[rows, columns], sems.at[part])
        )
        copies[-1].start()
    wait_all(copies)


def call(kernel, outs, *operands, scratch=(), macs=0, out_spec=VMEM):
    specs, arrays = [], []
    for operand in operands:
        spec, array = operand if isinstance(operand, tuple) else (VMEM, operand)
        specs.append(ANY if spec is HBM else spec)
        arrays.append(in_hbm(array) if spec is HBM else array)
    return pl.pallas_call(
        kernel,
        out_shape=outs,
        in_specs=specs,
        out_specs=[out_spec] * len(outs),
        scratch_shapes=scratch,
        compiler_params=PARAMS,
        cost_estimate=pl.CostEstimate(flops=2 * macs, bytes_accessed=0, transcendentals=0),
    )(*arrays)


def body(values, gate, residues, rates, skip, out_weight):
    shards, tp = lax.axis_size("seq"), lax.axis_size("tp")
    tok, chan = values.shape
    modes = rates.shape[0]
    chips = tp // 2
    away = chips - 1
    block = out_weight.shape[1] // tp
    here = pltpu.VMEM
    parts = 4 if chan % (4 * LANE) == 0 else 1
    cores = [(rank, rank ^ 1) for rank in range(tp)]
    sources = [(HBM, each) for each in (values, rates, residues, skip.reshape(1, chan), gate)]
    (wire,) = call(
        state_kernel,
        [jax.ShapeDtypeStruct((shards, modes, chan), BF16)],
        *sources[:2],
        scratch=[
            here((tok, chan), BF16),
            here((modes, chan), F32),
            pltpu.SemaphoreType.DMA((parts + 1,)),
        ],
    )
    states = lax.all_to_all(
        wire, "seq", split_axis=0, concat_axis=0, tiled=True,
        axis_index_groups=[group_order(shards)],
    )
    narrow = max(LANE, block // 4)
    wide = block - narrow
    weight = (HBM, out_weight)
    *tables, first_weight, kept_weight = call(
        local_kernel,
        [
            here((tok, chan), F32),
            here((modes * SUB, chan), F32),
            here((modes, chan), F32),
            here((modes, chan), F32),
            here((tok, chan), BF16),
            here((chan, away * narrow), BF16),
            here((chan, away * narrow), BF16),
        ],
        *sources, weight,
        scratch=[
            here((tok, chan), BF16),
            here((modes, chan), F32),
            here((modes, chan), F32),
            here((1, chan), F32),
            here((tok, chan), F32),
            here((SUB, LANE), F32),
            here((modes * SUB, LANE), F32),
            here((tok // SUB // SUB, modes * SUB, LANE), F32),
            here((tok, LANE), F32),
            pltpu.SemaphoreType.DMA((len(sources),)),
            pltpu.SemaphoreType.DMA((2, away * ROW_CUTS)),
        ],
    )

    gated, sent, sent_weight, last_weight = call(
        gate_kernel,
        [
            here((tok, chan), BF16),
            here((tok, away * narrow), BF16),
            here((chan, away * wide), BF16),
            here((chan, away * wide), BF16),
        ],
        states, *tables, first_weight, weight,
        scratch=[
            here((modes, chan), F32),
            pltpu.SemaphoreType.DMA((2, away * ROW_CUTS)),
        ],
    )
    moved_first = lax.ppermute(sent, "tp", cores)
    kept, sent = call(
        middle_kernel,
        [here((tok, away * narrow), F32), here((tok, away * wide), BF16)],
        gated, kept_weight, sent_weight,
    )
    moved = lax.ppermute(sent, "tp", cores)

    def to_chips(going):
        return [
            lax.ppermute(each, "tp", [(rank, (rank + 2 * hop) % tp) for rank in reversed(range(tp))])
            for hop, each in enumerate(going, 1)
        ]

    hint = 16 * tok * chan * block
    going = call(join_kernel, [here((tok, narrow), BF16)] * away, kept, moved_first, macs=hint)
    first = to_chips(going)
    going = call(
        going_kernel, [here((tok, wide), BF16)] * away,
        gated, last_weight, moved, (ANY, going[-1]),
    )
    second = to_chips(going)
    late = [here((chan, block), BF16), pltpu.SemaphoreType.DMA((ROW_CUTS,))]
    halves = call(
        late_kernel, [here((tok, block // 2), BF16)] * 2,
        gated, weight, (ANY, going[-1]), (ANY, first[-1]), scratch=late, macs=hint,
    )
    halves = [lax.ppermute(each, "tp", cores) for each in halves]
    done, own = call(
        own_kernel, [here((tok, narrow), BF16), here((tok, wide), F32)],
        gated, weight, *halves, *first, scratch=late,
    )
    (out,) = call(
        final_kernel, [jax.ShapeDtypeStruct((tok, block), BF16)], done, own, *second,
        scratch=[here((tok, wide), BF16), pltpu.SemaphoreType.DMA((3,))],
        out_spec=ANY,
    )
    return out


def solution(mesh):
    placed = (P("seq", "tp"), P("seq", "tp"), P(None, "tp"), P(None, "tp"), P("tp"), P("tp", None))
    return jax.shard_map(
        body, mesh=mesh, in_specs=placed, out_specs=P("seq", "tp"), check_vma=False
    )
```

```python
from functools import partial

import jax
import jax.numpy as jnp
from jax import lax
from jax.experimental import pallas as pl
from jax.experimental.pallas import tpu as pltpu
from jax.sharding import PartitionSpec as P

SUB, LANE = 8, 128
F32, BF16 = jnp.float32, jnp.bfloat16

VMEM = pl.BlockSpec(memory_space=pltpu.VMEM)
ANY = pl.BlockSpec(memory_space=pl.ANY)
HBM = "hbm"
PARAMS = pltpu.CompilerParams(vmem_limit_bytes=24 * 2**20)


def in_hbm(array):
    return pltpu.with_memory_space_constraint(array, pltpu.HBM)


def in_vmem(array):
    return pltpu.with_memory_space_constraint(array, pltpu.VMEM)


def row_of(block, mode):
    return jnp.broadcast_to(block[mode : mode + 1, :], (SUB, LANE))


def sublane():
    return lax.broadcasted_iota(jnp.int32, (SUB, LANE), 0)


def lanes_at(step):
    return pl.ds(pl.multiple_of(step * LANE, LANE), LANE)


def gains_of(residues, rates):
    return residues * jnp.sqrt(2.0 * rates)


def spread_table(tok):
    run = tok // SUB
    row = lax.broadcasted_iota(jnp.int32, (tok, tok), 0)
    col = lax.broadcasted_iota(jnp.int32, (tok, tok), 1)
    return (col == row % SUB * run + row // SUB).astype(F32).astype(BF16)


ROW_CUTS = 4


def column_copies(other, begin, slots, weight_hbm, out_ref, sems):
    rank = lax.axis_index("tp")
    chips = lax.axis_size("tp") // 2
    block = weight_hbm.shape[1] // (2 * chips)
    wide = out_ref.shape[1] // len(slots)
    tall = out_ref.shape[0] // ROW_CUTS
    core = 1 - rank % 2 if other else rank % 2
    copies = []
    for at, slot in enumerate(slots):
        owner = (rank // 2 + slot) % chips * 2 + core
        columns = pl.ds(pl.multiple_of(owner * block + begin, LANE), wide)
        for cut in range(ROW_CUTS):
            rows = pl.ds(cut * tall, tall)
            copies.append(
                pltpu.make_async_copy(
                    weight_hbm.at[rows, columns],
                    out_ref.at[rows, pl.ds(at * wide, wide)],
                    sems.at[at * ROW_CUTS + cut],
                )
            )
            copies[-1].start()
    return copies


def group_order(count):
    return [(count // 2 + at) % count for at in range(count)]


def wait_all(copies):
    for copy in copies:
        copy.wait()


def state_kernel(values_hbm, rates_hbm, wire_ref, values_ref, rates_ref, sems):
    tok, chan = values_ref.shape
    modes = rates_ref.shape[0]
    parts = sems.shape[0] - 1
    width = chan // parts
    first = pltpu.make_async_copy(rates_hbm, rates_ref, sems.at[parts])
    first.start()
    pieces = []
    for part in range(parts):
        lanes = pl.ds(part * width, width)
        pieces.append(
            pltpu.make_async_copy(
                values_hbm.at[:, lanes], values_ref.at[:, lanes], sems.at[part]
            )
        )
        pieces[-1].start()
    left = (SUB - 1 - sublane()).astype(F32)
    first.wait()
    for index in range(chan // LANE):
        if index * LANE % width == 0:
            pieces[index * LANE // width].wait()
        lanes = slice(index * LANE, (index + 1) * LANE)
        rates = rates_ref[:, lanes]
        decay = jnp.exp(-float(SUB) * rates)
        decays = [row_of(decay, mode) for mode in range(modes)]
        held = [jnp.zeros((SUB, LANE), F32)] * modes
        for at in range(0, tok, 2 * SUB):
            pair = values_ref[at : at + 2 * SUB, lanes].astype(F32)
            for half in (pair[:SUB], pair[SUB:]):
                held = [decays[mode] * held[mode] + half for mode in range(modes)]
        rows = [
            jnp.sum(held[mode] * jnp.exp(-row_of(rates, mode) * left), axis=0, keepdims=True)
            for mode in range(modes)
        ]
        state = jnp.concatenate(rows, axis=0).astype(BF16)
        for shard in range(wire_ref.shape[0]):
            wire_ref[shard, :, lanes] = state


def local_kernel(
    values_hbm, rates_hbm, residues_hbm, skip_hbm, gate_hbm, weight_hbm,
    near_ref, reach_ref, decay_ref, far_ref, gate_ref, first_weight, kept_weight,
    values_ref, rates_ref, residues_ref, skip_ref, wide_ref, taps_ref, first_ref, snap_ref,
    order_ref, sems, weight_sems,
):
    tok, chan = values_ref.shape
    modes = rates_ref.shape[0]
    run = tok // SUB
    copies = [
        pltpu.make_async_copy(source, target, sems.at[at])
        for at, (source, target) in enumerate(
            (
                (values_hbm, values_ref),
                (rates_hbm, rates_ref),
                (residues_hbm, residues_ref),
                (skip_hbm, skip_ref),
                (gate_hbm, gate_ref),
            )
        )
    ]
    for copy in copies:
        copy.start()
    slots = range(1, lax.axis_size("tp") // 2)
    rest = column_copies(1, 0, slots, weight_hbm, first_weight, weight_sems.at[0])
    rest += column_copies(0, 0, slots, weight_hbm, kept_weight, weight_sems.at[1])
    rest.append(copies.pop())
    table = spread_table(tok)
    wait_all(copies)
    wide_ref[...] = jnp.dot(table, values_ref[...], preferred_element_type=F32)

    def step(index, carry):
        lanes = lanes_at(index)
        place = sublane()
        rates = rates_ref[:, lanes]
        gains = gains_of(residues_ref[:, lanes], rates)

        ahead = place.astype(F32)
        decay, decay_block = jnp.exp(-rates), jnp.exp(-float(SUB) * rates)
        decay_run = jnp.exp(-float(run) * rates)
        decays = [row_of(decay, mode) for mode in range(modes)]
        taps = jnp.where(place == 0, skip_ref[:, lanes], 0.0)
        for mode in range(modes):
            gain = row_of(gains, mode)
            term = gain * jnp.exp(-row_of(rates, mode) * ahead)
            taps = taps + term
            first_ref[mode * SUB : (mode + 1) * SUB, :] = gain * decays[mode]
            reach_ref[mode * SUB : (mode + 1) * SUB, lanes] = term * decays[mode]
        taps_ref[...] = taps

        held = [jnp.zeros((SUB, LANE), F32)] * modes
        for at in range(run):
            if at % SUB == 0:
                for mode in range(modes):
                    snap_ref[at // SUB, mode * SUB : (mode + 1) * SUB, :] = held[mode]
            value = wide_ref[at * SUB : (at + 1) * SUB, lanes]
            held = [decays[mode] * held[mode] + value for mode in range(modes)]
        for mode in range(modes):
            whole, power = held[mode], row_of(decay_run, mode)
            for shift in (1, 2, 4):
                moved = jnp.where(place >= shift, pltpu.roll(whole, shift, 0), 0.0)
                whole = whole + power * moved
                power = power * power
            before = jnp.where(place >= 1, pltpu.roll(whole, 1, 0), 0.0)
            rows = slice(mode * SUB, (mode + 1) * SUB)
            fade = row_of(decay_block, mode)
            for block in range(run // SUB):
                snap_ref[block, rows, :] = first_ref[rows, :] * (snap_ref[block, rows, :] + before)
                before = fade * before

        for block in range(run // SUB):
            values = [
                wide_ref[(block * SUB + at) * SUB : (block * SUB + at + 1) * SUB, lanes]
                for at in range(SUB)
            ]
            sums = [jnp.zeros((SUB, LANE), F32)] * SUB
            for lag in range(SUB):
                tap = jnp.broadcast_to(taps_ref[lag : lag + 1, :], (SUB, LANE))
                for at in range(lag, SUB):
                    sums[at] = sums[at] + tap * values[at - lag]
            terms = [
                snap_ref[block, mode * SUB : (mode + 1) * SUB, :] for mode in range(modes)
            ]
            for at in range(SUB):
                total = sums[at]
                for mode in range(modes):
                    total = total + terms[mode]
                terms = [terms[mode] * decays[mode] for mode in range(modes)]
                order_ref[pl.ds(block * SUB + at, SUB, stride=run), :] = total
        near_ref[:, lanes] = order_ref[...]
        decay_ref[:, lanes] = jnp.exp(-float(SUB) * rates)
        far_ref[:, lanes] = jnp.exp(-float(tok) * rates)
        return carry

    lax.fori_loop(0, chan // LANE, step, 0)
    wait_all(rest)


def gate_kernel(
    states_ref, near_ref, reach_ref, decay_ref, far_ref, gate_ref, weight_ref, weight_hbm,
    gated_ref, sent_ref, later_weight, last_weight, state_ref, sems,
):
    slots = range(1, lax.axis_size("tp") // 2)
    begin = weight_ref.shape[1] // len(slots)
    rest = column_copies(1, begin, slots, weight_hbm, later_weight, sems.at[0])
    rest += column_copies(0, begin, slots, weight_hbm, last_weight, sems.at[1])
    tok, chan = gate_ref.shape
    shards, modes = states_ref.shape[:2]
    place = lax.axis_index("seq")
    far = far_ref[...]
    before = jnp.zeros((modes, chan), F32)
    order = group_order(shards)
    for shard in range(shards - 1):
        passed = far * before + states_ref[order.index(shard)].astype(F32)
        before = jnp.where(shard < place, passed, before)
    state_ref[...] = before

    def step(index, carry):
        lanes = lanes_at(index)
        decays, terms = [], []
        for mode in range(modes):
            rows, row = slice(mode * SUB, (mode + 1) * SUB), slice(mode, mode + 1)
            decays.append(jnp.broadcast_to(decay_ref[row, lanes], (SUB, LANE)))
            state = jnp.broadcast_to(state_ref[row, lanes], (SUB, LANE))
            terms.append(state * reach_ref[rows, lanes])
        for at in range(0, tok, 2 * SUB):
            totals = []
            for first in (at, at + SUB):
                total = near_ref[first : first + SUB, lanes]
                for mode in range(modes):
                    total = total + terms[mode]
                terms = [terms[mode] * decays[mode] for mode in range(modes)]
                totals.append(total)
            rows = slice(at, at + 2 * SUB)
            gate = gate_ref[rows, lanes].astype(F32)
            gated_ref[rows, lanes] = (gate * jnp.concatenate(totals, axis=0)).astype(BF16)
        return carry

    lax.fori_loop(0, chan // LANE, step, 0)
    project(gated_ref, weight_ref, sent_ref)
    wait_all(rest)


def project(left_ref, right_ref, out_ref):
    total = out_ref.shape[1]
    tile = 2 * LANE if total % (2 * LANE) == 0 else LANE
    for first in range(0, total, tile):
        lanes = slice(first, first + tile)
        out_ref[:, lanes] = jnp.dot(
            left_ref[...], right_ref[:, lanes], preferred_element_type=F32
        ).astype(out_ref.dtype)


def product(gated_ref, weight):
    return jnp.dot(gated_ref[...], weight, preferred_element_type=F32)


def middle_kernel(gated_ref, kept_weight, sent_weight, kept_ref, sent_ref):
    project(gated_ref, kept_weight, kept_ref)
    project(gated_ref, sent_weight, sent_ref)


def join_kernel(kept_ref, moved_ref, *going_refs):
    wide = going_refs[0].shape[1]
    for at, going_ref in enumerate(going_refs):
        lanes = slice(at * wide, (at + 1) * wide)
        going_ref[...] = (kept_ref[:, lanes] + moved_ref[:, lanes].astype(F32)).astype(BF16)


def going_kernel(gated_ref, weight_ref, moved_ref, after_ref, *going_refs):
    wide = going_refs[0].shape[1]
    for at, going_ref in enumerate(going_refs):
        lanes = slice(at * wide, (at + 1) * wide)
        total = product(gated_ref, weight_ref[:, lanes])
        going_ref[...] = (total + moved_ref[:, lanes].astype(F32)).astype(BF16)


def late_kernel(gated_ref, weight_hbm, *refs):
    (low_ref, high_ref, weight_ref, sems) = refs[-4:]
    half = low_ref.shape[1]
    wait_all(column_copies(1, 0, range(1), weight_hbm, weight_ref, sems))
    low_ref[...] = product(gated_ref, weight_ref[:, :half]).astype(BF16)
    high_ref[...] = product(gated_ref, weight_ref[:, half:]).astype(BF16)


def own_kernel(gated_ref, weight_hbm, low_ref, high_ref, *refs):
    others, (first_ref, own_ref, weight_ref, sems) = refs[:-4], refs[-4:]
    narrow, half = first_ref.shape[1], low_ref.shape[1]
    wait_all(column_copies(0, 0, range(1), weight_hbm, weight_ref, sems))
    total = low_ref[:, :narrow].astype(F32) + product(gated_ref, weight_ref[:, :narrow])
    for other in others:
        total = total + other[...].astype(F32)
    first_ref[...] = total.astype(BF16)
    own_ref[:, : half - narrow] = low_ref[:, narrow:].astype(F32) + product(
        gated_ref, weight_ref[:, narrow:half]
    )
    own_ref[:, half - narrow :] = high_ref[...].astype(F32) + product(
        gated_ref, weight_ref[:, half:]
    )


def final_kernel(first_ref, own_ref, *refs):
    others, (out_hbm, wide_ref, sems) = refs[:-3], refs[-3:]
    tok, narrow = first_ref.shape
    count = sems.shape[0] - 1
    copies = [
        pltpu.make_async_copy(first_ref, out_hbm.at[:, pl.ds(0, narrow)], sems.at[count])
    ]
    copies[0].start()
    for part in range(count):
        rows = pl.ds(part * tok // count, tok // count)
        total = own_ref[rows, :]
        for other in others:
            total = total + other[rows, :].astype(F32)
        wide_ref[rows, :] = total.astype(BF16)
        columns = pl.ds(narrow, wide_ref.shape[1])
        copies.append(
            pltpu.make_async_copy(wide_ref.at[rows], out_hbm.at[rows, columns], sems.at[part])
        )
        copies[-1].start()
    wait_all(copies)


def call(kernel, outs, *operands, scratch=(), macs=0, out_spec=VMEM):
    specs, arrays = [], []
    for operand in operands:
        spec, array = operand if isinstance(operand, tuple) else (VMEM, operand)
        specs.append(ANY if spec is HBM else spec)
        arrays.append(in_hbm(array) if spec is HBM else array)
    return pl.pallas_call(
        kernel,
        out_shape=outs,
        in_specs=specs,
        out_specs=[out_spec] * len(outs),
        scratch_shapes=scratch,
        compiler_params=PARAMS,
        cost_estimate=pl.CostEstimate(flops=2 * macs, bytes_accessed=0, transcendentals=0),
    )(*arrays)


def body(values, gate, residues, rates, skip, out_weight):
    shards, tp = lax.axis_size("seq"), lax.axis_size("tp")
    tok, chan = values.shape
    modes = rates.shape[0]
    chips = tp // 2
    away = chips - 1
    block = out_weight.shape[1] // tp
    here = pltpu.VMEM
    parts = 4 if chan % (4 * LANE) == 0 else 1
    cores = [(rank, rank ^ 1) for rank in range(tp)]
    sources = [(HBM, each) for each in (values, rates, residues, skip.reshape(1, chan), gate)]
    (wire,) = call(
        state_kernel,
        [jax.ShapeDtypeStruct((shards, modes, chan), BF16)],
        *sources[:2],
        scratch=[
            here((tok, chan), BF16),
            here((modes, chan), F32),
            pltpu.SemaphoreType.DMA((parts + 1,)),
        ],
    )
    states = lax.all_to_all(
        wire, "seq", split_axis=0, concat_axis=0, tiled=True,
        axis_index_groups=[group_order(shards)],
    )
    narrow = max(LANE, block // 4)
    wide = block - narrow
    weight = (HBM, out_weight)
    *tables, first_weight, kept_weight = call(
        local_kernel,
        [
            here((tok, chan), F32),
            here((modes * SUB, chan), F32),
            here((modes, chan), F32),
            here((modes, chan), F32),
            here((tok, chan), BF16),
            here((chan, away * narrow), BF16),
            here((chan, away * narrow), BF16),
        ],
        *sources, weight,
        scratch=[
            here((tok, chan), BF16),
            here((modes, chan), F32),
            here((modes, chan), F32),
            here((1, chan), F32),
            here((tok, chan), F32),
            here((SUB, LANE), F32),
            here((modes * SUB, LANE), F32),
            here((tok // SUB // SUB, modes * SUB, LANE), F32),
            here((tok, LANE), F32),
            pltpu.SemaphoreType.DMA((len(sources),)),
            pltpu.SemaphoreType.DMA((2, away * ROW_CUTS)),
        ],
    )

    gated, sent, sent_weight, last_weight = call(
        gate_kernel,
        [
            here((tok, chan), BF16),
            here((tok, away * narrow), BF16),
            here((chan, away * wide), BF16),
            here((chan, away * wide), BF16),
        ],
        states, *tables, first_weight, weight,
        scratch=[
            here((modes, chan), F32),
            pltpu.SemaphoreType.DMA((2, away * ROW_CUTS)),
        ],
    )
    moved_first = lax.ppermute(sent, "tp", cores)
    kept, sent = call(
        middle_kernel,
        [here((tok, away * narrow), F32), here((tok, away * wide), BF16)],
        gated, kept_weight, sent_weight,
    )
    moved = lax.ppermute(sent, "tp", cores)

    def to_chips(going):
        return [
            lax.ppermute(each, "tp", [(rank, (rank + 2 * hop) % tp) for rank in reversed(range(tp))])
            for hop, each in enumerate(going, 1)
        ]

    hint = 16 * tok * chan * block
    going = call(join_kernel, [here((tok, narrow), BF16)] * away, kept, moved_first, macs=hint)
    first = to_chips(going)
    going = call(
        going_kernel, [here((tok, wide), BF16)] * away,
        gated, last_weight, moved, (ANY, going[-1]),
    )
    second = to_chips(going)
    late = [here((chan, block), BF16), pltpu.SemaphoreType.DMA((ROW_CUTS,))]
    halves = call(
        late_kernel, [here((tok, block // 2), BF16)] * 2,
        gated, weight, (ANY, going[-1]), (ANY, first[-1]), scratch=late, macs=hint,
    )
    halves = [lax.ppermute(each, "tp", cores) for each in halves]
    done, own = call(
        own_kernel, [here((tok, narrow), BF16), here((tok, wide), F32)],
        gated, weight, *halves, *first, scratch=late,
    )
    (out,) = call(
        final_kernel, [jax.ShapeDtypeStruct((tok, block), BF16)], done, own, *second,
        scratch=[here((tok, wide), BF16), pltpu.SemaphoreType.DMA((3,))],
        out_spec=ANY,
    )
    return out


def solution(mesh):
    placed = (P("seq", "tp"), P("seq", "tp"), P(None, "tp"), P(None, "tp"), P("tp"), P("tp", None))
    return jax.shard_map(
        body, mesh=mesh, in_specs=placed, out_specs=P("seq", "tp"), check_vma=False
    )
```

```python
from functools import partial

import jax
import jax.numpy as jnp
from jax import lax
from jax.experimental import pallas as pl
from jax.experimental.pallas import tpu as pltpu
from jax.sharding import PartitionSpec as P

SUB, LANE = 8, 128
F32, BF16 = jnp.float32, jnp.bfloat16

VMEM = pl.BlockSpec(memory_space=pltpu.VMEM)
ANY = pl.BlockSpec(memory_space=pl.ANY)
HBM = "hbm"
PARAMS = pltpu.CompilerParams(vmem_limit_bytes=24 * 2**20)


def in_hbm(array):
    return pltpu.with_memory_space_constraint(array, pltpu.HBM)


def in_vmem(array):
    return pltpu.with_memory_space_constraint(array, pltpu.VMEM)


def row_of(block, mode):
    return jnp.broadcast_to(block[mode : mode + 1, :], (SUB, LANE))


def sublane():
    return lax.broadcasted_iota(jnp.int32, (SUB, LANE), 0)


def lanes_at(step):
    return pl.ds(pl.multiple_of(step * LANE, LANE), LANE)


def gains_of(residues, rates):
    return residues * jnp.sqrt(2.0 * rates)


def spread_table(tok):
    run = tok // SUB
    row = lax.broadcasted_iota(jnp.int32, (tok, tok), 0)
    col = lax.broadcasted_iota(jnp.int32, (tok, tok), 1)
    return (col == row % SUB * run + row // SUB).astype(F32).astype(BF16)


ROW_CUTS = 4


def column_copies(other, begin, slots, weight_hbm, out_ref, sems):
    rank = lax.axis_index("tp")
    chips = lax.axis_size("tp") // 2
    block = weight_hbm.shape[1] // (2 * chips)
    wide = out_ref.shape[1] // len(slots)
    tall = out_ref.shape[0] // ROW_CUTS
    core = 1 - rank % 2 if other else rank % 2
    copies = []
    for at, slot in enumerate(slots):
        owner = (rank // 2 + slot) % chips * 2 + core
        columns = pl.ds(pl.multiple_of(owner * block + begin, LANE), wide)
        for cut in range(ROW_CUTS):
            rows = pl.ds(cut * tall, tall)
            copies.append(
                pltpu.make_async_copy(
                    weight_hbm.at[rows, columns],
                    out_ref.at[rows, pl.ds(at * wide, wide)],
                    sems.at[at * ROW_CUTS + cut],
                )
            )
            copies[-1].start()
    return copies


def group_order(count):
    return [(count // 2 + at) % count for at in range(count)]


def wait_all(copies):
    for copy in copies:
        copy.wait()


def state_kernel(values_hbm, rates_hbm, wire_ref, values_ref, rates_ref, sems):
    tok, chan = values_ref.shape
    modes = rates_ref.shape[0]
    parts = sems.shape[0] - 1
    width = chan // parts
    first = pltpu.make_async_copy(rates_hbm, rates_ref, sems.at[parts])
    first.start()
    pieces = []
    for part in range(parts):
        lanes = pl.ds(part * width, width)
        pieces.append(
            pltpu.make_async_copy(
                values_hbm.at[:, lanes], values_ref.at[:, lanes], sems.at[part]
            )
        )
        pieces[-1].start()
    left = (SUB - 1 - sublane()).astype(F32)
    first.wait()
    for index in range(chan // LANE):
        if index * LANE % width == 0:
            pieces[index * LANE // width].wait()
        lanes = slice(index * LANE, (index + 1) * LANE)
        rates = rates_ref[:, lanes]
        decay = jnp.exp(-float(SUB) * rates)
        decays = [row_of(decay, mode) for mode in range(modes)]
        held = [jnp.zeros((SUB, LANE), F32)] * modes
        for at in range(0, tok, 2 * SUB):
            pair = values_ref[at : at + 2 * SUB, lanes].astype(F32)
            for half in (pair[:SUB], pair[SUB:]):
                held = [decays[mode] * held[mode] + half for mode in range(modes)]
        rows = [
            jnp.sum(held[mode] * jnp.exp(-row_of(rates, mode) * left), axis=0, keepdims=True)
            for mode in range(modes)
        ]
        state = jnp.concatenate(rows, axis=0).astype(BF16)
        for shard in range(wire_ref.shape[0]):
            wire_ref[shard, :, lanes] = state


def local_kernel(
    values_hbm, rates_hbm, residues_hbm, skip_hbm, gate_hbm, weight_hbm,
    near_ref, reach_ref, decay_ref, far_ref, gate_ref, first_weight, kept_weight,
    sent_weight, last_weight,
    values_ref, rates_ref, residues_ref, skip_ref, wide_ref, taps_ref, first_ref, snap_ref,
    order_ref, sent_held, last_held, sems, weight_sems, out_sems,
):
    tok, chan = values_ref.shape
    modes = rates_ref.shape[0]
    run = tok // SUB
    copies = [
        pltpu.make_async_copy(source, target, sems.at[at])
        for at, (source, target) in enumerate(
            (
                (values_hbm, values_ref),
                (rates_hbm, rates_ref),
                (residues_hbm, residues_ref),
                (skip_hbm, skip_ref),
                (gate_hbm, gate_ref),
            )
        )
    ]
    for copy in copies:
        copy.start()
    slots = range(1, lax.axis_size("tp") // 2)
    rest = column_copies(1, 0, slots, weight_hbm, first_weight, weight_sems.at[0])
    rest += column_copies(0, 0, slots, weight_hbm, kept_weight, weight_sems.at[1])
    begin = kept_weight.shape[1] // len(slots)
    passing = column_copies(1, begin, slots, weight_hbm, sent_held, weight_sems.at[2])
    passing += column_copies(0, begin, slots, weight_hbm, last_held, weight_sems.at[3])
    rest.append(copies.pop())
    table = spread_table(tok)
    wait_all(copies)
    wide_ref[...] = jnp.dot(table, values_ref[...], preferred_element_type=F32)

    def step(index, carry):
        lanes = lanes_at(index)
        place = sublane()
        rates = rates_ref[:, lanes]
        gains = gains_of(residues_ref[:, lanes], rates)

        ahead = place.astype(F32)
        decay, decay_block = jnp.exp(-rates), jnp.exp(-float(SUB) * rates)
        decay_run = jnp.exp(-float(run) * rates)
        decays = [row_of(decay, mode) for mode in range(modes)]
        taps = jnp.where(place == 0, skip_ref[:, lanes], 0.0)
        for mode in range(modes):
            gain = row_of(gains, mode)
            term = gain * jnp.exp(-row_of(rates, mode) * ahead)
            taps = taps + term
            first_ref[mode * SUB : (mode + 1) * SUB, :] = gain * decays[mode]
            reach_ref[mode * SUB : (mode + 1) * SUB, lanes] = term * decays[mode]
        taps_ref[...] = taps

        held = [jnp.zeros((SUB, LANE), F32)] * modes
        for at in range(run):
            if at % SUB == 0:
                for mode in range(modes):
                    snap_ref[at // SUB, mode * SUB : (mode + 1) * SUB, :] = held[mode]
            value = wide_ref[at * SUB : (at + 1) * SUB, lanes]
            held = [decays[mode] * held[mode] + value for mode in range(modes)]
        for mode in range(modes):
            whole, power = held[mode], row_of(decay_run, mode)
            for shift in (1, 2, 4):
                moved = jnp.where(place >= shift, pltpu.roll(whole, shift, 0), 0.0)
                whole = whole + power * moved
                power = power * power
            before = jnp.where(place >= 1, pltpu.roll(whole, 1, 0), 0.0)
            rows = slice(mode * SUB, (mode + 1) * SUB)
            fade = row_of(decay_block, mode)
            for block in range(run // SUB):
                snap_ref[block, rows, :] = first_ref[rows, :] * (snap_ref[block, rows, :] + before)
                before = fade * before

        for block in range(run // SUB):
            values = [
                wide_ref[(block * SUB + at) * SUB : (block * SUB + at + 1) * SUB, lanes]
                for at in range(SUB)
            ]
            sums = [jnp.zeros((SUB, LANE), F32)] * SUB
            for lag in range(SUB):
                tap = jnp.broadcast_to(taps_ref[lag : lag + 1, :], (SUB, LANE))
                for at in range(lag, SUB):
                    sums[at] = sums[at] + tap * values[at - lag]
            terms = [
                snap_ref[block, mode * SUB : (mode + 1) * SUB, :] for mode in range(modes)
            ]
            for at in range(SUB):
                total = sums[at]
                for mode in range(modes):
                    total = total + terms[mode]
                terms = [terms[mode] * decays[mode] for mode in range(modes)]
                order_ref[pl.ds(block * SUB + at, SUB, stride=run), :] = total
        near_ref[:, lanes] = order_ref[...]
        decay_ref[:, lanes] = jnp.exp(-float(SUB) * rates)
        far_ref[:, lanes] = jnp.exp(-float(tok) * rates)
        return carry

    steps = chan // LANE
    lax.fori_loop(0, steps // 2, step, 0)
    wait_all(passing)
    for at, (held, target) in enumerate(((sent_held, sent_weight), (last_held, last_weight))):
        rest.append(pltpu.make_async_copy(held, target, out_sems.at[at]))
        rest[-1].start()
    lax.fori_loop(steps // 2, steps, step, 0)
    wait_all(rest)


def gate_kernel(
    states_ref, near_ref, reach_ref, decay_ref, far_ref, gate_ref, weight_ref,
    gated_ref, sent_ref, state_ref,
):
    tok, chan = gate_ref.shape
    shards, modes = states_ref.shape[:2]
    place = lax.axis_index("seq")
    far = far_ref[...]
    before = jnp.zeros((modes, chan), F32)
    order = group_order(shards)
    for shard in range(shards - 1):
        passed = far * before + states_ref[order.index(shard)].astype(F32)
        before = jnp.where(shard < place, passed, before)
    state_ref[...] = before

    def step(index, carry):
        lanes = lanes_at(index)
        decays, terms = [], []
        for mode in range(modes):
            rows, row = slice(mode * SUB, (mode + 1) * SUB), slice(mode, mode + 1)
            decays.append(jnp.broadcast_to(decay_ref[row, lanes], (SUB, LANE)))
            state = jnp.broadcast_to(state_ref[row, lanes], (SUB, LANE))
            terms.append(state * reach_ref[rows, lanes])
        for at in range(0, tok, 2 * SUB):
            totals = []
            for first in (at, at + SUB):
                total = near_ref[first : first + SUB, lanes]
                for mode in range(modes):
                    total = total + terms[mode]
                terms = [terms[mode] * decays[mode] for mode in range(modes)]
                totals.append(total)
            rows = slice(at, at + 2 * SUB)
            gate = gate_ref[rows, lanes].astype(F32)
            gated_ref[rows, lanes] = (gate * jnp.concatenate(totals, axis=0)).astype(BF16)
        return carry

    lax.fori_loop(0, chan // LANE, step, 0)
    project(gated_ref, weight_ref, sent_ref)


def project(left_ref, right_ref, out_ref):
    total = out_ref.shape[1]
    tile = 2 * LANE if total % (2 * LANE) == 0 else LANE
    for first in range(0, total, tile):
        lanes = slice(first, first + tile)
        out_ref[:, lanes] = jnp.dot(
            left_ref[...], right_ref[:, lanes], preferred_element_type=F32
        ).astype(out_ref.dtype)


def product(gated_ref, weight):
    return jnp.dot(gated_ref[...], weight, preferred_element_type=F32)


def middle_kernel(gated_ref, kept_weight, sent_weight, kept_ref, sent_ref):
    project(gated_ref, kept_weight, kept_ref)
    project(gated_ref, sent_weight, sent_ref)


def join_kernel(kept_ref, moved_ref, *going_refs):
    wide = going_refs[0].shape[1]
    for at, going_ref in enumerate(going_refs):
        lanes = slice(at * wide, (at + 1) * wide)
        going_ref[...] = (kept_ref[:, lanes] + moved_ref[:, lanes].astype(F32)).astype(BF16)


def going_kernel(gated_ref, weight_ref, moved_ref, after_ref, *going_refs):
    wide = going_refs[0].shape[1]
    for at, going_ref in enumerate(going_refs):
        lanes = slice(at * wide, (at + 1) * wide)
        total = product(gated_ref, weight_ref[:, lanes])
        going_ref[...] = (total + moved_ref[:, lanes].astype(F32)).astype(BF16)


def late_kernel(gated_ref, weight_hbm, *refs):
    (low_ref, high_ref, weight_ref, sems) = refs[-4:]
    half = low_ref.shape[1]
    wait_all(column_copies(1, 0, range(1), weight_hbm, weight_ref, sems))
    low_ref[...] = product(gated_ref, weight_ref[:, :half]).astype(BF16)
    high_ref[...] = product(gated_ref, weight_ref[:, half:]).astype(BF16)


def own_kernel(gated_ref, weight_hbm, low_ref, high_ref, *refs):
    others, (first_ref, own_ref, weight_ref, sems) = refs[:-4], refs[-4:]
    narrow, half = first_ref.shape[1], low_ref.shape[1]
    wait_all(column_copies(0, 0, range(1), weight_hbm, weight_ref, sems))
    total = low_ref[:, :narrow].astype(F32) + product(gated_ref, weight_ref[:, :narrow])
    for other in others:
        total = total + other[...].astype(F32)
    first_ref[...] = total.astype(BF16)
    own_ref[:, : half - narrow] = low_ref[:, narrow:].astype(F32) + product(
        gated_ref, weight_ref[:, narrow:half]
    )
    own_ref[:, half - narrow :] = high_ref[...].astype(F32) + product(
        gated_ref, weight_ref[:, half:]
    )


def final_kernel(first_ref, own_ref, *refs):
    others, (out_hbm, wide_ref, sems) = refs[:-3], refs[-3:]
    tok, narrow = first_ref.shape
    count = sems.shape[0] - 1
    copies = [
        pltpu.make_async_copy(first_ref, out_hbm.at[:, pl.ds(0, narrow)], sems.at[count])
    ]
    copies[0].start()
    for part in range(count):
        rows = pl.ds(part * tok // count, tok // count)
        total = own_ref[rows, :]
        for other in others:
            total = total + other[rows, :].astype(F32)
        wide_ref[rows, :] = total.astype(BF16)
        columns = pl.ds(narrow, wide_ref.shape[1])
        copies.append(
            pltpu.make_async_copy(wide_ref.at[rows], out_hbm.at[rows, columns], sems.at[part])
        )
        copies[-1].start()
    wait_all(copies)


def call(kernel, outs, *operands, scratch=(), macs=0, out_spec=VMEM, in_place=0):
    specs, arrays = [], []
    for operand in operands:
        spec, array = operand if isinstance(operand, tuple) else (VMEM, operand)
        specs.append(ANY if spec is HBM else spec)
        arrays.append(in_hbm(array) if spec is HBM else array)
    return pl.pallas_call(
        kernel,
        out_shape=outs,
        in_specs=specs,
        out_specs=[out_spec] * (len(outs) - in_place) + [ANY] * in_place,
        scratch_shapes=scratch,
        compiler_params=PARAMS,
        cost_estimate=pl.CostEstimate(flops=2 * macs, bytes_accessed=0, transcendentals=0),
    )(*arrays)


def body(values, gate, residues, rates, skip, out_weight):
    shards, tp = lax.axis_size("seq"), lax.axis_size("tp")
    tok, chan = values.shape
    modes = rates.shape[0]
    chips = tp // 2
    away = chips - 1
    block = out_weight.shape[1] // tp
    here = pltpu.VMEM
    parts = 4 if chan % (4 * LANE) == 0 else 1
    cores = [(rank, rank ^ 1) for rank in range(tp)]
    sources = [(HBM, each) for each in (values, rates, residues, skip.reshape(1, chan), gate)]
    (wire,) = call(
        state_kernel,
        [jax.ShapeDtypeStruct((shards, modes, chan), BF16)],
        *sources[:2],
        scratch=[
            here((tok, chan), BF16),
            here((modes, chan), F32),
            pltpu.SemaphoreType.DMA((parts + 1,)),
        ],
    )
    states = lax.all_to_all(
        wire, "seq", split_axis=0, concat_axis=0, tiled=True,
        axis_index_groups=[group_order(shards)],
    )
    narrow = max(LANE, block // 4)
    wide = block - narrow
    weight = (HBM, out_weight)
    *tables, first_weight, kept_weight, sent_weight, last_weight = call(
        local_kernel,
        [
            here((tok, chan), F32),
            here((modes * SUB, chan), F32),
            here((modes, chan), F32),
            here((modes, chan), F32),
            here((tok, chan), BF16),
            here((chan, away * narrow), BF16),
            here((chan, away * narrow), BF16),
            pltpu.HBM((chan, away * wide), BF16),
            pltpu.HBM((chan, away * wide), BF16),
        ],
        *sources, weight,
        in_place=2,
        scratch=[
            here((tok, chan), BF16),
            here((modes, chan), F32),
            here((modes, chan), F32),
            here((1, chan), F32),
            here((tok, chan), F32),
            here((SUB, LANE), F32),
            here((modes * SUB, LANE), F32),
            here((tok // SUB // SUB, modes * SUB, LANE), F32),
            here((tok, LANE), F32),
            here((chan, away * wide), BF16),
            here((chan, away * wide), BF16),
            pltpu.SemaphoreType.DMA((len(sources),)),
            pltpu.SemaphoreType.DMA((4, away * ROW_CUTS)),
            pltpu.SemaphoreType.DMA((2,)),
        ],
    )

    hint = 16 * tok * chan * block
    gated, sent = call(
        gate_kernel,
        [here((tok, chan), BF16), here((tok, away * narrow), BF16)],
        states, *tables, first_weight,
        scratch=[here((modes, chan), F32)], macs=hint,
    )
    moved_first = lax.ppermute(sent, "tp", cores)
    kept, sent = call(
        middle_kernel,
        [here((tok, away * narrow), F32), here((tok, away * wide), BF16)],
        gated, kept_weight, sent_weight,
    )
    moved = lax.ppermute(sent, "tp", cores)

    def to_chips(going):
        return [
            lax.ppermute(each, "tp", [(rank, (rank + 2 * hop) % tp) for rank in reversed(range(tp))])
            for hop, each in enumerate(going, 1)
        ]

    going = call(join_kernel, [here((tok, narrow), BF16)] * away, kept, moved_first, macs=hint)
    first = to_chips(going)
    going = call(
        going_kernel, [here((tok, wide), BF16)] * away,
        gated, last_weight, moved, (ANY, going[-1]),
    )
    second = to_chips(going)
    late = [here((chan, block), BF16), pltpu.SemaphoreType.DMA((ROW_CUTS,))]
    halves = call(
        late_kernel, [here((tok, block // 2), BF16)] * 2,
        gated, weight, (ANY, going[-1]), (ANY, first[-1]), scratch=late, macs=hint,
    )
    halves = [lax.ppermute(each, "tp", cores) for each in halves]
    done, own = call(
        own_kernel, [here((tok, narrow), BF16), here((tok, wide), F32)],
        gated, weight, *halves, *first, scratch=late,
    )
    (out,) = call(
        final_kernel, [jax.ShapeDtypeStruct((tok, block), BF16)], done, own, *second,
        scratch=[here((tok, wide), BF16), pltpu.SemaphoreType.DMA((3,))],
        out_spec=ANY,
    )
    return out


def solution(mesh):
    placed = (P("seq", "tp"), P("seq", "tp"), P(None, "tp"), P(None, "tp"), P("tp"), P("tp", None))
    return jax.shard_map(
        body, mesh=mesh, in_specs=placed, out_specs=P("seq", "tp"), check_vma=False
    )
```

```python
from functools import partial

import jax
import jax.numpy as jnp
from jax import lax
from jax.experimental import pallas as pl
from jax.experimental.pallas import tpu as pltpu
from jax.sharding import PartitionSpec as P

SUB, LANE = 8, 128
F32, BF16 = jnp.float32, jnp.bfloat16

VMEM = pl.BlockSpec(memory_space=pltpu.VMEM)
ANY = pl.BlockSpec(memory_space=pl.ANY)
HBM = "hbm"
PARAMS = pltpu.CompilerParams(vmem_limit_bytes=24 * 2**20)


def in_hbm(array):
    return pltpu.with_memory_space_constraint(array, pltpu.HBM)


def in_vmem(array):
    return pltpu.with_memory_space_constraint(array, pltpu.VMEM)


def row_of(block, mode):
    return jnp.broadcast_to(block[mode : mode + 1, :], (SUB, LANE))


def sublane():
    return lax.broadcasted_iota(jnp.int32, (SUB, LANE), 0)


def lanes_at(step):
    return pl.ds(pl.multiple_of(step * LANE, LANE), LANE)


def gains_of(residues, rates):
    return residues * jnp.sqrt(2.0 * rates)


def spread_table(tok):
    run = tok // SUB
    row = lax.broadcasted_iota(jnp.int32, (tok, tok), 0)
    col = lax.broadcasted_iota(jnp.int32, (tok, tok), 1)
    return (col == row % SUB * run + row // SUB).astype(F32).astype(BF16)


ROW_CUTS = 4


def column_copies(other, begin, slots, weight_hbm, out_ref, sems):
    rank = lax.axis_index("tp")
    chips = lax.axis_size("tp") // 2
    block = weight_hbm.shape[1] // (2 * chips)
    wide = out_ref.shape[1] // len(slots)
    tall = out_ref.shape[0] // ROW_CUTS
    core = 1 - rank % 2 if other else rank % 2
    copies = []
    for at, slot in enumerate(slots):
        owner = (rank // 2 + slot) % chips * 2 + core
        columns = pl.ds(pl.multiple_of(owner * block + begin, LANE), wide)
        for cut in range(ROW_CUTS):
            rows = pl.ds(cut * tall, tall)
            copies.append(
                pltpu.make_async_copy(
                    weight_hbm.at[rows, columns],
                    out_ref.at[rows, pl.ds(at * wide, wide)],
                    sems.at[at * ROW_CUTS + cut],
                )
            )
            copies[-1].start()
    return copies


def group_order(count):
    return [(count // 2 + at) % count for at in range(count)]


def wait_all(copies):
    for copy in copies:
        copy.wait()


def state_kernel(values_hbm, rates_hbm, wire_ref, values_ref, rates_ref, sems):
    tok, chan = values_ref.shape
    modes = rates_ref.shape[0]
    parts = sems.shape[0] - 1
    width = chan // parts
    first = pltpu.make_async_copy(rates_hbm, rates_ref, sems.at[parts])
    first.start()
    pieces = []
    for part in range(parts):
        lanes = pl.ds(part * width, width)
        pieces.append(
            pltpu.make_async_copy(
                values_hbm.at[:, lanes], values_ref.at[:, lanes], sems.at[part]
            )
        )
        pieces[-1].start()
    left = (SUB - 1 - sublane()).astype(F32)
    first.wait()
    for index in range(chan // LANE):
        if index * LANE % width == 0:
            pieces[index * LANE // width].wait()
        lanes = slice(index * LANE, (index + 1) * LANE)
        rates = rates_ref[:, lanes]
        decay = jnp.exp(-float(SUB) * rates)
        decays = [row_of(decay, mode) for mode in range(modes)]
        held = [jnp.zeros((SUB, LANE), F32)] * modes
        for at in range(0, tok, 2 * SUB):
            pair = values_ref[at : at + 2 * SUB, lanes].astype(F32)
            for half in (pair[:SUB], pair[SUB:]):
                held = [decays[mode] * held[mode] + half for mode in range(modes)]
        rows = [
            jnp.sum(held[mode] * jnp.exp(-row_of(rates, mode) * left), axis=0, keepdims=True)
            for mode in range(modes)
        ]
        state = jnp.concatenate(rows, axis=0).astype(BF16)
        for shard in range(wire_ref.shape[0]):
            wire_ref[shard, :, lanes] = state


def local_kernel(
    values_hbm, rates_hbm, residues_hbm, skip_hbm, gate_hbm, weight_hbm,
    near_ref, reach_ref, decay_ref, far_ref, gate_ref, first_weight, kept_weight,
    sent_weight, last_weight,
    values_ref, rates_ref, residues_ref, skip_ref, wide_ref, taps_ref, first_ref, snap_ref,
    order_ref, sent_held, last_held, sems, weight_sems, out_sems,
):
    tok, chan = values_ref.shape
    modes = rates_ref.shape[0]
    run = tok // SUB
    copies = [
        pltpu.make_async_copy(source, target, sems.at[at])
        for at, (source, target) in enumerate(
            (
                (values_hbm, values_ref),
                (rates_hbm, rates_ref),
                (residues_hbm, residues_ref),
                (skip_hbm, skip_ref),
                (gate_hbm, gate_ref),
            )
        )
    ]
    for copy in copies:
        copy.start()
    slots = range(1, lax.axis_size("tp") // 2)
    rest = column_copies(1, 0, slots, weight_hbm, first_weight, weight_sems.at[0])
    rest += column_copies(0, 0, slots, weight_hbm, kept_weight, weight_sems.at[1])
    begin = kept_weight.shape[1] // len(slots)
    passing = column_copies(1, begin, slots, weight_hbm, sent_held, weight_sems.at[2])
    passing += column_copies(0, begin, slots, weight_hbm, last_held, weight_sems.at[3])
    rest.append(copies.pop())
    table = spread_table(tok)
    wait_all(copies)
    wide_ref[...] = jnp.dot(table, values_ref[...], preferred_element_type=F32)

    def step(index, carry):
        lanes = lanes_at(index)
        place = sublane()
        rates = rates_ref[:, lanes]
        gains = gains_of(residues_ref[:, lanes], rates)

        ahead = place.astype(F32)
        decay, decay_block = jnp.exp(-rates), jnp.exp(-float(SUB) * rates)
        decay_run = jnp.exp(-float(run) * rates)
        decays = [row_of(decay, mode) for mode in range(modes)]
        taps = jnp.where(place == 0, skip_ref[:, lanes], 0.0)
        for mode in range(modes):
            gain = row_of(gains, mode)
            term = gain * jnp.exp(-row_of(rates, mode) * ahead)
            taps = taps + term
            first_ref[mode * SUB : (mode + 1) * SUB, :] = gain * decays[mode]
            reach_ref[mode * SUB : (mode + 1) * SUB, lanes] = term * decays[mode]
        taps_ref[...] = taps

        held = [jnp.zeros((SUB, LANE), F32)] * modes
        for at in range(run):
            if at % SUB == 0:
                for mode in range(modes):
                    snap_ref[at // SUB, mode * SUB : (mode + 1) * SUB, :] = held[mode]
            value = wide_ref[at * SUB : (at + 1) * SUB, lanes]
            held = [decays[mode] * held[mode] + value for mode in range(modes)]
        for mode in range(modes):
            whole, power = held[mode], row_of(decay_run, mode)
            for shift in (1, 2, 4):
                moved = jnp.where(place >= shift, pltpu.roll(whole, shift, 0), 0.0)
                whole = whole + power * moved
                power = power * power
            before = jnp.where(place >= 1, pltpu.roll(whole, 1, 0), 0.0)
            rows = slice(mode * SUB, (mode + 1) * SUB)
            fade = row_of(decay_block, mode)
            for block in range(run // SUB):
                snap_ref[block, rows, :] = first_ref[rows, :] * (snap_ref[block, rows, :] + before)
                before = fade * before

        for block in range(run // SUB):
            values = [
                wide_ref[(block * SUB + at) * SUB : (block * SUB + at + 1) * SUB, lanes]
                for at in range(SUB)
            ]
            sums = [jnp.zeros((SUB, LANE), F32)] * SUB
            for lag in range(SUB):
                tap = jnp.broadcast_to(taps_ref[lag : lag + 1, :], (SUB, LANE))
                for at in range(lag, SUB):
                    sums[at] = sums[at] + tap * values[at - lag]
            terms = [
                snap_ref[block, mode * SUB : (mode + 1) * SUB, :] for mode in range(modes)
            ]
            for at in range(SUB):
                total = sums[at]
                for mode in range(modes):
                    total = total + terms[mode]
                terms = [terms[mode] * decays[mode] for mode in range(modes)]
                order_ref[pl.ds(block * SUB + at, SUB, stride=run), :] = total
        near_ref[:, lanes] = order_ref[...]
        decay_ref[:, lanes] = jnp.exp(-float(SUB) * rates)
        far_ref[:, lanes] = jnp.exp(-float(tok) * rates)
        return carry

    steps = chan // LANE
    lax.fori_loop(0, steps // 2, step, 0)
    wait_all(passing)
    for at, (held, target) in enumerate(((sent_held, sent_weight), (last_held, last_weight))):
        rest.append(pltpu.make_async_copy(held, target, out_sems.at[at]))
        rest[-1].start()
    lax.fori_loop(steps // 2, steps, step, 0)
    wait_all(rest)


def gate_kernel(
    states_ref, near_ref, reach_ref, decay_ref, far_ref, gate_ref, weight_ref,
    gated_ref, sent_ref, state_ref, total_ref,
):
    tok, chan = gate_ref.shape
    shards, modes = states_ref.shape[:2]
    place = lax.axis_index("seq")
    far = far_ref[...]
    before = jnp.zeros((modes, chan), F32)
    order = group_order(shards)
    for shard in range(shards - 1):
        passed = far * before + states_ref[order.index(shard)].astype(F32)
        before = jnp.where(shard < place, passed, before)
    state_ref[...] = before

    batch = 2 * LANE

    def carry_pass(index):
        lanes = lanes_at(index)
        decays, terms = [], []
        for mode in range(modes):
            rows, row = slice(mode * SUB, (mode + 1) * SUB), slice(mode, mode + 1)
            decays.append(jnp.broadcast_to(decay_ref[row, lanes], (SUB, LANE)))
            state = jnp.broadcast_to(state_ref[row, lanes], (SUB, LANE))
            terms.append(state * reach_ref[rows, lanes])
        for at in range(0, tok, 2 * SUB):
            totals = []
            for first in (at, at + SUB):
                total = near_ref[first : first + SUB, lanes]
                for mode in range(modes):
                    total = total + terms[mode]
                terms = [terms[mode] * decays[mode] for mode in range(modes)]
                totals.append(total)
            rows = slice(at, at + 2 * SUB)
            gate = gate_ref[rows, lanes].astype(F32)
            gated_ref[rows, lanes] = (gate * jnp.concatenate(totals, axis=0)).astype(BF16)

    def partial_product(index):
        channels = pl.ds(pl.multiple_of(index * batch, batch), batch)
        return jnp.dot(
            gated_ref[:, channels], weight_ref[channels, :], preferred_element_type=F32
        )

    def step(index, carry):
        total_ref[...] += partial_product(index - 1)
        for half in range(2):
            carry_pass(2 * index + half)
        return carry

    for half in range(2):
        carry_pass(half)
    total_ref[...] = jnp.zeros_like(total_ref)
    steps = chan // batch
    lax.fori_loop(1, steps, step, 0)
    sent_ref[...] = (total_ref[...] + partial_product(steps - 1)).astype(BF16)


def project(left_ref, right_ref, out_ref):
    total = out_ref.shape[1]
    tile = 2 * LANE if total % (2 * LANE) == 0 else LANE
    for first in range(0, total, tile):
        lanes = slice(first, first + tile)
        out_ref[:, lanes] = jnp.dot(
            left_ref[...], right_ref[:, lanes], preferred_element_type=F32
        ).astype(out_ref.dtype)


def product(gated_ref, weight):
    return jnp.dot(gated_ref[...], weight, preferred_element_type=F32)


def middle_kernel(gated_ref, kept_weight, sent_weight, kept_ref, sent_ref):
    project(gated_ref, kept_weight, kept_ref)
    project(gated_ref, sent_weight, sent_ref)


def join_kernel(kept_ref, moved_ref, *going_refs):
    wide = going_refs[0].shape[1]
    for at, going_ref in enumerate(going_refs):
        lanes = slice(at * wide, (at + 1) * wide)
        going_ref[...] = (kept_ref[:, lanes] + moved_ref[:, lanes].astype(F32)).astype(BF16)


def going_kernel(gated_ref, weight_ref, moved_ref, after_ref, *going_refs):
    wide = going_refs[0].shape[1]
    for at, going_ref in enumerate(going_refs):
        lanes = slice(at * wide, (at + 1) * wide)
        total = product(gated_ref, weight_ref[:, lanes])
        going_ref[...] = (total + moved_ref[:, lanes].astype(F32)).astype(BF16)


def late_kernel(gated_ref, weight_hbm, *refs):
    (low_ref, high_ref, weight_ref, sems) = refs[-4:]
    half = low_ref.shape[1]
    wait_all(column_copies(1, 0, range(1), weight_hbm, weight_ref, sems))
    low_ref[...] = product(gated_ref, weight_ref[:, :half]).astype(BF16)
    high_ref[...] = product(gated_ref, weight_ref[:, half:]).astype(BF16)


def own_kernel(gated_ref, weight_hbm, low_ref, high_ref, *refs):
    others, (first_ref, own_ref, weight_ref, sems) = refs[:-4], refs[-4:]
    narrow, half = first_ref.shape[1], low_ref.shape[1]
    wait_all(column_copies(0, 0, range(1), weight_hbm, weight_ref, sems))
    total = low_ref[:, :narrow].astype(F32) + product(gated_ref, weight_ref[:, :narrow])
    for other in others:
        total = total + other[...].astype(F32)
    first_ref[...] = total.astype(BF16)
    own_ref[:, : half - narrow] = low_ref[:, narrow:].astype(F32) + product(
        gated_ref, weight_ref[:, narrow:half]
    )
    own_ref[:, half - narrow :] = high_ref[...].astype(F32) + product(
        gated_ref, weight_ref[:, half:]
    )


def final_kernel(first_ref, own_ref, *refs):
    others, (out_hbm, wide_ref, sems) = refs[:-3], refs[-3:]
    tok, narrow = first_ref.shape
    count = sems.shape[0] - 1
    copies = [
        pltpu.make_async_copy(first_ref, out_hbm.at[:, pl.ds(0, narrow)], sems.at[count])
    ]
    copies[0].start()
    for part in range(count):
        rows = pl.ds(part * tok // count, tok // count)
        total = own_ref[rows, :]
        for other in others:
            total = total + other[rows, :].astype(F32)
        wide_ref[rows, :] = total.astype(BF16)
        columns = pl.ds(narrow, wide_ref.shape[1])
        copies.append(
            pltpu.make_async_copy(wide_ref.at[rows], out_hbm.at[rows, columns], sems.at[part])
        )
        copies[-1].start()
    wait_all(copies)


def call(kernel, outs, *operands, scratch=(), macs=0, out_spec=VMEM, in_place=0):
    specs, arrays = [], []
    for operand in operands:
        spec, array = operand if isinstance(operand, tuple) else (VMEM, operand)
        specs.append(ANY if spec is HBM else spec)
        arrays.append(in_hbm(array) if spec is HBM else array)
    return pl.pallas_call(
        kernel,
        out_shape=outs,
        in_specs=specs,
        out_specs=[out_spec] * (len(outs) - in_place) + [ANY] * in_place,
        scratch_shapes=scratch,
        compiler_params=PARAMS,
        cost_estimate=pl.CostEstimate(flops=2 * macs, bytes_accessed=0, transcendentals=0),
    )(*arrays)


def body(values, gate, residues, rates, skip, out_weight):
    shards, tp = lax.axis_size("seq"), lax.axis_size("tp")
    tok, chan = values.shape
    modes = rates.shape[0]
    chips = tp // 2
    away = chips - 1
    block = out_weight.shape[1] // tp
    here = pltpu.VMEM
    parts = 4 if chan % (4 * LANE) == 0 else 1
    cores = [(rank, rank ^ 1) for rank in range(tp)]
    sources = [(HBM, each) for each in (values, rates, residues, skip.reshape(1, chan), gate)]
    (wire,) = call(
        state_kernel,
        [jax.ShapeDtypeStruct((shards, modes, chan), BF16)],
        *sources[:2],
        scratch=[
            here((tok, chan), BF16),
            here((modes, chan), F32),
            pltpu.SemaphoreType.DMA((parts + 1,)),
        ],
    )
    states = lax.all_to_all(
        wire, "seq", split_axis=0, concat_axis=0, tiled=True,
        axis_index_groups=[group_order(shards)],
    )
    narrow = max(LANE, block // 4)
    wide = block - narrow
    weight = (HBM, out_weight)
    *tables, first_weight, kept_weight, sent_weight, last_weight = call(
        local_kernel,
        [
            here((tok, chan), F32),
            here((modes * SUB, chan), F32),
            here((modes, chan), F32),
            here((modes, chan), F32),
            here((tok, chan), BF16),
            here((chan, away * narrow), BF16),
            here((chan, away * narrow), BF16),
            pltpu.HBM((chan, away * wide), BF16),
            pltpu.HBM((chan, away * wide), BF16),
        ],
        *sources, weight,
        in_place=2,
        scratch=[
            here((tok, chan), BF16),
            here((modes, chan), F32),
            here((modes, chan), F32),
            here((1, chan), F32),
            here((tok, chan), F32),
            here((SUB, LANE), F32),
            here((modes * SUB, LANE), F32),
            here((tok // SUB // SUB, modes * SUB, LANE), F32),
            here((tok, LANE), F32),
            here((chan, away * wide), BF16),
            here((chan, away * wide), BF16),
            pltpu.SemaphoreType.DMA((len(sources),)),
            pltpu.SemaphoreType.DMA((4, away * ROW_CUTS)),
            pltpu.SemaphoreType.DMA((2,)),
        ],
    )

    hint = 16 * tok * chan * block
    gated, sent = call(
        gate_kernel,
        [here((tok, chan), BF16), here((tok, away * narrow), BF16)],
        states, *tables, first_weight,
        scratch=[here((modes, chan), F32), here((tok, away * narrow), F32)], macs=hint,
    )
    moved_first = lax.ppermute(sent, "tp", cores)
    kept, sent = call(
        middle_kernel,
        [here((tok, away * narrow), F32), here((tok, away * wide), BF16)],
        gated, kept_weight, sent_weight,
    )
    moved = lax.ppermute(sent, "tp", cores)

    def to_chips(going):
        return [
            lax.ppermute(each, "tp", [(rank, (rank + 2 * hop) % tp) for rank in reversed(range(tp))])
            for hop, each in enumerate(going, 1)
        ]

    going = call(join_kernel, [here((tok, narrow), BF16)] * away, kept, moved_first, macs=hint)
    first = to_chips(going)
    going = call(
        going_kernel, [here((tok, wide), BF16)] * away,
        gated, last_weight, moved, (ANY, going[-1]),
    )
    second = to_chips(going)
    late = [here((chan, block), BF16), pltpu.SemaphoreType.DMA((ROW_CUTS,))]
    halves = call(
        late_kernel, [here((tok, block // 2), BF16)] * 2,
        gated, weight, (ANY, going[-1]), (ANY, first[-1]), scratch=late, macs=hint,
    )
    halves = [lax.ppermute(each, "tp", cores) for each in halves]
    done, own = call(
        own_kernel, [here((tok, narrow), BF16), here((tok, wide), F32)],
        gated, weight, *halves, *first, scratch=late,
    )
    (out,) = call(
        final_kernel, [jax.ShapeDtypeStruct((tok, block), BF16)], done, own, *second,
        scratch=[here((tok, wide), BF16), pltpu.SemaphoreType.DMA((3,))],
        out_spec=ANY,
    )
    return out


def solution(mesh):
    placed = (P("seq", "tp"), P("seq", "tp"), P(None, "tp"), P(None, "tp"), P("tp"), P("tp", None))
    return jax.shard_map(
        body, mesh=mesh, in_specs=placed, out_specs=P("seq", "tp"), check_vma=False
    )
```

```python
from functools import partial

import jax
import jax.numpy as jnp
from jax import lax
from jax.experimental import pallas as pl
from jax.experimental.pallas import tpu as pltpu
from jax.sharding import PartitionSpec as P

SUB, LANE = 8, 128
F32, BF16 = jnp.float32, jnp.bfloat16

VMEM = pl.BlockSpec(memory_space=pltpu.VMEM)
ANY = pl.BlockSpec(memory_space=pl.ANY)
HBM = "hbm"
PARAMS = pltpu.CompilerParams(vmem_limit_bytes=24 * 2**20)


def in_hbm(array):
    return pltpu.with_memory_space_constraint(array, pltpu.HBM)


def in_vmem(array):
    return pltpu.with_memory_space_constraint(array, pltpu.VMEM)


def row_of(block, mode):
    return jnp.broadcast_to(block[mode : mode + 1, :], (SUB, LANE))


def sublane():
    return lax.broadcasted_iota(jnp.int32, (SUB, LANE), 0)


def lanes_at(step):
    return pl.ds(pl.multiple_of(step * LANE, LANE), LANE)


def gains_of(residues, rates):
    return residues * jnp.sqrt(2.0 * rates)


def spread_table(tok):
    run = tok // SUB
    row = lax.broadcasted_iota(jnp.int32, (tok, tok), 0)
    col = lax.broadcasted_iota(jnp.int32, (tok, tok), 1)
    return (col == row % SUB * run + row // SUB).astype(F32).astype(BF16)


ROW_CUTS = 4
STEP_ROWS = 64


def column_copies(other, begin, slots, weight_hbm, out_ref, sems):
    rank = lax.axis_index("tp")
    chips = lax.axis_size("tp") // 2
    block = weight_hbm.shape[1] // (2 * chips)
    wide = out_ref.shape[1] // len(slots)
    tall = out_ref.shape[0] // ROW_CUTS
    core = 1 - rank % 2 if other else rank % 2
    copies = []
    for at, slot in enumerate(slots):
        owner = (rank // 2 + slot) % chips * 2 + core
        columns = pl.ds(pl.multiple_of(owner * block + begin, LANE), wide)
        for cut in range(ROW_CUTS):
            rows = pl.ds(cut * tall, tall)
            copies.append(
                pltpu.make_async_copy(
                    weight_hbm.at[rows, columns],
                    out_ref.at[rows, pl.ds(at * wide, wide)],
                    sems.at[at * ROW_CUTS + cut],
                )
            )
            copies[-1].start()
    return copies


def group_order(count):
    return [(count // 2 + at) % count for at in range(count)]


def wait_all(copies):
    for copy in copies:
        copy.wait()


def state_kernel(values_hbm, rates_hbm, wire_ref, values_ref, rates_ref, sems):
    tok, chan = values_ref.shape
    modes = rates_ref.shape[0]
    parts = sems.shape[0] - 1
    width = chan // parts
    first = pltpu.make_async_copy(rates_hbm, rates_ref, sems.at[parts])
    first.start()
    pieces = []
    for part in range(parts):
        lanes = pl.ds(part * width, width)
        pieces.append(
            pltpu.make_async_copy(
                values_hbm.at[:, lanes], values_ref.at[:, lanes], sems.at[part]
            )
        )
        pieces[-1].start()
    left = (SUB - 1 - sublane()).astype(F32)
    first.wait()
    for index in range(chan // LANE):
        if index * LANE % width == 0:
            pieces[index * LANE // width].wait()
        lanes = slice(index * LANE, (index + 1) * LANE)
        rates = rates_ref[:, lanes]
        decay = jnp.exp(-float(SUB) * rates)
        decays = [row_of(decay, mode) for mode in range(modes)]
        held = [jnp.zeros((SUB, LANE), F32)] * modes
        for at in range(0, tok, 2 * SUB):
            pair = values_ref[at : at + 2 * SUB, lanes].astype(F32)
            for half in (pair[:SUB], pair[SUB:]):
                held = [decays[mode] * held[mode] + half for mode in range(modes)]
        rows = [
            jnp.sum(held[mode] * jnp.exp(-row_of(rates, mode) * left), axis=0, keepdims=True)
            for mode in range(modes)
        ]
        state = jnp.concatenate(rows, axis=0).astype(BF16)
        for shard in range(wire_ref.shape[0]):
            wire_ref[shard, :, lanes] = state


def local_kernel(
    values_hbm, rates_hbm, residues_hbm, skip_hbm, gate_hbm, weight_hbm,
    near_ref, reach_ref, decay_ref, far_ref, gate_ref, first_weight, kept_weight,
    sent_weight, last_weight,
    values_ref, rates_ref, residues_ref, skip_ref, wide_ref, taps_ref, first_ref, snap_ref,
    order_ref, sent_held, last_held, sems, weight_sems, out_sems,
):
    tok, chan = values_ref.shape
    modes = rates_ref.shape[0]
    run = tok // SUB
    copies = [
        pltpu.make_async_copy(source, target, sems.at[at])
        for at, (source, target) in enumerate(
            (
                (values_hbm, values_ref),
                (rates_hbm, rates_ref),
                (residues_hbm, residues_ref),
                (skip_hbm, skip_ref),
                (gate_hbm, gate_ref),
            )
        )
    ]
    for copy in copies:
        copy.start()
    slots = range(1, lax.axis_size("tp") // 2)
    rest = column_copies(1, 0, slots, weight_hbm, first_weight, weight_sems.at[0])
    rest += column_copies(0, 0, slots, weight_hbm, kept_weight, weight_sems.at[1])
    begin = kept_weight.shape[1] // len(slots)
    passing = column_copies(1, begin, slots, weight_hbm, sent_held, weight_sems.at[2])
    passing += column_copies(0, begin, slots, weight_hbm, last_held, weight_sems.at[3])
    rest.append(copies.pop())
    table = spread_table(tok)
    wait_all(copies)
    wide_ref[...] = jnp.dot(table, values_ref[...], preferred_element_type=F32)

    def step(index, carry):
        lanes = lanes_at(index)
        place = sublane()
        rates = rates_ref[:, lanes]
        gains = gains_of(residues_ref[:, lanes], rates)

        ahead = place.astype(F32)
        decay, decay_block = jnp.exp(-rates), jnp.exp(-float(SUB) * rates)
        decay_run = jnp.exp(-float(run) * rates)
        decays = [row_of(decay, mode) for mode in range(modes)]
        taps = jnp.where(place == 0, skip_ref[:, lanes], 0.0)
        for mode in range(modes):
            gain = row_of(gains, mode)
            term = gain * jnp.exp(-row_of(rates, mode) * ahead)
            taps = taps + term
            first_ref[mode * SUB : (mode + 1) * SUB, :] = gain * decays[mode]
            reach_ref[mode * SUB : (mode + 1) * SUB, lanes] = term * decays[mode]
        taps_ref[...] = taps

        held = [jnp.zeros((SUB, LANE), F32)] * modes
        for at in range(run):
            if at % SUB == 0:
                for mode in range(modes):
                    snap_ref[at // SUB, mode * SUB : (mode + 1) * SUB, :] = held[mode]
            value = wide_ref[at * SUB : (at + 1) * SUB, lanes]
            held = [decays[mode] * held[mode] + value for mode in range(modes)]
        for mode in range(modes):
            whole, power = held[mode], row_of(decay_run, mode)
            for shift in (1, 2, 4):
                moved = jnp.where(place >= shift, pltpu.roll(whole, shift, 0), 0.0)
                whole = whole + power * moved
                power = power * power
            before = jnp.where(place >= 1, pltpu.roll(whole, 1, 0), 0.0)
            rows = slice(mode * SUB, (mode + 1) * SUB)
            fade = row_of(decay_block, mode)
            for block in range(run // SUB):
                snap_ref[block, rows, :] = first_ref[rows, :] * (snap_ref[block, rows, :] + before)
                before = fade * before

        for block in range(run // SUB):
            values = [
                wide_ref[(block * SUB + at) * SUB : (block * SUB + at + 1) * SUB, lanes]
                for at in range(SUB)
            ]
            sums = [jnp.zeros((SUB, LANE), F32)] * SUB
            for lag in range(SUB):
                tap = jnp.broadcast_to(taps_ref[lag : lag + 1, :], (SUB, LANE))
                for at in range(lag, SUB):
                    sums[at] = sums[at] + tap * values[at - lag]
            terms = [
                snap_ref[block, mode * SUB : (mode + 1) * SUB, :] for mode in range(modes)
            ]
            for at in range(SUB):
                total = sums[at]
                for mode in range(modes):
                    total = total + terms[mode]
                terms = [terms[mode] * decays[mode] for mode in range(modes)]
                order_ref[pl.ds(block * SUB + at, SUB, stride=run), :] = total
        near_ref[:, lanes] = order_ref[...]
        decay_ref[:, lanes] = jnp.exp(-float(SUB) * rates)
        far_ref[:, lanes] = jnp.exp(-float(tok) * rates)
        return carry

    steps = chan // LANE
    lax.fori_loop(0, steps // 2, step, 0)
    wait_all(passing)
    for at, (held, target) in enumerate(((sent_held, sent_weight), (last_held, last_weight))):
        rest.append(pltpu.make_async_copy(held, target, out_sems.at[at]))
        rest[-1].start()
    lax.fori_loop(steps // 2, steps, step, 0)
    wait_all(rest)


def gate_kernel(
    states_ref, near_ref, reach_ref, decay_ref, far_ref, gate_ref, weight_ref,
    gated_ref, sent_ref, state_ref,
):
    tok, chan = gate_ref.shape
    shards, modes = states_ref.shape[:2]
    place = lax.axis_index("seq")
    far = far_ref[...]
    before = jnp.zeros((modes, chan), F32)
    order = group_order(shards)
    for shard in range(shards - 1):
        passed = far * before + states_ref[order.index(shard)].astype(F32)
        before = jnp.where(shard < place, passed, before)
    state_ref[...] = before

    def step(index, carry):
        lanes = lanes_at(index)
        decays, terms = [], []
        for mode in range(modes):
            rows, row = slice(mode * SUB, (mode + 1) * SUB), slice(mode, mode + 1)
            decays.append(jnp.broadcast_to(decay_ref[row, lanes], (SUB, LANE)))
            state = jnp.broadcast_to(state_ref[row, lanes], (SUB, LANE))
            terms.append(state * reach_ref[rows, lanes])
        def rows_step(group, terms):
            terms = list(terms)
            for at in range(0, STEP_ROWS, 2 * SUB):
                totals = []
                for first in (at, at + SUB):
                    rows = pl.ds(pl.multiple_of(group * STEP_ROWS + first, SUB), SUB)
                    total = near_ref[rows, lanes]
                    for mode in range(modes):
                        total = total + terms[mode]
                    terms = [terms[mode] * decays[mode] for mode in range(modes)]
                    totals.append(total)
                rows = pl.ds(pl.multiple_of(group * STEP_ROWS + at, 2 * SUB), 2 * SUB)
                gate = gate_ref[rows, lanes].astype(F32)
                gated_ref[rows, lanes] = (gate * jnp.concatenate(totals, axis=0)).astype(BF16)
            return tuple(terms)

        lax.fori_loop(0, tok // STEP_ROWS, rows_step, tuple(terms))
        return carry

    lax.fori_loop(0, chan // LANE, step, 0)
    project(gated_ref, weight_ref, sent_ref)


def project(left_ref, right_ref, out_ref):
    total = out_ref.shape[1]
    tile = 2 * LANE if total % (2 * LANE) == 0 else LANE
    for first in range(0, total, tile):
        lanes = slice(first, first + tile)
        out_ref[:, lanes] = jnp.dot(
            left_ref[...], right_ref[:, lanes], preferred_element_type=F32
        ).astype(out_ref.dtype)


def product(gated_ref, weight):
    return jnp.dot(gated_ref[...], weight, preferred_element_type=F32)


def middle_kernel(gated_ref, kept_weight, sent_weight, kept_ref, sent_ref):
    project(gated_ref, kept_weight, kept_ref)
    project(gated_ref, sent_weight, sent_ref)


def join_kernel(kept_ref, moved_ref, *going_refs):
    wide = going_refs[0].shape[1]
    for at, going_ref in enumerate(going_refs):
        lanes = slice(at * wide, (at + 1) * wide)
        going_ref[...] = (kept_ref[:, lanes] + moved_ref[:, lanes].astype(F32)).astype(BF16)


def going_kernel(gated_ref, weight_ref, moved_ref, after_ref, *going_refs):
    wide = going_refs[0].shape[1]
    for at, going_ref in enumerate(going_refs):
        lanes = slice(at * wide, (at + 1) * wide)
        total = product(gated_ref, weight_ref[:, lanes])
        going_ref[...] = (total + moved_ref[:, lanes].astype(F32)).astype(BF16)


def late_kernel(gated_ref, weight_hbm, *refs):
    (low_ref, high_ref, weight_ref, sems) = refs[-4:]
    half = low_ref.shape[1]
    wait_all(column_copies(1, 0, range(1), weight_hbm, weight_ref, sems))
    low_ref[...] = product(gated_ref, weight_ref[:, :half]).astype(BF16)
    high_ref[...] = product(gated_ref, weight_ref[:, half:]).astype(BF16)


def own_kernel(gated_ref, weight_hbm, low_ref, high_ref, *refs):
    others, (first_ref, own_ref, weight_ref, sems) = refs[:-4], refs[-4:]
    narrow, half = first_ref.shape[1], low_ref.shape[1]
    wait_all(column_copies(0, 0, range(1), weight_hbm, weight_ref, sems))
    total = low_ref[:, :narrow].astype(F32) + product(gated_ref, weight_ref[:, :narrow])
    for other in others:
        total = total + other[...].astype(F32)
    first_ref[...] = total.astype(BF16)
    own_ref[:, : half - narrow] = low_ref[:, narrow:].astype(F32) + product(
        gated_ref, weight_ref[:, narrow:half]
    )
    own_ref[:, half - narrow :] = high_ref[...].astype(F32) + product(
        gated_ref, weight_ref[:, half:]
    )


def final_kernel(first_ref, own_ref, *refs):
    others, (out_hbm, wide_ref, sems) = refs[:-3], refs[-3:]
    tok, narrow = first_ref.shape
    count = sems.shape[0] - 1
    copies = [
        pltpu.make_async_copy(first_ref, out_hbm.at[:, pl.ds(0, narrow)], sems.at[count])
    ]
    copies[0].start()
    for part in range(count):
        rows = pl.ds(part * tok // count, tok // count)
        total = own_ref[rows, :]
        for other in others:
            total = total + other[rows, :].astype(F32)
        wide_ref[rows, :] = total.astype(BF16)
        columns = pl.ds(narrow, wide_ref.shape[1])
        copies.append(
            pltpu.make_async_copy(wide_ref.at[rows], out_hbm.at[rows, columns], sems.at[part])
        )
        copies[-1].start()
    wait_all(copies)


def call(kernel, outs, *operands, scratch=(), macs=0, out_spec=VMEM, in_place=0):
    specs, arrays = [], []
    for operand in operands:
        spec, array = operand if isinstance(operand, tuple) else (VMEM, operand)
        specs.append(ANY if spec is HBM else spec)
        arrays.append(in_hbm(array) if spec is HBM else array)
    return pl.pallas_call(
        kernel,
        out_shape=outs,
        in_specs=specs,
        out_specs=[out_spec] * (len(outs) - in_place) + [ANY] * in_place,
        scratch_shapes=scratch,
        compiler_params=PARAMS,
        cost_estimate=pl.CostEstimate(flops=2 * macs, bytes_accessed=0, transcendentals=0),
    )(*arrays)


def body(values, gate, residues, rates, skip, out_weight):
    shards, tp = lax.axis_size("seq"), lax.axis_size("tp")
    tok, chan = values.shape
    modes = rates.shape[0]
    chips = tp // 2
    away = chips - 1
    block = out_weight.shape[1] // tp
    here = pltpu.VMEM
    parts = 4 if chan % (4 * LANE) == 0 else 1
    cores = [(rank, rank ^ 1) for rank in range(tp)]
    sources = [(HBM, each) for each in (values, rates, residues, skip.reshape(1, chan), gate)]
    (wire,) = call(
        state_kernel,
        [jax.ShapeDtypeStruct((shards, modes, chan), BF16)],
        *sources[:2],
        scratch=[
            here((tok, chan), BF16),
            here((modes, chan), F32),
            pltpu.SemaphoreType.DMA((parts + 1,)),
        ],
    )
    states = lax.all_to_all(
        wire, "seq", split_axis=0, concat_axis=0, tiled=True,
        axis_index_groups=[group_order(shards)],
    )
    narrow = max(LANE, block // 4)
    wide = block - narrow
    weight = (HBM, out_weight)
    *tables, first_weight, kept_weight, sent_weight, last_weight = call(
        local_kernel,
        [
            here((tok, chan), F32),
            here((modes * SUB, chan), F32),
            here((modes, chan), F32),
            here((modes, chan), F32),
            here((tok, chan), BF16),
            here((chan, away * narrow), BF16),
            here((chan, away * narrow), BF16),
            pltpu.HBM((chan, away * wide), BF16),
            pltpu.HBM((chan, away * wide), BF16),
        ],
        *sources, weight,
        in_place=2,
        scratch=[
            here((tok, chan), BF16),
            here((modes, chan), F32),
            here((modes, chan), F32),
            here((1, chan), F32),
            here((tok, chan), F32),
            here((SUB, LANE), F32),
            here((modes * SUB, LANE), F32),
            here((tok // SUB // SUB, modes * SUB, LANE), F32),
            here((tok, LANE), F32),
            here((chan, away * wide), BF16),
            here((chan, away * wide), BF16),
            pltpu.SemaphoreType.DMA((len(sources),)),
            pltpu.SemaphoreType.DMA((4, away * ROW_CUTS)),
            pltpu.SemaphoreType.DMA((2,)),
        ],
    )

    hint = 16 * tok * chan * block
    gated, sent = call(
        gate_kernel,
        [here((tok, chan), BF16), here((tok, away * narrow), BF16)],
        states, *tables, first_weight,
        scratch=[here((modes, chan), F32)], macs=hint,
    )
    moved_first = lax.ppermute(sent, "tp", cores)
    kept, sent = call(
        middle_kernel,
        [here((tok, away * narrow), F32), here((tok, away * wide), BF16)],
        gated, kept_weight, sent_weight,
    )
    moved = lax.ppermute(sent, "tp", cores)

    def to_chips(going):
        return [
            lax.ppermute(each, "tp", [(rank, (rank + 2 * hop) % tp) for rank in reversed(range(tp))])
            for hop, each in enumerate(going, 1)
        ]

    going = call(join_kernel, [here((tok, narrow), BF16)] * away, kept, moved_first, macs=hint)
    first = to_chips(going)
    going = call(
        going_kernel, [here((tok, wide), BF16)] * away,
        gated, last_weight, moved, (ANY, going[-1]),
    )
    second = to_chips(going)
    late = [here((chan, block), BF16), pltpu.SemaphoreType.DMA((ROW_CUTS,))]
    halves = call(
        late_kernel, [here((tok, block // 2), BF16)] * 2,
        gated, weight, (ANY, going[-1]), (ANY, first[-1]), scratch=late, macs=hint,
    )
    halves = [lax.ppermute(each, "tp", cores) for each in halves]
    done, own = call(
        own_kernel, [here((tok, narrow), BF16), here((tok, wide), F32)],
        gated, weight, *halves, *first, scratch=late,
    )
    (out,) = call(
        final_kernel, [jax.ShapeDtypeStruct((tok, block), BF16)], done, own, *second,
        scratch=[here((tok, wide), BF16), pltpu.SemaphoreType.DMA((3,))],
        out_spec=ANY,
    )
    return out


def solution(mesh):
    placed = (P("seq", "tp"), P("seq", "tp"), P(None, "tp"), P(None, "tp"), P("tp"), P("tp", None))
    return jax.shard_map(
        body, mesh=mesh, in_specs=placed, out_specs=P("seq", "tp"), check_vma=False
    )
```

```python
from functools import partial

import jax
import jax.numpy as jnp
from jax import lax
from jax.experimental import pallas as pl
from jax.experimental.pallas import tpu as pltpu
from jax.sharding import PartitionSpec as P

SUB, LANE = 8, 128
F32, BF16 = jnp.float32, jnp.bfloat16

VMEM = pl.BlockSpec(memory_space=pltpu.VMEM)
ANY = pl.BlockSpec(memory_space=pl.ANY)
HBM = "hbm"
PARAMS = pltpu.CompilerParams(vmem_limit_bytes=24 * 2**20)


def in_hbm(array):
    return pltpu.with_memory_space_constraint(array, pltpu.HBM)


def in_vmem(array):
    return pltpu.with_memory_space_constraint(array, pltpu.VMEM)


def row_of(block, mode):
    return jnp.broadcast_to(block[mode : mode + 1, :], (SUB, LANE))


def sublane():
    return lax.broadcasted_iota(jnp.int32, (SUB, LANE), 0)


def lanes_at(step):
    return pl.ds(pl.multiple_of(step * LANE, LANE), LANE)


def gains_of(residues, rates):
    return residues * jnp.sqrt(2.0 * rates)


def spread_table(tok):
    run = tok // SUB
    row = lax.broadcasted_iota(jnp.int32, (tok, tok), 0)
    col = lax.broadcasted_iota(jnp.int32, (tok, tok), 1)
    return (col == row % SUB * run + row // SUB).astype(F32).astype(BF16)


ROW_CUTS = 4


def column_copies(other, begin, slots, weight_hbm, out_ref, sems):
    rank = lax.axis_index("tp")
    chips = lax.axis_size("tp") // 2
    block = weight_hbm.shape[1] // (2 * chips)
    wide = out_ref.shape[1] // len(slots)
    tall = out_ref.shape[0] // ROW_CUTS
    core = 1 - rank % 2 if other else rank % 2
    copies = []
    for at, slot in enumerate(slots):
        owner = (rank // 2 + slot) % chips * 2 + core
        columns = pl.ds(pl.multiple_of(owner * block + begin, LANE), wide)
        for cut in range(ROW_CUTS):
            rows = pl.ds(cut * tall, tall)
            copies.append(
                pltpu.make_async_copy(
                    weight_hbm.at[rows, columns],
                    out_ref.at[rows, pl.ds(at * wide, wide)],
                    sems.at[at * ROW_CUTS + cut],
                )
            )
            copies[-1].start()
    return copies


def group_order(count):
    return [(count // 2 + 1 + at) % count for at in range(count)]


def wait_all(copies):
    for copy in copies:
        copy.wait()


def state_kernel(values_hbm, rates_hbm, wire_ref, values_ref, rates_ref, sems):
    tok, chan = values_ref.shape
    modes = rates_ref.shape[0]
    parts = sems.shape[0] - 1
    width = chan // parts
    first = pltpu.make_async_copy(rates_hbm, rates_ref, sems.at[parts])
    first.start()
    pieces = []
    for part in range(parts):
        lanes = pl.ds(part * width, width)
        pieces.append(
            pltpu.make_async_copy(
                values_hbm.at[:, lanes], values_ref.at[:, lanes], sems.at[part]
            )
        )
        pieces[-1].start()
    left = (SUB - 1 - sublane()).astype(F32)
    first.wait()
    for index in range(chan // LANE):
        if index * LANE % width == 0:
            pieces[index * LANE // width].wait()
        lanes = slice(index * LANE, (index + 1) * LANE)
        rates = rates_ref[:, lanes]
        decay = jnp.exp(-float(SUB) * rates)
        decays = [row_of(decay, mode) for mode in range(modes)]
        held = [jnp.zeros((SUB, LANE), F32)] * modes
        for at in range(0, tok, 2 * SUB):
            pair = values_ref[at : at + 2 * SUB, lanes].astype(F32)
            for half in (pair[:SUB], pair[SUB:]):
                held = [decays[mode] * held[mode] + half for mode in range(modes)]
        rows = [
            jnp.sum(held[mode] * jnp.exp(-row_of(rates, mode) * left), axis=0, keepdims=True)
            for mode in range(modes)
        ]
        state = jnp.concatenate(rows, axis=0).astype(BF16)
        for shard in range(wire_ref.shape[0]):
            wire_ref[shard, :, lanes] = state


def local_kernel(
    values_hbm, rates_hbm, residues_hbm, skip_hbm, gate_hbm, weight_hbm,
    near_ref, reach_ref, decay_ref, far_ref, gate_ref, first_weight, kept_weight,
    sent_weight, last_weight,
    values_ref, rates_ref, residues_ref, skip_ref, wide_ref, taps_ref, first_ref, snap_ref,
    order_ref, sent_held, last_held, sems, weight_sems, out_sems,
):
    tok, chan = values_ref.shape
    modes = rates_ref.shape[0]
    run = tok // SUB
    copies = [
        pltpu.make_async_copy(source, target, sems.at[at])
        for at, (source, target) in enumerate(
            (
                (values_hbm, values_ref),
                (rates_hbm, rates_ref),
                (residues_hbm, residues_ref),
                (skip_hbm, skip_ref),
                (gate_hbm, gate_ref),
            )
        )
    ]
    for copy in copies:
        copy.start()
    slots = range(1, lax.axis_size("tp") // 2)
    rest = column_copies(1, 0, slots, weight_hbm, first_weight, weight_sems.at[0])
    rest += column_copies(0, 0, slots, weight_hbm, kept_weight, weight_sems.at[1])
    begin = kept_weight.shape[1] // len(slots)
    passing = column_copies(1, begin, slots, weight_hbm, sent_held, weight_sems.at[2])
    passing += column_copies(0, begin, slots, weight_hbm, last_held, weight_sems.at[3])
    rest.append(copies.pop())
    table = spread_table(tok)
    wait_all(copies)
    wide_ref[...] = jnp.dot(table, values_ref[...], preferred_element_type=F32)

    def step(index, carry):
        lanes = lanes_at(index)
        place = sublane()
        rates = rates_ref[:, lanes]
        gains = gains_of(residues_ref[:, lanes], rates)

        ahead = place.astype(F32)
        decay, decay_block = jnp.exp(-rates), jnp.exp(-float(SUB) * rates)
        decay_run = jnp.exp(-float(run) * rates)
        decays = [row_of(decay, mode) for mode in range(modes)]
        taps = jnp.where(place == 0, skip_ref[:, lanes], 0.0)
        for mode in range(modes):
            gain = row_of(gains, mode)
            term = gain * jnp.exp(-row_of(rates, mode) * ahead)
            taps = taps + term
            first_ref[mode * SUB : (mode + 1) * SUB, :] = gain * decays[mode]
            reach_ref[mode * SUB : (mode + 1) * SUB, lanes] = term * decays[mode]
        taps_ref[...] = taps

        held = [jnp.zeros((SUB, LANE), F32)] * modes
        for at in range(run):
            if at % SUB == 0:
                for mode in range(modes):
                    snap_ref[at // SUB, mode * SUB : (mode + 1) * SUB, :] = held[mode]
            value = wide_ref[at * SUB : (at + 1) * SUB, lanes]
            held = [decays[mode] * held[mode] + value for mode in range(modes)]
        for mode in range(modes):
            whole, power = held[mode], row_of(decay_run, mode)
            for shift in (1, 2, 4):
                moved = jnp.where(place >= shift, pltpu.roll(whole, shift, 0), 0.0)
                whole = whole + power * moved
                power = power * power
            before = jnp.where(place >= 1, pltpu.roll(whole, 1, 0), 0.0)
            rows = slice(mode * SUB, (mode + 1) * SUB)
            fade = row_of(decay_block, mode)
            for block in range(run // SUB):
                snap_ref[block, rows, :] = first_ref[rows, :] * (snap_ref[block, rows, :] + before)
                before = fade * before

        for block in range(run // SUB):
            values = [
                wide_ref[(block * SUB + at) * SUB : (block * SUB + at + 1) * SUB, lanes]
                for at in range(SUB)
            ]
            sums = [jnp.zeros((SUB, LANE), F32)] * SUB
            for lag in range(SUB):
                tap = jnp.broadcast_to(taps_ref[lag : lag + 1, :], (SUB, LANE))
                for at in range(lag, SUB):
                    sums[at] = sums[at] + tap * values[at - lag]
            terms = [
                snap_ref[block, mode * SUB : (mode + 1) * SUB, :] for mode in range(modes)
            ]
            for at in range(SUB):
                total = sums[at]
                for mode in range(modes):
                    total = total + terms[mode]
                terms = [terms[mode] * decays[mode] for mode in range(modes)]
                order_ref[pl.ds(block * SUB + at, SUB, stride=run), :] = total
        near_ref[:, lanes] = order_ref[...]
        decay_ref[:, lanes] = jnp.exp(-float(SUB) * rates)
        far_ref[:, lanes] = jnp.exp(-float(tok) * rates)
        return carry

    steps = chan // LANE
    lax.fori_loop(0, steps // 2, step, 0)
    wait_all(passing)
    for at, (held, target) in enumerate(((sent_held, sent_weight), (last_held, last_weight))):
        rest.append(pltpu.make_async_copy(held, target, out_sems.at[at]))
        rest[-1].start()
    lax.fori_loop(steps // 2, steps, step, 0)
    wait_all(rest)


def gate_kernel(
    states_ref, near_ref, reach_ref, decay_ref, far_ref, gate_ref, weight_ref,
    gated_ref, sent_ref, state_ref,
):
    tok, chan = gate_ref.shape
    shards, modes = states_ref.shape[:2]
    place = lax.axis_index("seq")
    far = far_ref[...]
    before = jnp.zeros((modes, chan), F32)
    order = group_order(shards)
    for shard in range(shards - 1):
        passed = far * before + states_ref[order.index(shard)].astype(F32)
        before = jnp.where(shard < place, passed, before)
    state_ref[...] = before

    def step(index, carry):
        lanes = lanes_at(index)
        decays, terms = [], []
        for mode in range(modes):
            rows, row = slice(mode * SUB, (mode + 1) * SUB), slice(mode, mode + 1)
            decays.append(jnp.broadcast_to(decay_ref[row, lanes], (SUB, LANE)))
            state = jnp.broadcast_to(state_ref[row, lanes], (SUB, LANE))
            terms.append(state * reach_ref[rows, lanes])
        for at in range(0, tok, 2 * SUB):
            totals = []
            for first in (at, at + SUB):
                total = near_ref[first : first + SUB, lanes]
                for mode in range(modes):
                    total = total + terms[mode]
                terms = [terms[mode] * decays[mode] for mode in range(modes)]
                totals.append(total)
            rows = slice(at, at + 2 * SUB)
            gate = gate_ref[rows, lanes].astype(F32)
            gated_ref[rows, lanes] = (gate * jnp.concatenate(totals, axis=0)).astype(BF16)
        return carry

    lax.fori_loop(0, chan // LANE, step, 0)
    project(gated_ref, weight_ref, sent_ref)


def project(left_ref, right_ref, out_ref):
    total = out_ref.shape[1]
    tile = 2 * LANE if total % (2 * LANE) == 0 else LANE
    for first in range(0, total, tile):
        lanes = slice(first, first + tile)
        out_ref[:, lanes] = jnp.dot(
            left_ref[...], right_ref[:, lanes], preferred_element_type=F32
        ).astype(out_ref.dtype)


def product(gated_ref, weight):
    return jnp.dot(gated_ref[...], weight, preferred_element_type=F32)


def middle_kernel(gated_ref, kept_weight, sent_weight, kept_ref, sent_ref):
    project(gated_ref, kept_weight, kept_ref)
    project(gated_ref, sent_weight, sent_ref)


def join_kernel(kept_ref, moved_ref, *going_refs):
    wide = going_refs[0].shape[1]
    for at, going_ref in enumerate(going_refs):
        lanes = slice(at * wide, (at + 1) * wide)
        going_ref[...] = (kept_ref[:, lanes] + moved_ref[:, lanes].astype(F32)).astype(BF16)


def going_kernel(gated_ref, weight_ref, moved_ref, after_ref, *going_refs):
    wide = going_refs[0].shape[1]
    for at, going_ref in enumerate(going_refs):
        lanes = slice(at * wide, (at + 1) * wide)
        total = product(gated_ref, weight_ref[:, lanes])
        going_ref[...] = (total + moved_ref[:, lanes].astype(F32)).astype(BF16)


def late_kernel(gated_ref, weight_hbm, *refs):
    (low_ref, high_ref, weight_ref, sems) = refs[-4:]
    half = low_ref.shape[1]
    wait_all(column_copies(1, 0, range(1), weight_hbm, weight_ref, sems))
    low_ref[...] = product(gated_ref, weight_ref[:, :half]).astype(BF16)
    high_ref[...] = product(gated_ref, weight_ref[:, half:]).astype(BF16)


def own_kernel(gated_ref, weight_hbm, low_ref, high_ref, *refs):
    others, (first_ref, own_ref, weight_ref, sems) = refs[:-4], refs[-4:]
    narrow, half = first_ref.shape[1], low_ref.shape[1]
    wait_all(column_copies(0, 0, range(1), weight_hbm, weight_ref, sems))
    total = low_ref[:, :narrow].astype(F32) + product(gated_ref, weight_ref[:, :narrow])
    for other in others:
        total = total + other[...].astype(F32)
    first_ref[...] = total.astype(BF16)
    own_ref[:, : half - narrow] = low_ref[:, narrow:].astype(F32) + product(
        gated_ref, weight_ref[:, narrow:half]
    )
    own_ref[:, half - narrow :] = high_ref[...].astype(F32) + product(
        gated_ref, weight_ref[:, half:]
    )


def final_kernel(first_ref, own_ref, *refs):
    others, (out_hbm, wide_ref, sems) = refs[:-3], refs[-3:]
    tok, narrow = first_ref.shape
    count = sems.shape[0] - 1
    copies = [
        pltpu.make_async_copy(first_ref, out_hbm.at[:, pl.ds(0, narrow)], sems.at[count])
    ]
    copies[0].start()
    for part in range(count):
        rows = pl.ds(part * tok // count, tok // count)
        total = own_ref[rows, :]
        for other in others:
            total = total + other[rows, :].astype(F32)
        wide_ref[rows, :] = total.astype(BF16)
        columns = pl.ds(narrow, wide_ref.shape[1])
        copies.append(
            pltpu.make_async_copy(wide_ref.at[rows], out_hbm.at[rows, columns], sems.at[part])
        )
        copies[-1].start()
    wait_all(copies)


def call(kernel, outs, *operands, scratch=(), macs=0, out_spec=VMEM, in_place=0):
    specs, arrays = [], []
    for operand in operands:
        spec, array = operand if isinstance(operand, tuple) else (VMEM, operand)
        specs.append(ANY if spec is HBM else spec)
        arrays.append(in_hbm(array) if spec is HBM else array)
    return pl.pallas_call(
        kernel,
        out_shape=outs,
        in_specs=specs,
        out_specs=[out_spec] * (len(outs) - in_place) + [ANY] * in_place,
        scratch_shapes=scratch,
        compiler_params=PARAMS,
        cost_estimate=pl.CostEstimate(flops=2 * macs, bytes_accessed=0, transcendentals=0),
    )(*arrays)


def body(values, gate, residues, rates, skip, out_weight):
    shards, tp = lax.axis_size("seq"), lax.axis_size("tp")
    tok, chan = values.shape
    modes = rates.shape[0]
    chips = tp // 2
    away = chips - 1
    block = out_weight.shape[1] // tp
    here = pltpu.VMEM
    parts = 4 if chan % (4 * LANE) == 0 else 1
    cores = [(rank, rank ^ 1) for rank in range(tp)]
    sources = [(HBM, each) for each in (values, rates, residues, skip.reshape(1, chan), gate)]
    (wire,) = call(
        state_kernel,
        [jax.ShapeDtypeStruct((shards, modes, chan), BF16)],
        *sources[:2],
        scratch=[
            here((tok, chan), BF16),
            here((modes, chan), F32),
            pltpu.SemaphoreType.DMA((parts + 1,)),
        ],
    )
    states = lax.all_to_all(
        wire, "seq", split_axis=0, concat_axis=0, tiled=True,
        axis_index_groups=[group_order(shards)],
    )
    narrow = max(LANE, block // 4)
    wide = block - narrow
    weight = (HBM, out_weight)
    *tables, first_weight, kept_weight, sent_weight, last_weight = call(
        local_kernel,
        [
            here((tok, chan), F32),
            here((modes * SUB, chan), F32),
            here((modes, chan), F32),
            here((modes, chan), F32),
            here((tok, chan), BF16),
            here((chan, away * narrow), BF16),
            here((chan, away * narrow), BF16),
            pltpu.HBM((chan, away * wide), BF16),
            pltpu.HBM((chan, away * wide), BF16),
        ],
        *sources, weight,
        in_place=2,
        scratch=[
            here((tok, chan), BF16),
            here((modes, chan), F32),
            here((modes, chan), F32),
            here((1, chan), F32),
            here((tok, chan), F32),
            here((SUB, LANE), F32),
            here((modes * SUB, LANE), F32),
            here((tok // SUB // SUB, modes * SUB, LANE), F32),
            here((tok, LANE), F32),
            here((chan, away * wide), BF16),
            here((chan, away * wide), BF16),
            pltpu.SemaphoreType.DMA((len(sources),)),
            pltpu.SemaphoreType.DMA((4, away * ROW_CUTS)),
            pltpu.SemaphoreType.DMA((2,)),
        ],
    )

    hint = 16 * tok * chan * block
    gated, sent = call(
        gate_kernel,
        [here((tok, chan), BF16), here((tok, away * narrow), BF16)],
        states, *tables, first_weight,
        scratch=[here((modes, chan), F32)], macs=hint,
    )
    moved_first = lax.ppermute(sent, "tp", cores)
    kept, sent = call(
        middle_kernel,
        [here((tok, away * narrow), F32), here((tok, away * wide), BF16)],
        gated, kept_weight, sent_weight,
    )
    moved = lax.ppermute(sent, "tp", cores)

    def to_chips(going):
        return [
            lax.ppermute(each, "tp", [(rank, (rank + 2 * hop) % tp) for rank in reversed(range(tp))])
            for hop, each in enumerate(going, 1)
        ]

    going = call(join_kernel, [here((tok, narrow), BF16)] * away, kept, moved_first, macs=hint)
    first = to_chips(going)
    going = call(
        going_kernel, [here((tok, wide), BF16)] * away,
        gated, last_weight, moved, (ANY, going[-1]),
    )
    second = to_chips(going)
    late = [here((chan, block), BF16), pltpu.SemaphoreType.DMA((ROW_CUTS,))]
    halves = call(
        late_kernel, [here((tok, block // 2), BF16)] * 2,
        gated, weight, (ANY, going[-1]), (ANY, first[-1]), scratch=late, macs=hint,
    )
    halves = [lax.ppermute(each, "tp", cores) for each in halves]
    done, own = call(
        own_kernel, [here((tok, narrow), BF16), here((tok, wide), F32)],
        gated, weight, *halves, *first, scratch=late,
    )
    (out,) = call(
        final_kernel, [jax.ShapeDtypeStruct((tok, block), BF16)], done, own, *second,
        scratch=[here((tok, wide), BF16), pltpu.SemaphoreType.DMA((3,))],
        out_spec=ANY,
    )
    return out


def solution(mesh):
    placed = (P("seq", "tp"), P("seq", "tp"), P(None, "tp"), P(None, "tp"), P("tp"), P("tp", None))
    return jax.shard_map(
        body, mesh=mesh, in_specs=placed, out_specs=P("seq", "tp"), check_vma=False
    )
```

```python
from functools import partial

import jax
import jax.numpy as jnp
from jax import lax
from jax.experimental import pallas as pl
from jax.experimental.pallas import tpu as pltpu
from jax.sharding import PartitionSpec as P

SUB, LANE = 8, 128
F32, BF16 = jnp.float32, jnp.bfloat16

VMEM = pl.BlockSpec(memory_space=pltpu.VMEM)
ANY = pl.BlockSpec(memory_space=pl.ANY)
HBM = "hbm"
PARAMS = pltpu.CompilerParams(vmem_limit_bytes=24 * 2**20)


def in_hbm(array):
    return pltpu.with_memory_space_constraint(array, pltpu.HBM)


def in_vmem(array):
    return pltpu.with_memory_space_constraint(array, pltpu.VMEM)


def row_of(block, mode):
    return jnp.broadcast_to(block[mode : mode + 1, :], (SUB, LANE))


def sublane():
    return lax.broadcasted_iota(jnp.int32, (SUB, LANE), 0)


def lanes_at(step):
    return pl.ds(pl.multiple_of(step * LANE, LANE), LANE)


def gains_of(residues, rates):
    return residues * jnp.sqrt(2.0 * rates)


def spread_table(tok):
    run = tok // SUB
    row = lax.broadcasted_iota(jnp.int32, (tok, tok), 0)
    col = lax.broadcasted_iota(jnp.int32, (tok, tok), 1)
    return (col == row % SUB * run + row // SUB).astype(F32).astype(BF16)


ROW_CUTS = 4


def column_copies(other, begin, slots, weight_hbm, out_ref, sems):
    rank = lax.axis_index("tp")
    chips = lax.axis_size("tp") // 2
    block = weight_hbm.shape[1] // (2 * chips)
    wide = out_ref.shape[1] // len(slots)
    tall = out_ref.shape[0] // ROW_CUTS
    core = 1 - rank % 2 if other else rank % 2
    copies = []
    for at, slot in enumerate(slots):
        owner = (rank // 2 + slot) % chips * 2 + core
        columns = pl.ds(pl.multiple_of(owner * block + begin, LANE), wide)
        for cut in range(ROW_CUTS):
            rows = pl.ds(cut * tall, tall)
            copies.append(
                pltpu.make_async_copy(
                    weight_hbm.at[rows, columns],
                    out_ref.at[rows, pl.ds(at * wide, wide)],
                    sems.at[at * ROW_CUTS + cut],
                )
            )
            copies[-1].start()
    return copies


def group_order(count):
    return [(count // 2 + at) % count for at in range(count)]


def wait_all(copies):
    for copy in copies:
        copy.wait()


def state_kernel(values_hbm, rates_hbm, wire_ref, values_ref, rates_ref, sems):
    tok, chan = values_ref.shape
    modes = rates_ref.shape[0]
    parts = sems.shape[0] - 1
    width = chan // parts
    first = pltpu.make_async_copy(rates_hbm, rates_ref, sems.at[parts])
    first.start()
    pieces = []
    for part in range(parts):
        lanes = pl.ds(part * width, width)
        pieces.append(
            pltpu.make_async_copy(
                values_hbm.at[:, lanes], values_ref.at[:, lanes], sems.at[part]
            )
        )
        pieces[-1].start()
    left = (SUB - 1 - sublane()).astype(F32)
    first.wait()
    for index in range(chan // LANE):
        if index * LANE % width == 0:
            pieces[index * LANE // width].wait()
        lanes = slice(index * LANE, (index + 1) * LANE)
        rates = rates_ref[:, lanes]
        decay = jnp.exp(-float(SUB) * rates)
        decays = [row_of(decay, mode) for mode in range(modes)]
        held = [jnp.zeros((SUB, LANE), F32)] * modes
        for at in range(0, tok, 2 * SUB):
            pair = values_ref[at : at + 2 * SUB, lanes].astype(F32)
            for half in (pair[:SUB], pair[SUB:]):
                held = [decays[mode] * held[mode] + half for mode in range(modes)]
        rows = [
            jnp.sum(held[mode] * jnp.exp(-row_of(rates, mode) * left), axis=0, keepdims=True)
            for mode in range(modes)
        ]
        state = jnp.concatenate(rows, axis=0).astype(BF16)
        for shard in range(wire_ref.shape[0]):
            wire_ref[shard, :, lanes] = state


def local_kernel(
    values_hbm, rates_hbm, residues_hbm, skip_hbm, gate_hbm, weight_hbm,
    near_ref, reach_ref, decay_ref, far_ref, gate_ref, first_weight, kept_weight,
    sent_weight, last_weight,
    values_ref, rates_ref, residues_ref, skip_ref, wide_ref, taps_ref, first_ref, snap_ref,
    order_ref, sent_held, last_held, sems, weight_sems, out_sems,
):
    tok, chan = values_ref.shape
    modes = rates_ref.shape[0]
    run = tok // SUB
    copies = [
        pltpu.make_async_copy(source, target, sems.at[at])
        for at, (source, target) in enumerate(
            (
                (values_hbm, values_ref),
                (rates_hbm, rates_ref),
                (residues_hbm, residues_ref),
                (skip_hbm, skip_ref),
                (gate_hbm, gate_ref),
            )
        )
    ]
    for copy in copies:
        copy.start()
    slots = range(1, lax.axis_size("tp") // 2)
    rest = column_copies(1, 0, slots, weight_hbm, first_weight, weight_sems.at[0])
    rest += column_copies(0, 0, slots, weight_hbm, kept_weight, weight_sems.at[1])
    begin = kept_weight.shape[1] // len(slots)
    passing = column_copies(1, begin, slots, weight_hbm, sent_held, weight_sems.at[2])
    passing += column_copies(0, begin, slots, weight_hbm, last_held, weight_sems.at[3])
    rest.append(copies.pop())
    table = spread_table(tok)
    wait_all(copies)
    wide_ref[...] = jnp.dot(table, values_ref[...], preferred_element_type=F32)

    def step(index, carry):
        lanes = lanes_at(index)
        place = sublane()
        rates = rates_ref[:, lanes]
        gains = gains_of(residues_ref[:, lanes], rates)

        ahead = place.astype(F32)
        decay, decay_block = jnp.exp(-rates), jnp.exp(-float(SUB) * rates)
        decay_run = jnp.exp(-float(run) * rates)
        decays = [row_of(decay, mode) for mode in range(modes)]
        taps = jnp.where(place == 0, skip_ref[:, lanes], 0.0)
        for mode in range(modes):
            gain = row_of(gains, mode)
            term = gain * jnp.exp(-row_of(rates, mode) * ahead)
            taps = taps + term
            first_ref[mode * SUB : (mode + 1) * SUB, :] = gain * decays[mode]
            reach_ref[mode * SUB : (mode + 1) * SUB, lanes] = term * decays[mode]
        taps_ref[...] = taps

        held = [jnp.zeros((SUB, LANE), F32)] * modes
        for at in range(run):
            if at % SUB == 0:
                for mode in range(modes):
                    snap_ref[at // SUB, mode * SUB : (mode + 1) * SUB, :] = held[mode]
            value = wide_ref[at * SUB : (at + 1) * SUB, lanes]
            held = [decays[mode] * held[mode] + value for mode in range(modes)]
        for mode in range(modes):
            whole, power = held[mode], row_of(decay_run, mode)
            for shift in (1, 2, 4):
                moved = jnp.where(place >= shift, pltpu.roll(whole, shift, 0), 0.0)
                whole = whole + power * moved
                power = power * power
            before = jnp.where(place >= 1, pltpu.roll(whole, 1, 0), 0.0)
            rows = slice(mode * SUB, (mode + 1) * SUB)
            fade = row_of(decay_block, mode)
            for block in range(run // SUB):
                snap_ref[block, rows, :] = first_ref[rows, :] * (snap_ref[block, rows, :] + before)
                before = fade * before

        for block in range(run // SUB):
            values = [
                wide_ref[(block * SUB + at) * SUB : (block * SUB + at + 1) * SUB, lanes]
                for at in range(SUB)
            ]
            sums = [jnp.zeros((SUB, LANE), F32)] * SUB
            for lag in range(SUB):
                tap = jnp.broadcast_to(taps_ref[lag : lag + 1, :], (SUB, LANE))
                for at in range(lag, SUB):
                    sums[at] = sums[at] + tap * values[at - lag]
            terms = [
                snap_ref[block, mode * SUB : (mode + 1) * SUB, :] for mode in range(modes)
            ]
            for at in range(SUB):
                total = sums[at]
                for mode in range(modes):
                    total = total + terms[mode]
                terms = [terms[mode] * decays[mode] for mode in range(modes)]
                order_ref[pl.ds(block * SUB + at, SUB, stride=run), :] = total
        near_ref[:, lanes] = order_ref[:tok, :]
        decay_ref[:, lanes] = jnp.exp(-float(SUB) * rates)
        far_ref[:, lanes] = jnp.exp(-float(tok) * rates)
        return carry

    steps = chan // LANE
    lax.fori_loop(0, steps // 2, step, 0)
    wait_all(passing)
    for at, (held, target) in enumerate(((sent_held, sent_weight), (last_held, last_weight))):
        rest.append(pltpu.make_async_copy(held, target, out_sems.at[at]))
        rest[-1].start()
    lax.fori_loop(steps // 2, steps, step, 0)
    wait_all(rest)


def gate_kernel(
    states_ref, near_ref, reach_ref, decay_ref, far_ref, gate_ref, weight_ref,
    gated_ref, sent_ref, state_ref,
):
    tok, chan = gate_ref.shape
    shards, modes = states_ref.shape[:2]
    place = lax.axis_index("seq")
    far = far_ref[...]
    before = jnp.zeros((modes, chan), F32)
    order = group_order(shards)
    for shard in range(shards - 1):
        passed = far * before + states_ref[order.index(shard)].astype(F32)
        before = jnp.where(shard < place, passed, before)
    state_ref[...] = before

    def step(index, carry):
        lanes = lanes_at(index)
        decays, terms = [], []
        for mode in range(modes):
            rows, row = slice(mode * SUB, (mode + 1) * SUB), slice(mode, mode + 1)
            decays.append(jnp.broadcast_to(decay_ref[row, lanes], (SUB, LANE)))
            state = jnp.broadcast_to(state_ref[row, lanes], (SUB, LANE))
            terms.append(state * reach_ref[rows, lanes])
        for at in range(0, tok, 2 * SUB):
            totals = []
            for first in (at, at + SUB):
                total = near_ref[first : first + SUB, lanes]
                for mode in range(modes):
                    total = total + terms[mode]
                terms = [terms[mode] * decays[mode] for mode in range(modes)]
                totals.append(total)
            rows = slice(at, at + 2 * SUB)
            gate = gate_ref[rows, lanes].astype(F32)
            gated_ref[rows, lanes] = (gate * jnp.concatenate(totals, axis=0)).astype(BF16)
        return carry

    lax.fori_loop(0, chan // LANE, step, 0)
    project(gated_ref, weight_ref, sent_ref)


def project(left_ref, right_ref, out_ref):
    total = out_ref.shape[1]
    tile = 2 * LANE if total % (2 * LANE) == 0 else LANE
    for first in range(0, total, tile):
        lanes = slice(first, first + tile)
        out_ref[:, lanes] = jnp.dot(
            left_ref[...], right_ref[:, lanes], preferred_element_type=F32
        ).astype(out_ref.dtype)


def product(gated_ref, weight):
    return jnp.dot(gated_ref[...], weight, preferred_element_type=F32)


def middle_kernel(gated_ref, kept_weight, sent_weight, kept_ref, sent_ref):
    project(gated_ref, kept_weight, kept_ref)
    project(gated_ref, sent_weight, sent_ref)


def join_kernel(kept_ref, moved_ref, *going_refs):
    wide = going_refs[0].shape[1]
    for at, going_ref in enumerate(going_refs):
        lanes = slice(at * wide, (at + 1) * wide)
        going_ref[...] = (kept_ref[:, lanes] + moved_ref[:, lanes].astype(F32)).astype(BF16)


def going_kernel(gated_ref, weight_ref, moved_ref, after_ref, *going_refs):
    wide = going_refs[0].shape[1]
    for at, going_ref in enumerate(going_refs):
        lanes = slice(at * wide, (at + 1) * wide)
        total = product(gated_ref, weight_ref[:, lanes])
        going_ref[...] = (total + moved_ref[:, lanes].astype(F32)).astype(BF16)


def late_kernel(gated_ref, weight_hbm, *refs):
    (low_ref, high_ref, weight_ref, sems) = refs[-4:]
    half = low_ref.shape[1]
    wait_all(column_copies(1, 0, range(1), weight_hbm, weight_ref, sems))
    low_ref[...] = product(gated_ref, weight_ref[:, :half]).astype(BF16)
    high_ref[...] = product(gated_ref, weight_ref[:, half:]).astype(BF16)


def own_kernel(gated_ref, weight_hbm, low_ref, high_ref, *refs):
    others, (first_ref, own_ref, weight_ref, sems) = refs[:-4], refs[-4:]
    narrow, half = first_ref.shape[1], low_ref.shape[1]
    wait_all(column_copies(0, 0, range(1), weight_hbm, weight_ref, sems))
    total = low_ref[:, :narrow].astype(F32) + product(gated_ref, weight_ref[:, :narrow])
    for other in others:
        total = total + other[...].astype(F32)
    first_ref[...] = total.astype(BF16)
    own_ref[:, : half - narrow] = low_ref[:, narrow:].astype(F32) + product(
        gated_ref, weight_ref[:, narrow:half]
    )
    own_ref[:, half - narrow :] = high_ref[...].astype(F32) + product(
        gated_ref, weight_ref[:, half:]
    )


def final_kernel(first_ref, own_ref, *refs):
    others, (out_hbm, wide_ref, sems) = refs[:-3], refs[-3:]
    tok, narrow = first_ref.shape
    count = sems.shape[0] - 1
    copies = [
        pltpu.make_async_copy(first_ref, out_hbm.at[:, pl.ds(0, narrow)], sems.at[count])
    ]
    copies[0].start()
    for part in range(count):
        rows = pl.ds(part * tok // count, tok // count)
        total = own_ref[rows, :]
        for other in others:
            total = total + other[rows, :].astype(F32)
        wide_ref[rows, :] = total.astype(BF16)
        columns = pl.ds(narrow, wide_ref.shape[1])
        copies.append(
            pltpu.make_async_copy(wide_ref.at[rows], out_hbm.at[rows, columns], sems.at[part])
        )
        copies[-1].start()
    wait_all(copies)


def call(kernel, outs, *operands, scratch=(), macs=0, out_spec=VMEM, in_place=0):
    specs, arrays = [], []
    for operand in operands:
        spec, array = operand if isinstance(operand, tuple) else (VMEM, operand)
        specs.append(ANY if spec is HBM else spec)
        arrays.append(in_hbm(array) if spec is HBM else array)
    return pl.pallas_call(
        kernel,
        out_shape=outs,
        in_specs=specs,
        out_specs=[out_spec] * (len(outs) - in_place) + [ANY] * in_place,
        scratch_shapes=scratch,
        compiler_params=PARAMS,
        cost_estimate=pl.CostEstimate(flops=2 * macs, bytes_accessed=0, transcendentals=0),
    )(*arrays)


def body(values, gate, residues, rates, skip, out_weight):
    shards, tp = lax.axis_size("seq"), lax.axis_size("tp")
    tok, chan = values.shape
    modes = rates.shape[0]
    chips = tp // 2
    away = chips - 1
    block = out_weight.shape[1] // tp
    here = pltpu.VMEM
    parts = 4 if chan % (4 * LANE) == 0 else 1
    cores = [(rank, rank ^ 1) for rank in range(tp)]
    sources = [(HBM, each) for each in (values, rates, residues, skip.reshape(1, chan), gate)]
    (wire,) = call(
        state_kernel,
        [jax.ShapeDtypeStruct((shards, modes, chan), BF16)],
        *sources[:2],
        scratch=[
            here((tok, chan), BF16),
            here((modes, chan), F32),
            pltpu.SemaphoreType.DMA((parts + 1,)),
        ],
    )
    states = lax.all_to_all(
        wire, "seq", split_axis=0, concat_axis=0, tiled=True,
        axis_index_groups=[group_order(shards)],
    )
    narrow = max(LANE, block // 4)
    wide = block - narrow
    weight = (HBM, out_weight)
    *tables, first_weight, kept_weight, sent_weight, last_weight = call(
        local_kernel,
        [
            here((tok, chan), F32),
            here((modes * SUB, chan), F32),
            here((modes, chan), F32),
            here((modes, chan), F32),
            here((tok, chan), BF16),
            here((chan, away * narrow), BF16),
            here((chan, away * narrow), BF16),
            pltpu.HBM((chan, away * wide), BF16),
            pltpu.HBM((chan, away * wide), BF16),
        ],
        *sources, weight,
        in_place=2,
        scratch=[
            here((tok, chan), BF16),
            here((modes, chan), F32),
            here((modes, chan), F32),
            here((1, chan), F32),
            here((tok, chan), F32),
            here((SUB, LANE), F32),
            here((modes * SUB, LANE), F32),
            here((tok // SUB // SUB, modes * SUB, LANE), F32),
            here((tok + tok // SUB, LANE), F32),
            here((chan, away * wide), BF16),
            here((chan, away * wide), BF16),
            pltpu.SemaphoreType.DMA((len(sources),)),
            pltpu.SemaphoreType.DMA((4, away * ROW_CUTS)),
            pltpu.SemaphoreType.DMA((2,)),
        ],
    )

    hint = 16 * tok * chan * block
    gated, sent = call(
        gate_kernel,
        [here((tok, chan), BF16), here((tok, away * narrow), BF16)],
        states, *tables, first_weight,
        scratch=[here((modes, chan), F32)], macs=hint,
    )
    moved_first = lax.ppermute(sent, "tp", cores)
    kept, sent = call(
        middle_kernel,
        [here((tok, away * narrow), F32), here((tok, away * wide), BF16)],
        gated, kept_weight, sent_weight,
    )
    moved = lax.ppermute(sent, "tp", cores)

    def to_chips(going):
        return [
            lax.ppermute(each, "tp", [(rank, (rank + 2 * hop) % tp) for rank in reversed(range(tp))])
            for hop, each in enumerate(going, 1)
        ]

    going = call(join_kernel, [here((tok, narrow), BF16)] * away, kept, moved_first, macs=hint)
    first = to_chips(going)
    going = call(
        going_kernel, [here((tok, wide), BF16)] * away,
        gated, last_weight, moved, (ANY, going[-1]),
    )
    second = to_chips(going)
    late = [here((chan, block), BF16), pltpu.SemaphoreType.DMA((ROW_CUTS,))]
    halves = call(
        late_kernel, [here((tok, block // 2), BF16)] * 2,
        gated, weight, (ANY, going[-1]), (ANY, first[-1]), scratch=late, macs=hint,
    )
    halves = [lax.ppermute(each, "tp", cores) for each in halves]
    done, own = call(
        own_kernel, [here((tok, narrow), BF16), here((tok, wide), F32)],
        gated, weight, *halves, *first, scratch=late,
    )
    (out,) = call(
        final_kernel, [jax.ShapeDtypeStruct((tok, block), BF16)], done, own, *second,
        scratch=[here((tok, wide), BF16), pltpu.SemaphoreType.DMA((3,))],
        out_spec=ANY,
    )
    return out


def solution(mesh):
    placed = (P("seq", "tp"), P("seq", "tp"), P(None, "tp"), P(None, "tp"), P("tp"), P("tp", None))
    return jax.shard_map(
        body, mesh=mesh, in_specs=placed, out_specs=P("seq", "tp"), check_vma=False
    )
```

```python
from functools import partial

import jax
import jax.numpy as jnp
from jax import lax
from jax.experimental import pallas as pl
from jax.experimental.pallas import tpu as pltpu
from jax.sharding import PartitionSpec as P

SUB, LANE = 8, 128
F32, BF16 = jnp.float32, jnp.bfloat16

VMEM = pl.BlockSpec(memory_space=pltpu.VMEM)
ANY = pl.BlockSpec(memory_space=pl.ANY)
HBM = "hbm"
PARAMS = pltpu.CompilerParams(vmem_limit_bytes=24 * 2**20)


def in_hbm(array):
    return pltpu.with_memory_space_constraint(array, pltpu.HBM)


def in_vmem(array):
    return pltpu.with_memory_space_constraint(array, pltpu.VMEM)


def row_of(block, mode):
    return jnp.broadcast_to(block[mode : mode + 1, :], (SUB, LANE))


def sublane():
    return lax.broadcasted_iota(jnp.int32, (SUB, LANE), 0)


def lanes_at(step):
    return pl.ds(pl.multiple_of(step * LANE, LANE), LANE)


def gains_of(residues, rates):
    return residues * jnp.sqrt(2.0 * rates)


def spread_table(tok):
    run = tok // SUB
    row = lax.broadcasted_iota(jnp.int32, (tok, tok), 0)
    col = lax.broadcasted_iota(jnp.int32, (tok, tok), 1)
    return (col == row % SUB * run + row // SUB).astype(F32).astype(BF16)


ROW_CUTS = 4


def column_copies(other, begin, slots, weight_hbm, out_ref, sems):
    rank = lax.axis_index("tp")
    chips = lax.axis_size("tp") // 2
    block = weight_hbm.shape[1] // (2 * chips)
    wide = out_ref.shape[1] // len(slots)
    tall = out_ref.shape[0] // ROW_CUTS
    core = 1 - rank % 2 if other else rank % 2
    copies = []
    for at, slot in enumerate(slots):
        owner = (rank // 2 + slot) % chips * 2 + core
        columns = pl.ds(pl.multiple_of(owner * block + begin, LANE), wide)
        for cut in range(ROW_CUTS):
            rows = pl.ds(cut * tall, tall)
            copies.append(
                pltpu.make_async_copy(
                    weight_hbm.at[rows, columns],
                    out_ref.at[rows, pl.ds(at * wide, wide)],
                    sems.at[at * ROW_CUTS + cut],
                )
            )
            copies[-1].start()
    return copies


def group_order(count):
    return [(count // 4 + at) % count for at in range(count)]


def wait_all(copies):
    for copy in copies:
        copy.wait()


def state_kernel(values_hbm, rates_hbm, wire_ref, values_ref, rates_ref, sems):
    tok, chan = values_ref.shape
    modes = rates_ref.shape[0]
    parts = sems.shape[0] - 1
    width = chan // parts
    first = pltpu.make_async_copy(rates_hbm, rates_ref, sems.at[parts])
    first.start()
    pieces = []
    for part in range(parts):
        lanes = pl.ds(part * width, width)
        pieces.append(
            pltpu.make_async_copy(
                values_hbm.at[:, lanes], values_ref.at[:, lanes], sems.at[part]
            )
        )
        pieces[-1].start()
    left = (SUB - 1 - sublane()).astype(F32)
    first.wait()
    for index in range(chan // LANE):
        if index * LANE % width == 0:
            pieces[index * LANE // width].wait()
        lanes = slice(index * LANE, (index + 1) * LANE)
        rates = rates_ref[:, lanes]
        decay = jnp.exp(-float(SUB) * rates)
        decays = [row_of(decay, mode) for mode in range(modes)]
        held = [jnp.zeros((SUB, LANE), F32)] * modes
        for at in range(0, tok, 2 * SUB):
            pair = values_ref[at : at + 2 * SUB, lanes].astype(F32)
            for half in (pair[:SUB], pair[SUB:]):
                held = [decays[mode] * held[mode] + half for mode in range(modes)]
        rows = [
            jnp.sum(held[mode] * jnp.exp(-row_of(rates, mode) * left), axis=0, keepdims=True)
            for mode in range(modes)
        ]
        state = jnp.concatenate(rows, axis=0).astype(BF16)
        for shard in range(wire_ref.shape[0]):
            wire_ref[shard, :, lanes] = state


def local_kernel(
    values_hbm, rates_hbm, residues_hbm, skip_hbm, gate_hbm, weight_hbm,
    near_ref, reach_ref, decay_ref, far_ref, gate_ref, first_weight, kept_weight,
    sent_weight, last_weight,
    values_ref, rates_ref, residues_ref, skip_ref, wide_ref, taps_ref, first_ref, snap_ref,
    order_ref, sent_held, last_held, sems, weight_sems, out_sems,
):
    tok, chan = values_ref.shape
    modes = rates_ref.shape[0]
    run = tok // SUB
    copies = [
        pltpu.make_async_copy(source, target, sems.at[at])
        for at, (source, target) in enumerate(
            (
                (values_hbm, values_ref),
                (rates_hbm, rates_ref),
                (residues_hbm, residues_ref),
                (skip_hbm, skip_ref),
                (gate_hbm, gate_ref),
            )
        )
    ]
    for copy in copies:
        copy.start()
    slots = range(1, lax.axis_size("tp") // 2)
    rest = column_copies(1, 0, slots, weight_hbm, first_weight, weight_sems.at[0])
    rest += column_copies(0, 0, slots, weight_hbm, kept_weight, weight_sems.at[1])
    begin = kept_weight.shape[1] // len(slots)
    passing = column_copies(1, begin, slots, weight_hbm, sent_held, weight_sems.at[2])
    passing += column_copies(0, begin, slots, weight_hbm, last_held, weight_sems.at[3])
    rest.append(copies.pop())
    table = spread_table(tok)
    wait_all(copies)
    wide_ref[...] = jnp.dot(table, values_ref[...], preferred_element_type=F32)

    def step(index, carry):
        lanes = lanes_at(index)
        place = sublane()
        rates = rates_ref[:, lanes]
        gains = gains_of(residues_ref[:, lanes], rates)

        ahead = place.astype(F32)
        decay, decay_block = jnp.exp(-rates), jnp.exp(-float(SUB) * rates)
        decay_run = jnp.exp(-float(run) * rates)
        decays = [row_of(decay, mode) for mode in range(modes)]
        taps = jnp.where(place == 0, skip_ref[:, lanes], 0.0)
        for mode in range(modes):
            gain = row_of(gains, mode)
            term = gain * jnp.exp(-row_of(rates, mode) * ahead)
            taps = taps + term
            first_ref[mode * SUB : (mode + 1) * SUB, :] = gain * decays[mode]
            reach_ref[mode * SUB : (mode + 1) * SUB, lanes] = term * decays[mode]
        taps_ref[...] = taps

        held = [jnp.zeros((SUB, LANE), F32)] * modes
        for at in range(run):
            if at % SUB == 0:
                for mode in range(modes):
                    snap_ref[at // SUB, mode * SUB : (mode + 1) * SUB, :] = held[mode]
            value = wide_ref[at * SUB : (at + 1) * SUB, lanes]
            held = [decays[mode] * held[mode] + value for mode in range(modes)]
        for mode in range(modes):
            whole, power = held[mode], row_of(decay_run, mode)
            for shift in (1, 2, 4):
                moved = jnp.where(place >= shift, pltpu.roll(whole, shift, 0), 0.0)
                whole = whole + power * moved
                power = power * power
            before = jnp.where(place >= 1, pltpu.roll(whole, 1, 0), 0.0)
            rows = slice(mode * SUB, (mode + 1) * SUB)
            fade = row_of(decay_block, mode)
            for block in range(run // SUB):
                snap_ref[block, rows, :] = first_ref[rows, :] * (snap_ref[block, rows, :] + before)
                before = fade * before

        for block in range(run // SUB):
            values = [
                wide_ref[(block * SUB + at) * SUB : (block * SUB + at + 1) * SUB, lanes]
                for at in range(SUB)
            ]
            sums = [jnp.zeros((SUB, LANE), F32)] * SUB
            for lag in range(SUB):
                tap = jnp.broadcast_to(taps_ref[lag : lag + 1, :], (SUB, LANE))
                for at in range(lag, SUB):
                    sums[at] = sums[at] + tap * values[at - lag]
            terms = [
                snap_ref[block, mode * SUB : (mode + 1) * SUB, :] for mode in range(modes)
            ]
            for at in range(SUB):
                total = sums[at]
                for mode in range(modes):
                    total = total + terms[mode]
                terms = [terms[mode] * decays[mode] for mode in range(modes)]
                order_ref[pl.ds(block * SUB + at, SUB, stride=run), :] = total
        near_ref[:, lanes] = order_ref[:tok, :]
        decay_ref[:, lanes] = jnp.exp(-float(SUB) * rates)
        far_ref[:, lanes] = jnp.exp(-float(tok) * rates)
        return carry

    steps = chan // LANE
    lax.fori_loop(0, steps // 2, step, 0)
    wait_all(passing)
    for at, (held, target) in enumerate(((sent_held, sent_weight), (last_held, last_weight))):
        rest.append(pltpu.make_async_copy(held, target, out_sems.at[at]))
        rest[-1].start()
    lax.fori_loop(steps // 2, steps, step, 0)
    wait_all(rest)


def gate_kernel(
    states_ref, near_ref, reach_ref, decay_ref, far_ref, gate_ref, weight_ref,
    gated_ref, sent_ref, state_ref,
):
    tok, chan = gate_ref.shape
    shards, modes = states_ref.shape[:2]
    place = lax.axis_index("seq")
    far = far_ref[...]
    before = jnp.zeros((modes, chan), F32)
    order = group_order(shards)
    for shard in range(shards - 1):
        passed = far * before + states_ref[order.index(shard)].astype(F32)
        before = jnp.where(shard < place, passed, before)
    state_ref[...] = before

    def step(index, carry):
        lanes = lanes_at(index)
        decays, terms = [], []
        for mode in range(modes):
            rows, row = slice(mode * SUB, (mode + 1) * SUB), slice(mode, mode + 1)
            decays.append(jnp.broadcast_to(decay_ref[row, lanes], (SUB, LANE)))
            state = jnp.broadcast_to(state_ref[row, lanes], (SUB, LANE))
            terms.append(state * reach_ref[rows, lanes])
        for at in range(0, tok, 2 * SUB):
            totals = []
            for first in (at, at + SUB):
                total = near_ref[first : first + SUB, lanes]
                for mode in range(modes):
                    total = total + terms[mode]
                terms = [terms[mode] * decays[mode] for mode in range(modes)]
                totals.append(total)
            rows = slice(at, at + 2 * SUB)
            gate = gate_ref[rows, lanes].astype(F32)
            gated_ref[rows, lanes] = (gate * jnp.concatenate(totals, axis=0)).astype(BF16)
        return carry

    lax.fori_loop(0, chan // LANE, step, 0)
    project(gated_ref, weight_ref, sent_ref)


def project(left_ref, right_ref, out_ref):
    total = out_ref.shape[1]
    tile = 2 * LANE if total % (2 * LANE) == 0 else LANE
    for first in range(0, total, tile):
        lanes = slice(first, first + tile)
        out_ref[:, lanes] = jnp.dot(
            left_ref[...], right_ref[:, lanes], preferred_element_type=F32
        ).astype(out_ref.dtype)


def product(gated_ref, weight):
    return jnp.dot(gated_ref[...], weight, preferred_element_type=F32)


def middle_kernel(gated_ref, kept_weight, sent_weight, kept_ref, sent_ref):
    project(gated_ref, kept_weight, kept_ref)
    project(gated_ref, sent_weight, sent_ref)


def join_kernel(kept_ref, moved_ref, *going_refs):
    wide = going_refs[0].shape[1]
    for at, going_ref in enumerate(going_refs):
        lanes = slice(at * wide, (at + 1) * wide)
        going_ref[...] = (kept_ref[:, lanes] + moved_ref[:, lanes].astype(F32)).astype(BF16)


def going_kernel(gated_ref, weight_ref, moved_ref, after_ref, *going_refs):
    wide = going_refs[0].shape[1]
    for at, going_ref in enumerate(going_refs):
        lanes = slice(at * wide, (at + 1) * wide)
        total = product(gated_ref, weight_ref[:, lanes])
        going_ref[...] = (total + moved_ref[:, lanes].astype(F32)).astype(BF16)


def late_kernel(gated_ref, weight_hbm, *refs):
    (low_ref, high_ref, weight_ref, sems) = refs[-4:]
    half = low_ref.shape[1]
    wait_all(column_copies(1, 0, range(1), weight_hbm, weight_ref, sems))
    low_ref[...] = product(gated_ref, weight_ref[:, :half]).astype(BF16)
    high_ref[...] = product(gated_ref, weight_ref[:, half:]).astype(BF16)


def own_kernel(gated_ref, weight_hbm, low_ref, high_ref, *refs):
    others, (first_ref, own_ref, weight_ref, sems) = refs[:-4], refs[-4:]
    narrow, half = first_ref.shape[1], low_ref.shape[1]
    wait_all(column_copies(0, 0, range(1), weight_hbm, weight_ref, sems))
    total = low_ref[:, :narrow].astype(F32) + product(gated_ref, weight_ref[:, :narrow])
    for other in others:
        total = total + other[...].astype(F32)
    first_ref[...] = total.astype(BF16)
    own_ref[:, : half - narrow] = low_ref[:, narrow:].astype(F32) + product(
        gated_ref, weight_ref[:, narrow:half]
    )
    own_ref[:, half - narrow :] = high_ref[...].astype(F32) + product(
        gated_ref, weight_ref[:, half:]
    )


def final_kernel(first_ref, own_ref, *refs):
    others, (out_hbm, wide_ref, sems) = refs[:-3], refs[-3:]
    tok, narrow = first_ref.shape
    count = sems.shape[0] - 1
    copies = [
        pltpu.make_async_copy(first_ref, out_hbm.at[:, pl.ds(0, narrow)], sems.at[count])
    ]
    copies[0].start()
    for part in range(count):
        rows = pl.ds(part * tok // count, tok // count)
        total = own_ref[rows, :]
        for other in others:
            total = total + other[rows, :].astype(F32)
        wide_ref[rows, :] = total.astype(BF16)
        columns = pl.ds(narrow, wide_ref.shape[1])
        copies.append(
            pltpu.make_async_copy(wide_ref.at[rows], out_hbm.at[rows, columns], sems.at[part])
        )
        copies[-1].start()
    wait_all(copies)


def call(kernel, outs, *operands, scratch=(), macs=0, out_spec=VMEM, in_place=0):
    specs, arrays = [], []
    for operand in operands:
        spec, array = operand if isinstance(operand, tuple) else (VMEM, operand)
        specs.append(ANY if spec is HBM else spec)
        arrays.append(in_hbm(array) if spec is HBM else array)
    return pl.pallas_call(
        kernel,
        out_shape=outs,
        in_specs=specs,
        out_specs=[out_spec] * (len(outs) - in_place) + [ANY] * in_place,
        scratch_shapes=scratch,
        compiler_params=PARAMS,
        cost_estimate=pl.CostEstimate(flops=2 * macs, bytes_accessed=0, transcendentals=0),
    )(*arrays)


def body(values, gate, residues, rates, skip, out_weight):
    shards, tp = lax.axis_size("seq"), lax.axis_size("tp")
    tok, chan = values.shape
    modes = rates.shape[0]
    chips = tp // 2
    away = chips - 1
    block = out_weight.shape[1] // tp
    here = pltpu.VMEM
    parts = 4 if chan % (4 * LANE) == 0 else 1
    cores = [(rank, rank ^ 1) for rank in range(tp)]
    sources = [(HBM, each) for each in (values, rates, residues, skip.reshape(1, chan), gate)]
    (wire,) = call(
        state_kernel,
        [jax.ShapeDtypeStruct((shards, modes, chan), BF16)],
        *sources[:2],
        scratch=[
            here((tok, chan), BF16),
            here((modes, chan), F32),
            pltpu.SemaphoreType.DMA((parts + 1,)),
        ],
    )
    states = lax.all_to_all(
        wire, "seq", split_axis=0, concat_axis=0, tiled=True,
        axis_index_groups=[group_order(shards)],
    )
    narrow = max(LANE, block // 4)
    wide = block - narrow
    weight = (HBM, out_weight)
    *tables, first_weight, kept_weight, sent_weight, last_weight = call(
        local_kernel,
        [
            here((tok, chan), F32),
            here((modes * SUB, chan), F32),
            here((modes, chan), F32),
            here((modes, chan), F32),
            here((tok, chan), BF16),
            here((chan, away * narrow), BF16),
            here((chan, away * narrow), BF16),
            pltpu.HBM((chan, away * wide), BF16),
            pltpu.HBM((chan, away * wide), BF16),
        ],
        *sources, weight,
        in_place=2,
        scratch=[
            here((tok, chan), BF16),
            here((modes, chan), F32),
            here((modes, chan), F32),
            here((1, chan), F32),
            here((tok, chan), F32),
            here((SUB, LANE), F32),
            here((modes * SUB, LANE), F32),
            here((tok // SUB // SUB, modes * SUB, LANE), F32),
            here((tok + tok // SUB, LANE), F32),
            here((chan, away * wide), BF16),
            here((chan, away * wide), BF16),
            pltpu.SemaphoreType.DMA((len(sources),)),
            pltpu.SemaphoreType.DMA((4, away * ROW_CUTS)),
            pltpu.SemaphoreType.DMA((2,)),
        ],
    )

    hint = 16 * tok * chan * block
    gated, sent = call(
        gate_kernel,
        [here((tok, chan), BF16), here((tok, away * narrow), BF16)],
        states, *tables, first_weight,
        scratch=[here((modes, chan), F32)], macs=hint,
    )
    moved_first = lax.ppermute(sent, "tp", cores)
    kept, sent = call(
        middle_kernel,
        [here((tok, away * narrow), F32), here((tok, away * wide), BF16)],
        gated, kept_weight, sent_weight,
    )
    moved = lax.ppermute(sent, "tp", cores)

    def to_chips(going):
        return [
            lax.ppermute(each, "tp", [(rank, (rank + 2 * hop) % tp) for rank in reversed(range(tp))])
            for hop, each in enumerate(going, 1)
        ]

    going = call(join_kernel, [here((tok, narrow), BF16)] * away, kept, moved_first, macs=hint)
    first = to_chips(going)
    going = call(
        going_kernel, [here((tok, wide), BF16)] * away,
        gated, last_weight, moved, (ANY, going[-1]),
    )
    second = to_chips(going)
    late = [here((chan, block), BF16), pltpu.SemaphoreType.DMA((ROW_CUTS,))]
    halves = call(
        late_kernel, [here((tok, block // 2), BF16)] * 2,
        gated, weight, (ANY, going[-1]), (ANY, first[-1]), scratch=late, macs=hint,
    )
    halves = [lax.ppermute(each, "tp", cores) for each in halves]
    done, own = call(
        own_kernel, [here((tok, narrow), BF16), here((tok, wide), F32)],
        gated, weight, *halves, *first, scratch=late,
    )
    (out,) = call(
        final_kernel, [jax.ShapeDtypeStruct((tok, block), BF16)], done, own, *second,
        scratch=[here((tok, wide), BF16), pltpu.SemaphoreType.DMA((3,))],
        out_spec=ANY,
    )
    return out


def solution(mesh):
    placed = (P("seq", "tp"), P("seq", "tp"), P(None, "tp"), P(None, "tp"), P("tp"), P("tp", None))
    return jax.shard_map(
        body, mesh=mesh, in_specs=placed, out_specs=P("seq", "tp"), check_vma=False
    )
```
